32 devices in a mesh: lat: 4 (over y, x), rad: 8 (over z, core).
Axes of the slice: x: 2, y: 2, z: 4, core: 2. Of those that a mesh axis runs over, the one named last changes fastest.
Arguments:
- displacement: float32 [3, 32, 256, 384], P(None, 'rad', 'lat'), may hold values from -6 to 6
- forcing: float32 [3, 32, 256, 384], P(None, 'rad', 'lat'), may hold values from -12 to 12
- layer_id: int32 [32], P('rad'), may hold values from 0 to 11
- stiffness: float32 [12], replicated, may hold values from 0.3 to 3
- coupling: float32 [12, 3, 3], replicated, may hold values from -0.5 to 0.5
- cycle_id: int32 [256, 384], P('lat'), may hold values from 0 to 1535, as said below
- cycle_count: int32 [1536], replicated, may hold values from 32 to 96, as said below
- gravity: float32 [2, 2, 512], replicated, may hold values from -96 to 96
Outputs:
- smoothed: float32 [3, 32, 256, 384], P(None, 'rad', 'lat')
- potential: float32 [2, 256, 384], P(None, 'lat')
The draws below stay inside these ranges and needn't reach their ends.
Inputs may be any that keep to these rules, and one draw needn't show every extreme that they name: Every cycle holds at least one point, and cycle_id never falls along the lateral points taken row by row. cycle_count[j] is the number of points whose cycle_id is j.
All inputs are finite; a program needn't handle non-finite values.
Results may differ from the reference program's by a relative error of at most 0.0001.
Values sent between devices are 32-bit elements; how exact they have to be, the bound alone decides.
No kernel may reach another device: no remote copies, remote signals or barrier semaphores. Data moves between devices by JAX's collectives and lax.ppermute only.
A program may use at most 64 MiB of HBM per device.

```python
import math
import jax
import jax.numpy as jnp
from jax import lax

QB = 384
SWEEPS = 2
NMAT = 12
NRING = 1536
L = 512
NR = 32
NA = 256


def cycle_layout(key):
    base_key = jax.random.fold_in(key, 7)
    points = NA * QB
    base = points // NRING
    extra = points - base * NRING
    half = base // 2
    third = NRING // 3
    ranks = jnp.arange(NRING, dtype=jnp.int32)
    spread = jnp.where(ranks < third, half, jnp.where(ranks < 2 * third, 0, -half))
    spread = spread + (ranks < extra).astype(jnp.int32)
    order = jax.random.permutation(base_key, NRING).astype(jnp.int32)
    counts = (base + spread[order]).astype(jnp.int32)
    cycle_of = jnp.repeat(jnp.arange(NRING, dtype=jnp.int32), counts, total_repeat_length=points)
    return (cycle_of.reshape(NA, QB).astype(jnp.int32), counts)


def draw_cycle_id(key, part):
    return cycle_layout(key)[0]


def draw_cycle_count(key, part):
    return cycle_layout(key)[1]


def place_ends(values, key, low, top_value):
    place = [jax.random.randint(jax.random.fold_in(key, axis), (), 0, length) for axis, length in enumerate(values.shape)]
    main_axis = values.shape.index(max(values.shape))
    next_to = place[:main_axis] + [(place[main_axis] + 1) % values.shape[main_axis]] + place[main_axis + 1:]
    return values.at[tuple(place)].set(low).at[tuple(next_to)].set(top_value)


def levels(key, dims, pieces, least, high):
    factor_of, own = 1.0, jax.random.fold_in(key, 6)
    for axis_at, blocks in pieces:
        draws = jnp.exp(jax.random.uniform(jax.random.fold_in(own, axis_at), (blocks,), jnp.float32, least / len(pieces), high / len(pieces)))
        factor_of = factor_of * jnp.repeat(draws, dims[axis_at] // blocks).reshape([-1 if axis == axis_at else 1 for axis in range(len(dims))])
    return factor_of


def centred(rng, dims, deviation, reach, shards=(), kind=jnp.bfloat16):
    entries = jax.random.normal(rng, dims, jnp.float32) * deviation
    if len(shards) > 0:
        entries = levels(rng, dims, shards, -0.22, 0.18) * entries
    return jnp.clip(entries, min=-reach, max=reach).astype(kind)


def setup_inputs(seed: int = 0) -> dict:
    streams_of = jax.random.split(jax.random.key(seed), 9)
    return {
        "displacement": centred(streams_of[0], (3, NR, NA, QB), 1.0, 6.0, ((1, 8), (2, 4)), jnp.float32),
        "forcing": centred(streams_of[1], (3, NR, NA, QB), 2.0, 12.0, ((1, 8), (2, 4)), jnp.float32),
        "layer_id": place_ends(jax.random.randint(streams_of[2], (NR,), 0, NMAT), jax.random.fold_in(streams_of[2], 1), 0, NMAT - 1).astype(jnp.int32),
        "stiffness": jnp.clip(jnp.exp(jax.random.uniform(streams_of[3], (NMAT,), jnp.float32, math.log(0.3), math.log(3.0))), 0.3, 3.0),
        "coupling": jnp.clip(jax.random.uniform(streams_of[4], (NMAT, 3, 3), jnp.float32, -0.5, 0.5), -0.5, 0.5),
        "cycle_id": draw_cycle_id(jax.random.fold_in(streams_of[8], 71), 0),
        "cycle_count": draw_cycle_count(jax.random.fold_in(streams_of[8], 71), 0),
        "gravity": centred(streams_of[7], (2, 2, L), 16.0, 96.0, (), jnp.float32),
    }


OMEGA = 0.8
HIGHEST = lax.Precision.HIGHEST

def zonal_table(degrees, first_cycle, cycle_span, cycle_total):
    degree = jnp.arange(degrees, dtype=jnp.int32)[:, None]
    cycle_index = (first_cycle + jnp.arange(cycle_span, dtype=jnp.int32))[None, :]
    phases = degree * (2 * cycle_index + 1) % (4 * cycle_total)
    return jnp.cos(jnp.pi * phases.astype(jnp.float32) / (2.0 * cycle_total))

def apply_operator(padded, layer_mu, layer_coupling):
    center = padded[:, 1:-1, 1:-1, 1:-1]
    beside = padded[:, 2:, 1:-1, 1:-1] + padded[:, :-2, 1:-1, 1:-1]
    beside = beside + padded[:, 1:-1, 2:, 1:-1] + padded[:, 1:-1, :-2, 1:-1]
    beside = beside + padded[:, 1:-1, 1:-1, 2:] + padded[:, 1:-1, 1:-1, :-2]
    coupled = jnp.einsum('rcd,drab->crab', layer_coupling, center, precision=HIGHEST)
    return layer_mu[None, :, None, None] * (6.0 * center - beside) + coupled

def diagonal_of(layer_mu, layer_coupling):
    own = jnp.transpose(jnp.diagonal(layer_coupling, axis1=1, axis2=2))
    return 6.0 * layer_mu[None, :, None, None] + own[:, :, None, None]

def reference(displacement, forcing, layer_id, stiffness, coupling, cycle_id, cycle_count, gravity):
    layer_mu = stiffness[layer_id]
    layer_coupling = coupling[layer_id]
    diagonal = diagonal_of(layer_mu, layer_coupling)
    current = displacement
    for sweep_index in range(SWEEPS):
        padded = jnp.pad(current, ((0, 0), (1, 1), (1, 1), (1, 1)))
        current = current + OMEGA * (forcing - apply_operator(padded, layer_mu, layer_coupling)) / diagonal
    boundary = jnp.stack([current[0, -1], current[0, 0]])
    flat_ids = cycle_id.reshape(-1)
    cycle_sums = jax.vmap(lambda row_values: jax.ops.segment_sum(row_values, flat_ids, num_segments=NRING))(boundary.reshape(2, -1))
    cycle_means = cycle_sums / cycle_count.astype(jnp.float32)[None, :]
    basis = zonal_table(L, 0, NRING, NRING)
    scale = math.sqrt(2.0 / NRING)
    coefficients = scale * jnp.dot(cycle_means, basis.T, precision=HIGHEST)
    modes = gravity[:, 0] * coefficients[0][None, :] + gravity[:, 1] * coefficients[1][None, :]
    cycle_potential = scale * jnp.dot(modes, basis, precision=HIGHEST)
    potential = jnp.take(cycle_potential, cycle_id, axis=1)
    return (current, potential)
```

```python
import functools
import math

import jax
import jax.numpy as jnp
import numpy as np
from jax import lax
from jax.experimental import pallas as pl
from jax.experimental.pallas import tpu as pltpu
from jax.sharding import PartitionSpec as P

SWEEPS = 2
OMEGA = 0.8
LEAST_COUNT = 32
LANES = 128
SUB = 8
PAD = 8
COEFS = 16
VMEM_LIMIT = 40 * 1024 * 1024

VMEM = pl.BlockSpec(memory_space=pltpu.VMEM)
SMEM = pl.BlockSpec(memory_space=pltpu.SMEM)
ANY = pl.BlockSpec(memory_space=pl.ANY)


def basis_table(degrees, cycles):
    groups = degrees // SUB
    degree = np.arange(degrees, dtype=np.int64)[:, None]
    cycle = np.arange(cycles, dtype=np.int64)[None, :]
    phase = degree * (2 * cycle + 1) % (4 * cycles)
    table = np.cos(np.pi * phase / (2.0 * cycles)).astype(np.float32)
    table = table.reshape(SUB, groups, cycles // LANES, LANES).transpose(2, 1, 0, 3)
    return np.ascontiguousarray(table.reshape(cycles // LANES, degrees, LANES))


def iota(shape, dim):
    return lax.broadcasted_iota(jnp.int32, shape, dim)


def lane_gather(values, index):
    return jnp.take_along_axis(values, index, axis=1, mode="promise_in_bounds")


def layer_scalars(layer, lid, stiff, coup):
    material = lid[layer]
    mu = stiff[material]
    return mu, [[coup[material, c, d] for d in range(3)] for c in range(3)]


def coefficient_rows(mu, k, width=LANES):
    row = iota((COEFS, width), 0)
    top = jnp.zeros((COEFS, width), jnp.float32)
    below = jnp.ones((COEFS, width), jnp.float32)
    for c in range(3):
        diag = 6.0 * mu + k[c][c]
        others = [d for d in range(3) if d != c]
        entries = [(c, 1.0), (3 + c, mu), (6 + 2 * c, k[c][others[0]]), (7 + 2 * c, k[c][others[1]])]
        for at, value in entries:
            top = jnp.where(row == at, OMEGA * value, top)
            below = jnp.where(row == at, diag, below)
    return top / below


def spread(row, width):
    full = jnp.broadcast_to(row, (SUB, LANES))
    return jnp.concatenate([full] * (width // LANES), axis=1)


def beside(current, before, after):
    width = current.shape[1]
    sub, col = iota(current.shape, 0), iota(current.shape, 1)
    up = jnp.where(sub == 0, jnp.broadcast_to(before, current.shape), pltpu.roll(current, 1, 0))
    down = jnp.where(sub == SUB - 1, jnp.broadcast_to(after, current.shape), pltpu.roll(current, SUB - 1, 0))
    left = jnp.where(col == 0, 0.0, pltpu.roll(current, 1, 1))
    right = jnp.where(col == width - 1, 0.0, pltpu.roll(current, width - 1, 1))
    return (up + down) + (left + right)


def relax(c, centers, neighbours, force, rows):
    d0, d1 = [d for d in range(3) if d != c]
    value = rows[c] * force + rows[3 + c] * neighbours
    value = value - (rows[6 + 2 * c] * centers[d0] + rows[7 + 2 * c] * centers[d1])
    return value + (1.0 - OMEGA) * centers[c]


def analysis_kernel(
    disp, forc, lid, stiff, coup, ids, cnt, tbl,
    up, dn, pay, held, coef_out,
    ut, ub, uf, ft, fb, st, sb, ue, fe, tab, cur, far_sem, near_sem, tab_sem,
):
    layers, rows, width = disp.shape[1:]
    chunks = cnt.shape[0]
    groups = tbl.shape[1] // SUB
    per_row = width // LANES
    lat, lats = lax.axis_index("lat"), lax.axis_size("lat")
    rad, rads = lax.axis_index("rad"), lax.axis_size("rad")
    bottom = rad == 0
    edge = jnp.where(bottom, 0, layers - 1)
    inner = jnp.where(bottom, 1, layers - 2)
    deep = jnp.where(bottom, 2, layers - 3)
    inside = pl.ds(PAD, rows)

    near = [
        pltpu.make_async_copy(disp.at[:, edge], ut.at[:, inside], near_sem.at[0]),
        pltpu.make_async_copy(disp.at[:, inner], ub.at[:, inside], near_sem.at[1]),
        pltpu.make_async_copy(disp.at[0, deep], uf.at[inside], near_sem.at[2]),
        pltpu.make_async_copy(forc.at[:, edge], ft.at[:, inside], near_sem.at[3]),
        pltpu.make_async_copy(forc.at[0, inner], fb.at[inside], near_sem.at[4]),
    ]
    for copy in near:
        copy.start()
    edges = [
        pltpu.make_async_copy(disp.at[:, :, pl.ds(0, SUB)], ue.at[0], near_sem.at[5]),
        pltpu.make_async_copy(disp.at[:, :, pl.ds(rows - SUB, SUB)], ue.at[1], near_sem.at[6]),
        pltpu.make_async_copy(forc.at[:, :, pl.ds(0, SUB)], fe.at[0], near_sem.at[7]),
        pltpu.make_async_copy(forc.at[:, :, pl.ds(rows - SUB, SUB)], fe.at[1], near_sem.at[8]),
    ]
    for copy in edges:
        copy.start()
    table = [pltpu.make_async_copy(tbl.at[q], tab.at[q], tab_sem.at[q]) for q in range(chunks)]
    for copy in table:
        copy.start()
    bulk = [
        pltpu.make_async_copy(disp.at[:, layers - 1], up.at[0], far_sem.at[0]),
        pltpu.make_async_copy(disp.at[:, layers - 2], up.at[1], far_sem.at[1]),
        pltpu.make_async_copy(forc.at[:, layers - 1], up.at[2], far_sem.at[2]),
        pltpu.make_async_copy(disp.at[:, 0], dn.at[0], far_sem.at[3]),
        pltpu.make_async_copy(disp.at[:, 1], dn.at[1], far_sem.at[4]),
        pltpu.make_async_copy(forc.at[:, 0], dn.at[2], far_sem.at[5]),
    ]
    for copy in bulk:
        copy.start()

    blank = jnp.zeros((SUB, width), jnp.float32)
    for ref in (ut, ub, ft):
        for c in range(3):
            ref[c, 0:PAD, :] = blank
            ref[c, PAD + rows:, :] = blank
    for ref in (uf, fb):
        ref[0:PAD, :] = blank
        ref[PAD + rows:, :] = blank

    parity = lax.rem(rad, 2)
    coef_low = coefficient_rows(*layer_scalars(0, lid, stiff, coup))
    coef_high = coefficient_rows(*layer_scalars(layers - 1, lid, stiff, coup))
    coef_out[0] = jnp.where(parity == 0, coef_high, coef_low)
    coef_out[1] = jnp.where(parity == 0, coef_low, coef_high)
    cur[0] = jnp.where(bottom, coef_low, coef_high)
    cur[1] = coefficient_rows(*layer_scalars(inner, lid, stiff, coup))

    lane = iota((1, LANES), 1)
    counts = cnt[...]
    ends = counts
    step = 1
    while step < LANES:
        ends = ends + jnp.where(iota(counts.shape, 1) >= step, pltpu.roll(ends, step, 1), 0)
        step *= 2
    run = jnp.zeros((1, 1), jnp.int32)
    end_rows = []
    for q in range(chunks):
        row = ends[q:q + 1, :]
        end_rows.append(jnp.broadcast_to(row + run, (SUB, LANES)))
        run = run + row[:, LANES - 1:]

    sub8, lane8 = iota((SUB, LANES), 0), iota((SUB, LANES), 1)
    first_id = jnp.broadcast_to(ids[0:1, 0:1], (SUB, LANES))
    last_id = jnp.broadcast_to(ids[rows - 1:rows, width - 1:width], (SUB, LANES))
    before = sub8 < 2
    index = jnp.where(before, first_id - 1 - lane8, last_id + lane8)
    place, part = jnp.bitwise_and(index, LANES - 1), jnp.right_shift(index, 7)
    limits = jnp.where(before, 0, 2 ** 30)
    for q in range(chunks):
        limits = jnp.where(part == q, lane_gather(end_rows[q], place), limits)
    limits = jnp.where(before, limits, -limits)
    wide_sub = iota((SUB, width), 0)
    wide_before = wide_sub < 2
    row_of = lat * rows + jnp.where(wide_before, wide_sub - 2, wide_sub - 2 + rows)
    point = row_of * width + iota((SUB, width), 1)
    point = jnp.where(wide_before, point, -1 - point)
    passed = jnp.zeros((SUB, width), jnp.int32)
    for i in range(2 * width // LEAST_COUNT + 2):
        limit = jnp.broadcast_to(limits[:, i:i + 1], (SUB, width))
        passed = passed + jnp.where(point < limit, 1, 0)
    wide = lambda x: jnp.concatenate([x] * per_row, axis=1)
    spill_ids = jnp.where(wide_before, wide(first_id) - passed, wide(last_id) + passed)
    spill_ids = jnp.where(wide_sub < 4, spill_ids, 0)

    for copy in near:
        copy.wait()

    total = rows // SUB + 2
    outer = [spread(cur[0, j:j + 1, :], width) for j in range(12)]
    inward = [spread(cur[1, j:j + 1, :], width) for j in range(12)]
    mu_inner = inward

    def group(ref, g):
        return ref[SUB * g:SUB * g + SUB, :]

    def lateral(ref, g):
        zero = jnp.zeros((1, width), jnp.float32)
        row_before = ref[SUB * g - 1:SUB * g, :] if g > 0 else zero
        row_after = ref[SUB * g + SUB:SUB * g + SUB + 1, :] if g < total - 1 else zero
        return beside(group(ref, g), row_before, row_after)

    for g in range(total):
        tops = [group(ut.at[c], g) for c in range(3)]
        inners = [group(ub.at[c], g) for c in range(3)]
        keep = None
        if g == 0:
            keep = lat > 0
        if g == total - 1:
            keep = lat < lats - 1
        for c in range(3):
            value = relax(c, tops, inners[c] + lateral(ut.at[c], g), group(ft.at[c], g), outer)
            if keep is not None:
                value = jnp.where(keep, value, 0.0)
            st[c, SUB * g:SUB * g + SUB, :] = value
        value = relax(0, inners, tops[0] + group(uf, g) + lateral(ub.at[0], g), group(fb, g), mu_inner)
        if keep is not None:
            value = jnp.where(keep, value, 0.0)
        sb[SUB * g:SUB * g + SUB, :] = value

    def swept(g):
        sts = [group(st.at[c], g) for c in range(3)]
        return relax(0, sts, group(sb, g) + lateral(st.at[0], g), group(ft.at[0], g), outer)

    met = (width - 2) // LEAST_COUNT + 2
    parts = [jnp.zeros((SUB, LANES), jnp.float32) for _ in range(chunks)]

    def add_window(values, cycle, parts):
        first = cycle[:, 0:1]
        offset = cycle - jnp.broadcast_to(first, cycle.shape)
        window = jnp.zeros((SUB, LANES), jnp.float32)
        for t in range(met):
            total_t = jnp.sum(jnp.where(offset == t, values, 0.0), axis=1, keepdims=True)
            window = jnp.where(lane8 == t, jnp.broadcast_to(total_t, window.shape), window)
        start = jnp.broadcast_to(first, (SUB, LANES))
        out = []
        for q in range(chunks):
            at = q * LANES + lane8 - start
            got = lane_gather(window, jnp.bitwise_and(at, LANES - 1))
            out.append(parts[q] + jnp.where(jnp.right_shift(at, 7) == 0, got, 0.0))
        return out

    head, tail = swept(0), swept(total - 1)
    spilled = jnp.where(wide_before, pltpu.roll(head, 2, 0), pltpu.roll(tail, 2, 0))
    weight = jnp.where(wide_before, jnp.where(lat > 0, 1.0, 0.0), jnp.where(lat < lats - 1, 1.0, 0.0))
    parts = add_window(spilled * jnp.where(wide_sub < 4, weight, 0.0), spill_ids, parts)
    for g in range(1, total - 1):
        parts = add_window(swept(g), ids[SUB * (g - 1):SUB * g, :], parts)

    means = []
    for q in range(chunks):
        mean = jnp.sum(parts[q], axis=0, keepdims=True) / counts[q:q + 1, :].astype(jnp.float32)
        means.append(jnp.broadcast_to(mean, (SUB, LANES)))

    for copy in table:
        copy.wait()
    half = jnp.where(bottom, groups, 0)
    result = jnp.zeros((SUB, LANES), jnp.float32)
    for g in range(groups):
        acc = tab[0, SUB * g:SUB * g + SUB, :] * means[0]
        for q in range(1, chunks):
            acc = acc + tab[q, SUB * g:SUB * g + SUB, :] * means[q]
        column = jnp.sum(acc, axis=1, keepdims=True)
        result = jnp.where(lane8 == g + half, jnp.broadcast_to(column, result.shape), result)
    at_end = jnp.logical_or(bottom, rad == rads - 1)
    pay[0:SUB, :] = jnp.concatenate(
        [jnp.where(at_end, result, 0.0)] + [jnp.zeros((SUB, LANES), jnp.float32)] * (per_row - 1), axis=1
    )

    for copy in edges:
        copy.wait()
    tall = 3 * layers

    def pack(side, ref, base):
        first = 0 if side == 0 else SUB - 2
        last = 0 if side == 0 else SUB - 1
        for c in range(3):
            for r in range(layers):
                at = base + 2 * (c * layers + r)
                ref[at:at + 2, :] = ue[side, c, r, first:first + 2, :]
                at = base + 2 * tall + c * layers + r
                ref[at:at + 1, :] = fe[side, c, r, last:last + 1, :]

    @pl.when(lax.rem(lat, 2) == 0)
    def _():
        pack(1, pay, SUB)
        pack(0, held, 0)

    @pl.when(lax.rem(lat, 2) == 1)
    def _():
        pack(0, pay, SUB)
        pack(1, held, 0)

    for copy in bulk:
        copy.wait()


def sweep_kernel(
    disp, forc, lid, stiff, coup, lo, hi, low, high, cor_lo, cor_hi, coef_lo, coef_hi,
    out,
    u, f, s, cf, near_sem,
):
    layers, rows, width = disp.shape[1:]
    lat, lats = lax.axis_index("lat"), lax.axis_size("lat")
    inside = pl.ds(PAD, rows)
    top = layers + 2
    copies = [
        pltpu.make_async_copy(disp, u.at[:, pl.ds(2, layers), inside], near_sem.at[0]),
        pltpu.make_async_copy(lo.at[0], u.at[:, 1, inside], near_sem.at[1]),
        pltpu.make_async_copy(lo.at[1], u.at[:, 0, inside], near_sem.at[2]),
        pltpu.make_async_copy(hi.at[0], u.at[:, top, inside], near_sem.at[3]),
        pltpu.make_async_copy(hi.at[1], u.at[:, top + 1, inside], near_sem.at[4]),
        pltpu.make_async_copy(forc, f.at[:, pl.ds(2, layers), inside], near_sem.at[5]),
        pltpu.make_async_copy(lo.at[2], f.at[:, 1, inside], near_sem.at[6]),
        pltpu.make_async_copy(hi.at[2], f.at[:, top, inside], near_sem.at[7]),
    ]
    for copy in copies:
        copy.start()

    cf[1] = coef_lo[...]
    cf[top] = coef_hi[...]
    for r in range(layers):
        cf[2 + r] = coefficient_rows(*layer_scalars(r, lid, stiff, coup))
    tall = 3 * layers
    end = PAD + rows
    for c in range(3):
        for r in range(layers):
            at = 2 * (c * layers + r)
            u[c, 2 + r, PAD - 2:PAD, :] = low[at:at + 2, :]
            u[c, 2 + r, end:end + 2, :] = high[at:at + 2, :]
            at = 2 * tall + c * layers + r
            f[c, 2 + r, PAD - 1:PAD, :] = low[at:at + 1, :]
            f[c, 2 + r, end:end + 1, :] = high[at:at + 1, :]
        u[c, 1, PAD - 1:PAD, :] = cor_lo[c:c + 1, :]
        u[c, 1, end:end + 1, :] = cor_lo[3 + c:4 + c, :]
        u[c, top, PAD - 1:PAD, :] = cor_hi[c:c + 1, :]
        u[c, top, end:end + 1, :] = cor_hi[3 + c:4 + c, :]
    for copy in copies:
        copy.wait()

    total = rows // SUB + 2

    def update(src, layer, g):
        rows_of = [spread(cf[layer, j:j + 1, :], width) for j in range(12)]
        start = pl.multiple_of(SUB * g, SUB)
        here = pl.ds(start, SUB)
        ahead = pl.ds(jnp.maximum(start - 1, 0), 1)
        behind = pl.ds(jnp.minimum(start + SUB, SUB * total - 1), 1)
        centers = [src[c, layer, here, :] for c in range(3)]
        values = []
        for c in range(3):
            near = src[c, layer - 1, here, :] + src[c, layer + 1, here, :]
            near = near + beside(centers[c], src[c, layer, ahead, :], src[c, layer, behind, :])
            values.append(relax(c, centers, near, f[c, layer, here, :], rows_of))
        return values, here

    def first(step, carry):
        layer, g = 1 + step // total, lax.rem(step, total)
        values, here = update(u, layer, g)
        drop = jnp.logical_or(
            jnp.logical_and(g == 0, lat == 0), jnp.logical_and(g == total - 1, lat == lats - 1)
        )
        for c in range(3):
            s[c, layer, here, :] = jnp.where(drop, 0.0, values[c])
        return carry

    lax.fori_loop(0, (layers + 2) * total, first, 0)

    inner = total - 2

    def second(step, carry):
        layer, g = 2 + step // inner, 1 + lax.rem(step, inner)
        values, here = update(s, layer, g)
        there = pl.ds(pl.multiple_of(SUB * (g - 1), SUB), SUB)
        for c in range(3):
            out[c, layer - 2, there, :] = values[c]
        return carry

    lax.fori_loop(0, layers * inner, second, 0)


def synthesis_kernel(scale, coef, gain_a, gain_b, ids, tbl, out, tab, tab_sem):
    rows, width = ids.shape
    chunks = tbl.shape[0]
    groups = tbl.shape[1] // SUB
    table = [pltpu.make_async_copy(tbl.at[q], tab.at[q], tab_sem.at[q]) for q in range(chunks)]
    for copy in table:
        copy.start()
    lane8 = iota((SUB, LANES), 1)
    here = coef[...]
    other = pltpu.roll(here, groups, 1)
    left = lane8 < groups
    surface = jnp.where(left, here, other)
    core = jnp.where(left, other, here)
    modes = (gain_a[...] * surface + gain_b[...] * core) * scale
    for copy in table:
        copy.wait()
    zero = jnp.zeros((SUB, LANES), jnp.float32)
    sums = [[zero] * chunks for _ in range(2)]
    for g in range(groups):
        factors = [
            jnp.broadcast_to(modes[:, k * groups + g:k * groups + g + 1], (SUB, LANES)) for k in range(2)
        ]
        for q in range(chunks):
            block = tab[q, SUB * g:SUB * g + SUB, :]
            for k in range(2):
                sums[k][q] = sums[k][q] + factors[k] * block
    for k in range(2):
        for q in range(chunks):
            sums[k][q] = jnp.broadcast_to(jnp.sum(sums[k][q], axis=0, keepdims=True), (SUB, LANES))
    for a in range(rows // SUB):
        for b in range(width // LANES):
            spot = (slice(SUB * a, SUB * a + SUB), slice(LANES * b, LANES * b + LANES))
            cycle = ids[spot]
            place, part = jnp.bitwise_and(cycle, LANES - 1), jnp.right_shift(cycle, 7)
            values = [zero, zero]
            for q in range(chunks):
                chosen = part == q
                for k in range(2):
                    values[k] = jnp.where(chosen, lane_gather(sums[k][q], place), values[k])
            for k in range(2):
                out[(k,) + spot] = values[k]


def even_pairs(count):
    return [(i, i ^ 1) for i in range(count)]


def odd_pairs(count):
    pairs = []
    for i in range(1, count, 2):
        j = (i + 1) % count
        pairs += [(i, j), (j, i)]
    return pairs


def local(displacement, forcing, layer_id, stiffness, coupling, cycle_id, cycle_count, gravity):
    _, layers, rows, width = displacement.shape
    cycles, degrees = cycle_count.shape[0], gravity.shape[2]
    chunks, groups = cycles // LANES, degrees // SUB
    if 2 * groups != LANES or layers < 3:
        raise ValueError("unsupported sizes")
    lat, lats = lax.axis_index("lat"), lax.axis_size("lat")
    rad, rads = lax.axis_index("rad"), lax.axis_size("rad")
    lat_odd, rad_odd = lat % 2 == 1, rad % 2 == 1
    f32 = jnp.float32
    table = jnp.asarray(basis_table(degrees, cycles))
    tall = 3 * layers
    padded = rows + 2 * PAD
    edge_rows = -(-3 * tall // SUB) * SUB
    face = jax.ShapeDtypeStruct((3, 3, rows, width), f32)
    params = pltpu.CompilerParams(vmem_limit_bytes=VMEM_LIMIT)

    up, dn, pay, held, coefs = pl.pallas_call(
        analysis_kernel,
        out_shape=(
            face, face,
            jax.ShapeDtypeStruct((SUB + edge_rows, width), f32),
            jax.ShapeDtypeStruct((edge_rows, width), f32),
            jax.ShapeDtypeStruct((2, COEFS, LANES), f32),
        ),
        in_specs=[ANY, ANY, SMEM, SMEM, SMEM, VMEM, VMEM, ANY],
        out_specs=(ANY, ANY, VMEM, VMEM, VMEM),
        scratch_shapes=[
            pltpu.VMEM((3, padded, width), f32),
            pltpu.VMEM((3, padded, width), f32),
            pltpu.VMEM((padded, width), f32),
            pltpu.VMEM((3, padded, width), f32),
            pltpu.VMEM((padded, width), f32),
            pltpu.VMEM((3, padded, width), f32),
            pltpu.VMEM((padded, width), f32),
            pltpu.VMEM((2, 3, layers, SUB, width), f32),
            pltpu.VMEM((2, 3, layers, SUB, width), f32),
            pltpu.VMEM((chunks, degrees, LANES), f32),
            pltpu.VMEM((2, COEFS, LANES), f32),
            pltpu.SemaphoreType.DMA((6,)),
            pltpu.SemaphoreType.DMA((9,)),
            pltpu.SemaphoreType.DMA((chunks,)),
        ],
        compiler_params=params,
        name="analysis",
    )(displacement, forcing, layer_id, stiffness, coupling, cycle_id, cycle_count.reshape(chunks, LANES), table)

    low_far = lax.ppermute(up, "rad", [(i, i + 1) for i in range(rads - 1)])
    high_far = lax.ppermute(dn, "rad", [(i + 1, i) for i in range(rads - 1)])

    butterfly = lats == 4 and rads == 8
    coef = pay[:SUB, :LANES]
    got1 = lax.ppermute(pay, "lat", even_pairs(lats))
    if butterfly:
        coef = coef + got1[:SUB, :LANES]
    else:
        coef = lax.psum(coef, ("lat", "rad"))
    strip = jnp.concatenate([coef, jnp.zeros((SUB, width - LANES), f32)], axis=1)
    got2 = lax.ppermute(jnp.concatenate([strip, held], axis=0), "lat", odd_pairs(lats))
    if butterfly:
        coef = coef + got2[:SUB, :LANES]
    edge1, edge2 = got1[SUB:], got2[SUB:]
    low = jnp.where(lat > 0, jnp.where(lat_odd, edge1, edge2), 0.0)
    high = jnp.where(lat < lats - 1, jnp.where(lat_odd, edge2, edge1), 0.0)

    def corners(layer):
        picks = [low[2 * (c * layers + layer) + 1][None] for c in range(3)]
        picks += [high[2 * (c * layers + layer)][None] for c in range(3)]
        return jnp.concatenate(picks + [jnp.zeros((2, width), f32)], axis=0)

    def split(block):
        return jnp.concatenate(jnp.split(block, width // LANES, axis=1), axis=0)

    corner_low, corner_high = split(corners(0)), split(corners(layers - 1))
    send1 = jnp.where(rad_odd, corner_low, corner_high)
    send2 = jnp.where(rad_odd, corner_high, corner_low)
    got3 = lax.ppermute(jnp.concatenate([coef, coefs[0], send1], axis=0), "rad", even_pairs(rads))
    if butterfly:
        coef = coef + got3[:SUB]
    got4 = lax.ppermute(jnp.concatenate([coef, coefs[1], send2], axis=0), "rad", odd_pairs(rads))
    if butterfly:
        coef = coef + got4[:SUB]
        coef = coef + lax.ppermute(coef, "rad", [(0, 3), (7, 4), (2, 5), (5, 2), (1, 6), (6, 1)])

    below = jnp.where(rad > 0, jnp.where(rad_odd, got3, got4), 0.0)
    above = jnp.where(rad < rads - 1, jnp.where(rad_odd, got4, got3), 0.0)

    def join(block):
        return jnp.concatenate(jnp.split(block, width // LANES, axis=0), axis=1)

    corner_at = SUB + COEFS
    smoothed = pl.pallas_call(
        sweep_kernel,
        out_shape=jax.ShapeDtypeStruct(displacement.shape, f32),
        in_specs=[ANY, ANY, SMEM, SMEM, SMEM, ANY, ANY] + [VMEM] * 6,
        out_specs=VMEM,
        scratch_shapes=[
            pltpu.VMEM((3, layers + 4, padded, width), f32),
            pltpu.VMEM((3, layers + 4, padded, width), f32),
            pltpu.VMEM((3, layers + 4, padded, width), f32),
            pltpu.VMEM((layers + 4, COEFS, LANES), f32),
            pltpu.SemaphoreType.DMA((8,)),
        ],
        compiler_params=params,
        name="sweeps",
    )(
        displacement, forcing, layer_id, stiffness, coupling, low_far, high_far, low, high,
        join(below[corner_at:]), join(above[corner_at:]), below[SUB:corner_at], above[SUB:corner_at],
    )

    shaped = gravity.reshape(2, 2, SUB, groups)
    gain_a = jnp.concatenate([shaped[0, 0], shaped[1, 0]], axis=1)
    gain_b = jnp.concatenate([shaped[0, 1], shaped[1, 1]], axis=1)
    potential = pl.pallas_call(
        functools.partial(synthesis_kernel, 2.0 / cycles),
        out_shape=jax.ShapeDtypeStruct((2, rows, width), f32),
        in_specs=[VMEM, VMEM, VMEM, VMEM, ANY],
        out_specs=VMEM,
        scratch_shapes=[
            pltpu.VMEM((chunks, degrees, LANES), f32),
            pltpu.SemaphoreType.DMA((chunks,)),
        ],
        compiler_params=params,
        name="synthesis",
    )(coef, gain_a, gain_b, cycle_id, table)
    return smoothed, potential


def solution(mesh):
    in_specs = (
        P(None, "rad", "lat", None),
        P(None, "rad", "lat", None),
        P("rad"),
        P(),
        P(),
        P("lat", None),
        P(),
        P(),
    )
    out_specs = (P(None, "rad", "lat", None), P(None, "lat", None))
    return jax.shard_map(local, mesh=mesh, in_specs=in_specs, out_specs=out_specs, check_vma=False)
```

```python
import functools
import math

import jax
import jax.numpy as jnp
import numpy as np
from jax import lax
from jax.experimental import pallas as pl
from jax.experimental.pallas import tpu as pltpu
from jax.sharding import PartitionSpec as P

SWEEPS = 2
OMEGA = 0.8
LEAST_COUNT = 32
LANES = 128
SUB = 8
PAD = 8
COEFS = 16
BATCH = 5
VMEM_LIMIT = 16 * 1024 * 1024

VMEM = pl.BlockSpec(memory_space=pltpu.VMEM)
SMEM = pl.BlockSpec(memory_space=pltpu.SMEM)
HBM = pl.BlockSpec(memory_space=pltpu.HBM)
ANY = pl.BlockSpec(memory_space=pl.ANY)


def basis_table(degrees, cycles):
    groups = degrees // SUB
    degree = np.arange(degrees, dtype=np.int64)[:, None]
    cycle = np.arange(cycles, dtype=np.int64)[None, :]
    phase = degree * (2 * cycle + 1) % (4 * cycles)
    table = np.cos(np.pi * phase / (2.0 * cycles)).astype(np.float32)
    table = table.reshape(SUB, groups, cycles // LANES, LANES).transpose(2, 1, 0, 3)
    return np.ascontiguousarray(table.reshape(cycles // LANES, degrees, LANES))


def iota(shape, dim):
    return lax.broadcasted_iota(jnp.int32, shape, dim)


def lane_gather(values, index):
    return jnp.take_along_axis(values, index, axis=1, mode="promise_in_bounds")


def layer_scalars(layer, lid, stiff, coup):
    material = lid[layer]
    mu = stiff[material]
    return mu, [[coup[c, d, material] for d in range(3)] for c in range(3)]


def coefficient_rows(mu, k, width=LANES):
    row = iota((COEFS, width), 0)
    top = jnp.zeros((COEFS, width), jnp.float32)
    below = jnp.ones((COEFS, width), jnp.float32)
    for c in range(3):
        diag = 6.0 * mu + k[c][c]
        others = [d for d in range(3) if d != c]
        entries = [(c, 1.0), (3 + c, mu), (6 + 2 * c, k[c][others[0]]), (7 + 2 * c, k[c][others[1]])]
        for at, value in entries:
            top = jnp.where(row == at, OMEGA * value, top)
            below = jnp.where(row == at, diag, below)
    return top / below


def roll_rows(value, before, after):
    sub = iota(value.shape, 0)
    up = jnp.where(sub == 0, jnp.broadcast_to(before, value.shape), pltpu.roll(value, 1, 0))
    down = jnp.where(sub == SUB - 1, jnp.broadcast_to(after, value.shape), pltpu.roll(value, SUB - 1, 0))
    return up + down


def roll_columns(values):
    lane = iota(values[0].shape, 1)
    right = [pltpu.roll(value, 1, 1) for value in values]
    left = [pltpu.roll(value, LANES - 1, 1) for value in values]
    last = len(values) - 1
    return [
        jnp.where(lane == 0, right[j - 1] if j > 0 else 0.0, right[j])
        + jnp.where(lane == LANES - 1, left[j + 1] if j < last else 0.0, left[j])
        for j in range(len(values))
    ]


def relax(c, centers, neighbours, force, rows):
    d0, d1 = [d for d in range(3) if d != c]
    value = rows[c] * force + rows[3 + c] * neighbours
    value = value - (rows[6 + 2 * c] * centers[d0] + rows[7 + 2 * c] * centers[d1])
    return value + (1.0 - OMEGA) * centers[c]


def chunk(j):
    return pl.ds(LANES * j, LANES)


def spans(per_row, ref, *index):
    return [ref[index + (chunk(j),)] for j in range(per_row)]


def lane_scan(values, steps):
    lane = iota(values.shape, 1)
    step = 1
    while step < steps:
        values = values + jnp.where(lane >= step, pltpu.roll(values, step, 1), 0)
        step *= 2
    return values


def analysis_kernel(
    disp, forc, lid, stiff, coup, ids, cnt, tbl,
    up, dn, pay, held, send1, send2, every,
    u, f, cyc, num, tab, mat, s, windows, lids, stiffs, coups, first_ids, last_ids, near_sem, far_sem, tab_sem,
):
    layers, rows, width = disp.shape[1:]
    chunks = cnt.shape[0]
    groups = tbl.shape[1] // SUB
    per_row = width // LANES
    lat, lats = lax.axis_index("lat"), lax.axis_size("lat")
    rad, rads = lax.axis_index("rad"), lax.axis_size("rad")
    bottom = rad == 0
    at_end = jnp.logical_or(bottom, rad == rads - 1)
    edge = jnp.where(bottom, 0, layers - 1)
    inner = jnp.where(bottom, 1, layers - 2)
    deep = jnp.where(bottom, 2, layers - 3)
    total = rows // SUB

    small = [
        pltpu.make_async_copy(lid, lids, near_sem.at[0]),
        pltpu.make_async_copy(stiff, stiffs, near_sem.at[1]),
        pltpu.make_async_copy(coup, coups, near_sem.at[2]),
        pltpu.make_async_copy(ids.at[pl.ds(0, SUB), pl.ds(0, LANES)], first_ids, near_sem.at[3]),
        pltpu.make_async_copy(
            ids.at[pl.ds(rows - SUB, SUB), pl.ds(width - LANES, LANES)], last_ids, near_sem.at[4]
        ),
        pltpu.make_async_copy(cnt, num, near_sem.at[5]),
        pltpu.make_async_copy(ids, cyc, near_sem.at[6]),
    ]
    large = [
        pltpu.make_async_copy(disp, u, near_sem.at[7]),
        pltpu.make_async_copy(forc, f, near_sem.at[8]),
    ]
    table = [pltpu.make_async_copy(tbl.at[q], tab.at[q], tab_sem.at[q]) for q in range(chunks)]
    for copy in small + large + table:
        copy.start()
    bulk = [
        pltpu.make_async_copy(u.at[:, layers - 1], up.at[0], far_sem.at[0]),
        pltpu.make_async_copy(u.at[:, layers - 2], up.at[1], far_sem.at[1]),
        pltpu.make_async_copy(f.at[:, layers - 1], up.at[2], far_sem.at[2]),
        pltpu.make_async_copy(u.at[:, 0], dn.at[0], far_sem.at[3]),
        pltpu.make_async_copy(u.at[:, 1], dn.at[1], far_sem.at[4]),
        pltpu.make_async_copy(f.at[:, 0], dn.at[2], far_sem.at[5]),
    ]
    for copy in small:
        copy.wait()

    for r in range(layers):
        every[r] = coefficient_rows(*layer_scalars(r, lids, stiffs, coups))
    odd = lax.rem(rad, 2) == 1
    send1[...] = every[jnp.where(odd, 0, layers - 1)]
    send2[...] = every[jnp.where(odd, layers - 1, 0)]

    sub8, lane8 = iota((SUB, LANES), 0), iota((SUB, LANES), 1)
    before = sub8 < 2
    zero = jnp.zeros((SUB, LANES), jnp.float32)
    reach = 2 * width // LEAST_COUNT + 2
    first, last = first_ids[0, 0], last_ids[SUB - 1, LANES - 1]

    for copy in large:
        copy.wait()
    for copy in bulk:
        copy.start()
    pay[0:SUB, :] = jnp.zeros((SUB, width), jnp.float32)

    @pl.when(at_end)
    def _():
        own_first = jnp.zeros((SUB, LANES), jnp.int32)
        own_last = own_first
        for j in range(per_row):
            own_first = own_first + jnp.where(cyc[0:SUB, LANES * j:LANES * j + LANES] == first, 1, 0)
            own_last = own_last + jnp.where(cyc[rows - SUB:rows, LANES * j:LANES * j + LANES] == last, 1, 0)

        def total_of(count):
            count = jnp.sum(count.astype(jnp.float32), axis=1, keepdims=True)
            return jnp.broadcast_to(jnp.sum(count, axis=0, keepdims=True), (SUB, LANES)).astype(jnp.int32)

        held_here = jnp.where(before, total_of(own_first), total_of(own_last))
        index = jnp.where(before, first - lane8, last + lane8)
        place, part = jnp.bitwise_and(index, LANES - 1), jnp.right_shift(index, 7)
        lengths = jnp.full((SUB, LANES), 2 ** 20, jnp.int32)
        part_first, part_last = jnp.right_shift(first, 7), jnp.right_shift(last, 7)
        for q in (part_first - 1, part_first, part_last, part_last + 1):
            row = num[pl.ds(jnp.clip(q, 0, chunks - 1), 1), :]
            known = jnp.logical_and(part == q, jnp.logical_and(part >= 0, part < chunks))
            lengths = jnp.where(known, lane_gather(jnp.broadcast_to(row, (SUB, LANES)), place), lengths)
        lengths = lengths - jnp.where(lane8 == 0, held_here, 0)
        limits = lane_scan(lengths, reach)
        caps = [jnp.broadcast_to(limits[:, i:i + 1], (SUB, LANES)) for i in range(reach)]
        spill_ids = []
        for j in range(per_row):
            column = LANES * j + lane8
            away = jnp.where(before, (width - 1 - column) + jnp.where(sub8 == 0, width, 0),
                             column + jnp.where(sub8 == 3, width, 0))
            passed = jnp.zeros((SUB, LANES), jnp.int32)
            for i in range(reach):
                passed = passed + jnp.where(away >= caps[i], 1, 0)
            spill_ids.append(jnp.where(sub8 < 4, jnp.where(before, first - passed, last + passed), 0))

        mat[0] = every[edge]
        mat[1] = every[inner]
        outer = [jnp.broadcast_to(mat[0, j:j + 1, :], (SUB, LANES)) for j in range(12)]
        below = [jnp.broadcast_to(mat[1, j:j + 1, :], (SUB, LANES)) for j in range(12)]

        def rows_of(g):
            return slice(SUB * g, SUB * g + SUB)

        none = jnp.zeros((1, LANES), jnp.float32)

        def lateral(ref, g, index, ends):
            values = spans(per_row, ref, *index, rows_of(g))
            aside = roll_columns(values)
            out = []
            for j in range(per_row):
                above = ref[index + (slice(SUB * g - 1, SUB * g), chunk(j))] if g > 0 else ends[0][j]
                under = ref[index + (slice(SUB * g + SUB, SUB * g + SUB + 1), chunk(j))] if g < total - 1 else ends[1][j]
                out.append(roll_rows(values[j], above, under) + aside[j])
            return out

        nothing = [[none] * per_row] * 2
        for g in range(total):
            here = rows_of(g)
            tops = [spans(per_row, u, c, edge, here) for c in range(3)]
            unders = [spans(per_row, u, c, inner, here) for c in range(3)]
            deeper = spans(per_row, u, 0, deep, here)
            for c in range(3):
                near = lateral(u, g, (c, edge), nothing)
                force = spans(per_row, f, c, edge, here)
                for j in range(per_row):
                    s[c, here, chunk(j)] = relax(
                        c, [top[j] for top in tops], near[j] + unders[c][j], force[j], outer
                    )
            near = lateral(u, g, (0, inner), nothing)
            force = spans(per_row, f, 0, inner, here)
            for j in range(per_row):
                s[3, here, chunk(j)] = relax(
                    0, [under[j] for under in unders], near[j] + tops[0][j] + deeper[j], force[j], below
                )
        low_in = jnp.where(lat > 0, 1.0, 0.0)
        high_in = jnp.where(lat < lats - 1, 1.0, 0.0)
        weight = jnp.where(sub8 == 1, low_in, jnp.where(sub8 == 2, high_in, 0.0))

        def ends_of(ref, index, j):
            low = jnp.broadcast_to(ref[index + (slice(0, 1), chunk(j))], (SUB, LANES))
            high = jnp.broadcast_to(ref[index + (slice(rows - 1, rows), chunk(j))], (SUB, LANES))
            return jnp.where(sub8 == 1, low, jnp.where(sub8 == 2, high, 0.0))

        over = [[outer[3 + c] * ends_of(u, (c, edge), j) * weight for j in range(per_row)] for c in range(3)]
        over_inner = [below[3] * ends_of(u, (0, inner), j) * weight for j in range(per_row)]
        aside = roll_columns(over[0])
        spill = []
        for j in range(per_row):
            shifted = jnp.where(sub8 == 0, pltpu.roll(over[0][j], SUB - 1, 0),
                                jnp.where(sub8 == 3, pltpu.roll(over[0][j], 1, 0), 0.0))
            near = over_inner[j] + aside[j] + shifted + ends_of(s, (0,), j)
            value = relax(0, [over[c][j] for c in range(3)], near, zero, outer)
            spill.append(value * jnp.where(before, low_in, high_in))
        ends = [[over[0][j][1:2, :] for j in range(per_row)], [over[0][j][2:3, :] for j in range(per_row)]]

        met = (width - 2) // LEAST_COUNT + 2

        def window_of(values, cycles):
            start = jnp.broadcast_to(cycles[0][:, 0:1], (SUB, LANES))
            offsets = [cycle - start for cycle in cycles]
            window = zero
            for t in range(met):
                picked = [jnp.where(offset == t, value, 0.0) for offset, value in zip(offsets, values)]
                sum_t = jnp.sum(functools.reduce(jnp.add, picked), axis=1, keepdims=True)
                window = jnp.where(lane8 == t, jnp.broadcast_to(sum_t, (SUB, LANES)), window)
            return window, start

        windowed = [window_of(spill, spill_ids)]
        for g in range(total):
            here = rows_of(g)
            centers = [spans(per_row, s, c, here) for c in range(3)]
            near = lateral(s, g, (0,), ends)
            inners = spans(per_row, s, 3, here)
            force = spans(per_row, f, 0, edge, here)
            values = [
                relax(0, [center[j] for center in centers], near[j] + inners[j], force[j], outer)
                for j in range(per_row)
            ]
            windowed.append(window_of(values, spans(per_row, cyc, here)))
        for i, (window, start) in enumerate(windowed):
            windows[0, i] = window
            windows[1, i] = start.astype(jnp.float32)

        for copy in table:
            copy.wait()
        half = jnp.where(bottom, groups, 0)
        low_part = jnp.right_shift(jnp.maximum(first - reach, 0), 7)
        high_part = jnp.minimum(jnp.right_shift(last + reach, 7), chunks - 1)

        def batch(b, result):
            means = []
            parts = []
            for i in range(BATCH):
                q = low_part + b * BATCH + i
                part = jnp.minimum(q, chunks - 1)
                parts.append(part)
                acc = zero
                for w in range(total + 1):
                    at = q * LANES + lane8 - windows[1, w].astype(jnp.int32)
                    got = lane_gather(windows[0, w], jnp.bitwise_and(at, LANES - 1))
                    acc = acc + jnp.where(jnp.right_shift(at, 7) == 0, got, 0.0)
                mean = jnp.sum(acc, axis=0, keepdims=True) / num[pl.ds(part, 1), :].astype(jnp.float32)
                mean = jnp.where(q < chunks, mean, 0.0)
                means.append(jnp.broadcast_to(mean, (SUB, LANES)))
            for g in range(groups):
                acc = tab[parts[0], SUB * g:SUB * g + SUB, :] * means[0]
                for i in range(1, BATCH):
                    acc = acc + tab[parts[i], SUB * g:SUB * g + SUB, :] * means[i]
                column = jnp.broadcast_to(jnp.sum(acc, axis=1, keepdims=True), (SUB, LANES))
                result = jnp.where(lane8 == g + half, result + column, result)
            return result

        pay[0:SUB, 0:LANES] = lax.fori_loop(0, (high_part - low_part) // BATCH + 1, batch, zero)

    @pl.when(jnp.logical_not(at_end))
    def _():
        for copy in table:
            copy.wait()

    tall = 3 * layers

    def pack(ref, base, near, far):
        for c in range(3):
            for r in range(layers):
                at = base + c * layers + r
                ref[at:at + 1, :] = u[c, r, near:near + 1, :]
                ref[at + tall:at + tall + 1, :] = u[c, r, far:far + 1, :]
                ref[at + 2 * tall:at + 2 * tall + 1, :] = f[c, r, near:near + 1, :]

    @pl.when(lax.rem(lat, 2) == 0)
    def _():
        pack(pay, SUB, rows - 1, rows - 2)
        pack(held, 0, 0, 1)

    @pl.when(lax.rem(lat, 2) == 1)
    def _():
        pack(pay, SUB, 0, 1)
        pack(held, 0, rows - 1, rows - 2)

    for copy in bulk:
        copy.wait()


def sweep_kernel(
    u, f, lo, hi, got1, got2, got3, got4, every,
    out,
    s, rim, edges, cf,
):
    layers, rows, width = u.shape[1:]
    per_row = width // LANES
    total = rows // SUB
    tall = 3 * layers
    lat, lats = lax.axis_index("lat"), lax.axis_size("lat")
    rad, rads = lax.axis_index("rad"), lax.axis_size("rad")
    lat_odd, rad_odd = lax.rem(lat, 2) == 1, lax.rem(rad, 2) == 1
    low_in, high_in = lat > 0, lat < lats - 1
    sub8 = iota((SUB, LANES), 0)

    def side_rows(base, j):
        at = (slice(SUB + base, SUB + base + layers), chunk(j))
        one, two = got1[at], got2[at]
        low = jnp.where(low_in, jnp.where(lat_odd, one, two), 0.0)
        high = jnp.where(high_in, jnp.where(lat_odd, two, one), 0.0)
        return jnp.concatenate([low, high], axis=0)

    below = lambda at: jnp.where(rad > 0, jnp.where(rad_odd, got3[at], got4[at]), 0.0)
    above = lambda at: jnp.where(rad < rads - 1, jnp.where(rad_odd, got4[at], got3[at]), 0.0)
    cf[0] = below(slice(SUB, SUB + COEFS))
    cf[layers + 1] = above(slice(SUB, SUB + COEFS))
    for r in range(layers):
        cf[1 + r] = every[r]
    corner_low = [below(slice(SUB + COEFS + SUB * j, SUB + COEFS + SUB * j + SUB)) for j in range(per_row)]
    corner_high = [above(slice(SUB + COEFS + SUB * j, SUB + COEFS + SUB * j + SUB)) for j in range(per_row)]

    def coefficients(layer):
        return [jnp.broadcast_to(cf[layer, j:j + 1, :], (SUB, LANES)) for j in range(12)]

    near_rows = [[side_rows(c * layers, j) for j in range(per_row)] for c in range(3)]
    mixed = []
    for i in range(12):
        row = jnp.zeros((SUB, LANES), jnp.float32)
        for r in range(layers):
            here = jnp.broadcast_to(cf[1 + r, i:i + 1, :], (SUB, LANES))
            row = jnp.where(jnp.logical_or(sub8 == r, sub8 == layers + r), here, row)
        mixed.append(row)
    keep = jnp.where(sub8 < layers, jnp.where(low_in, 1.0, 0.0), jnp.where(high_in, 1.0, 0.0))
    for c in range(3):
        aside = roll_columns(near_rows[c])
        for j in range(per_row):
            value = near_rows[c][j]
            first_low, first_high = corner_low[j][c:c + 1, :], corner_low[j][3 + c:4 + c, :]
            last_low, last_high = corner_high[j][c:c + 1, :], corner_high[j][3 + c:4 + c, :]
            down = pltpu.roll(value, 1, 0)
            down = jnp.where(sub8 == 0, jnp.broadcast_to(first_low, down.shape), down)
            down = jnp.where(sub8 == layers, jnp.broadcast_to(first_high, down.shape), down)
            rise = pltpu.roll(value, SUB - 1, 0)
            rise = jnp.where(sub8 == layers - 1, jnp.broadcast_to(last_low, rise.shape), rise)
            rise = jnp.where(sub8 == SUB - 1, jnp.broadcast_to(last_high, rise.shape), rise)
            within = jnp.zeros((SUB, LANES), jnp.float32)
            for r in range(layers):
                head = jnp.broadcast_to(u[c, r, 0:1, chunk(j)], within.shape)
                tail = jnp.broadcast_to(u[c, r, rows - 1:rows, chunk(j)], within.shape)
                within = jnp.where(sub8 == r, head, jnp.where(sub8 == layers + r, tail, within))
            near = aside[j] + down + rise + within + side_rows(tall + c * layers, j)
            force = side_rows(2 * tall + c * layers, j)
            value = relax(c, [near_rows[d][j] for d in range(3)], near, force, mixed)
            value = value * keep
            for i in range(2 * layers):
                rim[i, c, :, chunk(j)] = jnp.broadcast_to(value[i:i + 1, :], (SUB, LANES))
                edges[i, c, :, chunk(j)] = jnp.broadcast_to(near_rows[c][j][i:i + 1, :], (SUB, LANES))

    def update(layer, g, center, lower, upper, force, ends):
        rows_here = slice(SUB * g, SUB * g + SUB)
        coef = coefficients(layer)
        values = [[center(c, rows_here, j) for j in range(per_row)] for c in range(3)]
        result = []
        for c in range(3):
            aside = roll_columns(values[c])
            line = []
            for j in range(per_row):
                before = center(c, slice(SUB * g - 1, SUB * g), j) if g > 0 else ends(c, 0, j)
                after = center(c, slice(SUB * g + SUB, SUB * g + SUB + 1), j) if g < total - 1 else ends(c, 1, j)
                near = roll_rows(values[c][j], before, after) + aside[j]
                near = near + (lower(c, rows_here, j) + upper(c, rows_here, j))
                line.append(relax(c, [values[d][j] for d in range(3)], near, force(c, rows_here, j), coef))
            result.append(line)
        return rows_here, result

    def reader(ref, *index):
        def read(c, at, j):
            full = tuple(c if i is None else i for i in index)
            return ref[full + (at, chunk(j))]
        return read

    def first(layer, center, lower, upper, force, ends):
        for g in range(total):
            at, result = update(layer, g, center, lower, upper, force, ends)
            for c in range(3):
                for j in range(per_row):
                    s[c, layer, at, chunk(j)] = result[c][j]

    def rows_beside(layer):
        return lambda c, side, j: edges[layer + layers * side, c, :, chunk(j)]

    def corner_rows(which):
        return lambda c, side, j: (corner_low, corner_high)[which][j][3 * side + c:3 * side + c + 1, :]

    top = layers - 1
    first(0, reader(lo, 0, None), reader(lo, 1, None), reader(u, None, 0), reader(lo, 2, None), corner_rows(0))
    first(1, reader(u, None, 0), reader(lo, 0, None), reader(u, None, 1), reader(f, None, 0), rows_beside(0))

    def middle(r, carry):
        first(r + 1, reader(u, None, r), reader(u, None, r - 1), reader(u, None, r + 1), reader(f, None, r), rows_beside(r))
        return carry

    lax.fori_loop(1, top, middle, 0)
    first(layers, reader(u, None, top), reader(u, None, top - 1), reader(hi, 0, None), reader(f, None, top), rows_beside(top))
    first(layers + 1, reader(hi, 0, None), reader(u, None, top), reader(hi, 1, None), reader(hi, 2, None), corner_rows(1))

    def last(r, carry):
        ends = lambda c, side, j: rim[r + layers * side, c, :, chunk(j)]
        for g in range(total):
            at, result = update(
                r + 1, g, reader(s, None, r + 1), reader(s, None, r), reader(s, None, r + 2), reader(f, None, r), ends
            )
            for c in range(3):
                for j in range(per_row):
                    out[c, r, at, chunk(j)] = result[c][j]
        return carry

    lax.fori_loop(0, layers, last, 0)


def synthesis_kernel(scale, coef, gain_a, gain_b, ids, tab, out, factors):
    rows, width = ids.shape
    chunks = tab.shape[0]
    groups = tab.shape[1] // SUB
    per_row = width // LANES
    lane8 = iota((SUB, LANES), 1)
    here = coef[...]
    other = pltpu.roll(here, groups, 1)
    left = lane8 < groups
    surface = jnp.where(left, here, other)
    core = jnp.where(left, other, here)
    modes = (gain_a[...] * surface + gain_b[...] * core) * scale
    zero = jnp.zeros((SUB, LANES), jnp.float32)
    for i in range(2 * groups):
        factors[i] = jnp.broadcast_to(modes[:, i:i + 1], (SUB, LANES))
    low_part = jnp.right_shift(jnp.min(ids[0:1, 0:LANES]), 7)
    high_part = jnp.right_shift(jnp.max(ids[rows - 1:rows, width - LANES:width]), 7)

    def batch(b, carry):
        parts = [low_part + b * BATCH + i for i in range(BATCH)]
        blocks = [jnp.minimum(part, chunks - 1) for part in parts]
        sums = [[zero] * BATCH for _ in range(2)]
        for g in range(groups):
            for i in range(BATCH):
                block = tab[blocks[i], SUB * g:SUB * g + SUB, :]
                for k in range(2):
                    sums[k][i] = sums[k][i] + factors[k * groups + g] * block
        for k in range(2):
            for i in range(BATCH):
                sums[k][i] = jnp.broadcast_to(jnp.sum(sums[k][i], axis=0, keepdims=True), (SUB, LANES))
        for a in range(rows // SUB):
            for j in range(per_row):
                spot = (slice(SUB * a, SUB * a + SUB), chunk(j))
                cycle = ids[spot]
                place, part = jnp.bitwise_and(cycle, LANES - 1), jnp.right_shift(cycle, 7)
                values = [jnp.where(b == 0, 0.0, out[(k,) + spot]) for k in range(2)]
                for i in range(BATCH):
                    chosen = part == parts[i]
                    for k in range(2):
                        values[k] = jnp.where(chosen, lane_gather(sums[k][i], place), values[k])
                for k in range(2):
                    out[(k,) + spot] = values[k]
        return carry

    lax.fori_loop(0, (high_part - low_part) // BATCH + 1, batch, 0)


def even_pairs(count):
    return [(i, i ^ 1) for i in range(count)]


def odd_pairs(count):
    pairs = []
    for i in range(1, count, 2):
        j = (i + 1) % count
        pairs += [(i, j), (j, i)]
    return pairs


def local(displacement, forcing, layer_id, stiffness, coupling, cycle_id, cycle_count, gravity):
    _, layers, rows, width = displacement.shape
    cycles, degrees = cycle_count.shape[0], gravity.shape[2]
    chunks, groups = cycles // LANES, degrees // SUB
    if 2 * groups != LANES or 2 * layers != SUB:
        raise ValueError("unsupported sizes")
    lat, lats = lax.axis_index("lat"), lax.axis_size("lat")
    rad, rads = lax.axis_index("rad"), lax.axis_size("rad")
    lat_odd, rad_odd = lat % 2 == 1, rad % 2 == 1
    f32 = jnp.float32
    table = jnp.asarray(basis_table(degrees, cycles))
    per_row = width // LANES
    tall = 3 * layers
    edge_rows = -(-3 * tall // SUB) * SUB
    face = jax.ShapeDtypeStruct((3, 3, rows, width), f32)
    grid = (3, layers, rows, width)

    up, dn, pay, held, mine1, mine2, every = pl.pallas_call(
        analysis_kernel,
        out_shape=(
            face, face,
            jax.ShapeDtypeStruct((SUB + edge_rows, width), f32),
            jax.ShapeDtypeStruct((edge_rows, width), f32),
            jax.ShapeDtypeStruct((COEFS, LANES), f32),
            jax.ShapeDtypeStruct((COEFS, LANES), f32),
            jax.ShapeDtypeStruct((layers, COEFS, LANES), f32),
        ),
        in_specs=[HBM] * 8,
        out_specs=(ANY, ANY) + (VMEM,) * 5,
        scratch_shapes=[
            pltpu.VMEM(grid, f32),
            pltpu.VMEM(grid, f32),
            pltpu.VMEM(cycle_id.shape, jnp.int32),
            pltpu.VMEM((chunks, LANES), jnp.int32),
            pltpu.VMEM((chunks, degrees, LANES), f32),
            pltpu.VMEM((2, COEFS, LANES), f32),
            pltpu.VMEM((4, rows, width), f32),
            pltpu.VMEM((2, rows // SUB + 1, SUB, LANES), f32),
            pltpu.SMEM(layer_id.shape, jnp.int32),
            pltpu.SMEM(stiffness.shape, f32),
            pltpu.SMEM(coupling.shape[1:] + coupling.shape[:1], f32),
            pltpu.SMEM((SUB, LANES), jnp.int32),
            pltpu.SMEM((SUB, LANES), jnp.int32),
            pltpu.SemaphoreType.DMA((9,)),
            pltpu.SemaphoreType.DMA((6,)),
            pltpu.SemaphoreType.DMA((chunks,)),
        ],
        compiler_params=pltpu.CompilerParams(vmem_limit_bytes=VMEM_LIMIT),
        name="analysis",
    )(
        *(
            pltpu.with_memory_space_constraint(value, pltpu.HBM)
            for value in (
                displacement, forcing, layer_id, stiffness, jnp.transpose(coupling, (1, 2, 0)), cycle_id,
                cycle_count.reshape(chunks, LANES), table,
            )
        )
    )

    low_far = lax.ppermute(up, "rad", [(i, i + 1) for i in range(rads - 1)])
    high_far = lax.ppermute(dn, "rad", [(i + 1, i) for i in range(rads - 1)])

    butterfly = lats == 4 and rads == 8
    coef = pay[:SUB, :LANES]
    got1 = lax.ppermute(pay, "lat", even_pairs(lats))
    if butterfly:
        coef = coef + got1[:SUB, :LANES]
    else:
        coef = lax.psum(coef, ("lat", "rad"))
    strip = jnp.concatenate([coef, jnp.zeros((SUB, width - LANES), f32)], axis=1)
    got2 = lax.ppermute(jnp.concatenate([strip, held], axis=0), "lat", odd_pairs(lats))
    if butterfly:
        coef = coef + got2[:SUB, :LANES]
    low = jnp.where(lat > 0, jnp.where(lat_odd, got1[SUB:SUB + tall], got2[SUB:SUB + tall]), 0.0)
    high = jnp.where(lat < lats - 1, jnp.where(lat_odd, got2[SUB:SUB + tall], got1[SUB:SUB + tall]), 0.0)

    def corners(layer):
        picks = [side[c * layers + layer][None] for side in (low, high) for c in range(3)]
        block = jnp.concatenate(picks + [jnp.zeros((SUB - 6, width), f32)], axis=0)
        return jnp.concatenate(jnp.split(block, per_row, axis=1), axis=0)

    corner_low, corner_high = corners(0), corners(layers - 1)
    send1 = jnp.where(rad_odd, corner_low, corner_high)
    send2 = jnp.where(rad_odd, corner_high, corner_low)
    got3 = lax.ppermute(jnp.concatenate([coef, mine1, send1], axis=0), "rad", even_pairs(rads))
    if butterfly:
        coef = coef + got3[:SUB]
    far = jnp.concatenate([coef, mine2, send2], axis=0)
    far, low_far, high_far = lax.optimization_barrier((far, low_far, high_far))
    got4 = lax.ppermute(far, "rad", odd_pairs(rads))
    if butterfly:
        coef = coef + got4[:SUB]
        coef = coef + lax.ppermute(coef, "rad", [(0, 3), (7, 4), (2, 5), (5, 2), (1, 6), (6, 1)])

    smoothed = pl.pallas_call(
        sweep_kernel,
        out_shape=jax.ShapeDtypeStruct(displacement.shape, f32),
        in_specs=[VMEM] * 9,
        out_specs=VMEM,
        scratch_shapes=[
            pltpu.VMEM((3, layers + 2, rows, width), f32),
            pltpu.VMEM((2 * layers, 3, SUB, width), f32),
            pltpu.VMEM((2 * layers, 3, SUB, width), f32),
            pltpu.VMEM((layers + 2, COEFS, LANES), f32),
        ],
        compiler_params=pltpu.CompilerParams(vmem_limit_bytes=VMEM_LIMIT),
        name="sweeps",
    )(displacement, forcing, low_far, high_far, got1, got2, got3, got4, every)
    coef, smoothed = lax.optimization_barrier((coef, smoothed))

    shaped = gravity.reshape(2, 2, SUB, groups)
    gain_a = jnp.concatenate([shaped[0, 0], shaped[1, 0]], axis=1)
    gain_b = jnp.concatenate([shaped[0, 1], shaped[1, 1]], axis=1)
    potential = pl.pallas_call(
        functools.partial(synthesis_kernel, 2.0 / cycles),
        out_shape=jax.ShapeDtypeStruct((2, rows, width), f32),
        in_specs=[VMEM] * 5,
        out_specs=VMEM,
        scratch_shapes=[pltpu.VMEM((2 * groups, SUB, LANES), f32)],
        compiler_params=pltpu.CompilerParams(vmem_limit_bytes=VMEM_LIMIT),
        name="synthesis",
    )(coef, gain_a, gain_b, cycle_id, table)
    return smoothed, potential


def solution(mesh):
    in_specs = (
        P(None, "rad", "lat", None),
        P(None, "rad", "lat", None),
        P("rad"),
        P(),
        P(),
        P("lat", None),
        P(),
        P(),
    )
    out_specs = (P(None, "rad", "lat", None), P(None, "lat", None))
    return jax.shard_map(local, mesh=mesh, in_specs=in_specs, out_specs=out_specs, check_vma=False)
```

```python
import functools
import math

import jax
import jax.numpy as jnp
import numpy as np
from jax import lax
from jax.experimental import pallas as pl
from jax.experimental.pallas import tpu as pltpu
from jax.sharding import PartitionSpec as P

SWEEPS = 2
OMEGA = 0.8
LEAST_COUNT = 32
LANES = 128
SUB = 8
PAD = 8
COEFS = 16
BATCH = 5
VMEM_LIMIT = 16 * 1024 * 1024

VMEM = pl.BlockSpec(memory_space=pltpu.VMEM)
SMEM = pl.BlockSpec(memory_space=pltpu.SMEM)
HBM = pl.BlockSpec(memory_space=pltpu.HBM)
ANY = pl.BlockSpec(memory_space=pl.ANY)


def basis_table(degrees, cycles):
    groups = degrees // SUB
    degree = np.arange(degrees, dtype=np.int64)[:, None]
    cycle = np.arange(cycles, dtype=np.int64)[None, :]
    phase = degree * (2 * cycle + 1) % (4 * cycles)
    table = np.cos(np.pi * phase / (2.0 * cycles)).astype(np.float32)
    table = table.reshape(SUB, groups, cycles // LANES, LANES).transpose(2, 1, 0, 3)
    return np.ascontiguousarray(table.reshape(cycles // LANES, degrees, LANES))


def iota(shape, dim):
    return lax.broadcasted_iota(jnp.int32, shape, dim)


def lane_gather(values, index):
    return jnp.take_along_axis(values, index, axis=1, mode="promise_in_bounds")


def layer_scalars(layer, lid, stiff, coup):
    material = lid[layer]
    mu = stiff[material]
    return mu, [[coup[c, d, material] for d in range(3)] for c in range(3)]


def coefficient_rows(mu, k, width=LANES):
    row = iota((COEFS, width), 0)
    top = jnp.zeros((COEFS, width), jnp.float32)
    below = jnp.ones((COEFS, width), jnp.float32)
    for c in range(3):
        diag = 6.0 * mu + k[c][c]
        others = [d for d in range(3) if d != c]
        entries = [(c, 1.0), (3 + c, mu), (6 + 2 * c, k[c][others[0]]), (7 + 2 * c, k[c][others[1]])]
        for at, value in entries:
            top = jnp.where(row == at, OMEGA * value, top)
            below = jnp.where(row == at, diag, below)
    return top / below


def roll_rows(value, before, after):
    sub = iota(value.shape, 0)
    up = jnp.where(sub == 0, jnp.broadcast_to(before, value.shape), pltpu.roll(value, 1, 0))
    down = jnp.where(sub == SUB - 1, jnp.broadcast_to(after, value.shape), pltpu.roll(value, SUB - 1, 0))
    return up + down


def roll_columns(values):
    lane = iota(values[0].shape, 1)
    right = [pltpu.roll(value, 1, 1) for value in values]
    left = [pltpu.roll(value, LANES - 1, 1) for value in values]
    last = len(values) - 1
    return [
        jnp.where(lane == 0, right[j - 1] if j > 0 else 0.0, right[j])
        + jnp.where(lane == LANES - 1, left[j + 1] if j < last else 0.0, left[j])
        for j in range(len(values))
    ]


def relax(c, centers, neighbours, force, rows):
    d0, d1 = [d for d in range(3) if d != c]
    value = rows[c] * force + rows[3 + c] * neighbours
    value = value - (rows[6 + 2 * c] * centers[d0] + rows[7 + 2 * c] * centers[d1])
    return value + (1.0 - OMEGA) * centers[c]


def chunk(j):
    return pl.ds(LANES * j, LANES)


def spans(per_row, ref, *index):
    return [ref[index + (chunk(j),)] for j in range(per_row)]


def lane_scan(values, steps):
    lane = iota(values.shape, 1)
    step = 1
    while step < steps:
        values = values + jnp.where(lane >= step, pltpu.roll(values, step, 1), 0)
        step *= 2
    return values


def first_sweep_kernel(
    disp, forc, lid, stiff, coup,
    u, f, s, kept, up, dn, every,
    lids, stiffs, coups, u_sem, f_sem, small_sem, face_sem, kept_sem,
):
    layers, rows, width = disp.shape[1:]
    per_row = width // LANES
    total = rows // SUB
    small = [
        pltpu.make_async_copy(lid, lids, small_sem.at[0]),
        pltpu.make_async_copy(stiff, stiffs, small_sem.at[1]),
        pltpu.make_async_copy(coup, coups, small_sem.at[2]),
    ]
    loads_u = [pltpu.make_async_copy(disp.at[:, r], u.at[:, r], u_sem.at[r]) for r in range(layers)]
    loads_f = [pltpu.make_async_copy(forc.at[:, r], f.at[:, r], f_sem.at[r]) for r in range(layers)]
    for copy in small:
        copy.start()
    for r in range(layers):
        loads_u[r].start()
        loads_f[r].start()
    for copy in small:
        copy.wait()
    for r in range(layers):
        every[r] = coefficient_rows(*layer_scalars(r, lids, stiffs, coups))
    none = jnp.zeros((1, LANES), jnp.float32)

    def sweep(layer, lower, upper):
        coef = [jnp.broadcast_to(every[layer, j:j + 1, :], (SUB, LANES)) for j in range(12)]
        for g in range(total):
            here = slice(SUB * g, SUB * g + SUB)
            values = [spans(per_row, u, c, layer, here) for c in range(3)]
            for c in range(3):
                aside = roll_columns(values[c])
                for j in range(per_row):
                    at = (c, layer)
                    before = u[at + (slice(SUB * g - 1, SUB * g), chunk(j))] if g > 0 else none
                    after = u[at + (slice(SUB * g + SUB, SUB * g + SUB + 1), chunk(j))] if g < total - 1 else none
                    near = roll_rows(values[c][j], before, after) + aside[j]
                    if lower is not None:
                        near = near + u[c, lower, here, chunk(j)]
                    if upper is not None:
                        near = near + u[c, upper, here, chunk(j)]
                    value = relax(c, [values[d][j] for d in range(3)], near, f[c, layer, here, chunk(j)], coef)
                    s[c, layer, here, chunk(j)] = value

    loads_u[0].wait()
    loads_f[0].wait()
    loads_u[1].wait()
    faces = [pltpu.make_async_copy(u.at[:, 0], dn.at[0], face_sem.at[0])]
    faces[0].start()
    sweep(0, None, 1)
    faces.append(pltpu.make_async_copy(s.at[:, 0], dn.at[1], face_sem.at[1]))
    faces[1].start()
    keeps = [pltpu.make_async_copy(s.at[:, r], kept.at[:, r], kept_sem.at[r]) for r in range(layers)]
    keeps[0].start()
    top = layers - 1
    for r in range(2, layers):
        loads_u[r].wait()
    for r in range(1, layers):
        loads_f[r].wait()
    faces.append(pltpu.make_async_copy(u.at[:, top], up.at[0], face_sem.at[2]))
    faces[2].start()
    sweep(top, top - 1, None)
    faces.append(pltpu.make_async_copy(s.at[:, top], up.at[1], face_sem.at[3]))
    faces[3].start()
    keeps[top].start()

    def middle(r, carry):
        sweep(r, r - 1, r + 1)
        pltpu.make_async_copy(s.at[:, r], kept.at[:, r], kept_sem.at[r]).start()
        return carry

    lax.fori_loop(1, top, middle, 0)
    for copy in faces + keeps:
        copy.wait()


def analysis_kernel(
    u, f, s, every, ids, cnt, tbl,
    pay, held, send1, send2,
    cyc, num, tab, mat, windows, first_ids, last_ids, near_sem, tab_sem,
):
    layers, rows, width = u.shape[1:]
    chunks = cnt.shape[0]
    groups = tbl.shape[1] // SUB
    per_row = width // LANES
    lat, lats = lax.axis_index("lat"), lax.axis_size("lat")
    rad, rads = lax.axis_index("rad"), lax.axis_size("rad")
    bottom = rad == 0
    at_end = jnp.logical_or(bottom, rad == rads - 1)
    edge = jnp.where(bottom, 0, layers - 1)
    inner = jnp.where(bottom, 1, layers - 2)
    total = rows // SUB

    small = [
        pltpu.make_async_copy(ids.at[pl.ds(0, SUB), pl.ds(0, LANES)], first_ids, near_sem.at[0]),
        pltpu.make_async_copy(
            ids.at[pl.ds(rows - SUB, SUB), pl.ds(width - LANES, LANES)], last_ids, near_sem.at[1]
        ),
        pltpu.make_async_copy(cnt, num, near_sem.at[2]),
        pltpu.make_async_copy(ids, cyc, near_sem.at[3]),
    ]
    table = [pltpu.make_async_copy(tbl.at[q], tab.at[q], tab_sem.at[q]) for q in range(chunks)]
    for copy in small + table:
        copy.start()

    odd = lax.rem(rad, 2) == 1
    send1[...] = every[jnp.where(odd, 0, layers - 1)]
    send2[...] = every[jnp.where(odd, layers - 1, 0)]

    sub8, lane8 = iota((SUB, LANES), 0), iota((SUB, LANES), 1)
    before = sub8 < 2
    zero = jnp.zeros((SUB, LANES), jnp.float32)
    reach = 2 * width // LEAST_COUNT + 2
    for copy in small:
        copy.wait()
    first, last = first_ids[0, 0], last_ids[SUB - 1, LANES - 1]
    pay[0:SUB, :] = jnp.zeros((SUB, width), jnp.float32)

    @pl.when(at_end)
    def _():
        own_first = jnp.zeros((SUB, LANES), jnp.int32)
        own_last = own_first
        for j in range(per_row):
            own_first = own_first + jnp.where(cyc[0:SUB, LANES * j:LANES * j + LANES] == first, 1, 0)
            own_last = own_last + jnp.where(cyc[rows - SUB:rows, LANES * j:LANES * j + LANES] == last, 1, 0)

        def total_of(count):
            count = jnp.sum(count.astype(jnp.float32), axis=1, keepdims=True)
            return jnp.broadcast_to(jnp.sum(count, axis=0, keepdims=True), (SUB, LANES)).astype(jnp.int32)

        held_here = jnp.where(before, total_of(own_first), total_of(own_last))
        index = jnp.where(before, first - lane8, last + lane8)
        place, part = jnp.bitwise_and(index, LANES - 1), jnp.right_shift(index, 7)
        lengths = jnp.full((SUB, LANES), 2 ** 20, jnp.int32)
        part_first, part_last = jnp.right_shift(first, 7), jnp.right_shift(last, 7)
        for q in (part_first - 1, part_first, part_last, part_last + 1):
            row = num[pl.ds(jnp.clip(q, 0, chunks - 1), 1), :]
            known = jnp.logical_and(part == q, jnp.logical_and(part >= 0, part < chunks))
            lengths = jnp.where(known, lane_gather(jnp.broadcast_to(row, (SUB, LANES)), place), lengths)
        lengths = lengths - jnp.where(lane8 == 0, held_here, 0)
        limits = lane_scan(lengths, reach)
        caps = [jnp.broadcast_to(limits[:, i:i + 1], (SUB, LANES)) for i in range(reach)]
        spill_ids = []
        for j in range(per_row):
            column = LANES * j + lane8
            away = jnp.where(before, (width - 1 - column) + jnp.where(sub8 == 0, width, 0),
                             column + jnp.where(sub8 == 3, width, 0))
            passed = jnp.zeros((SUB, LANES), jnp.int32)
            for i in range(reach):
                passed = passed + jnp.where(away >= caps[i], 1, 0)
            spill_ids.append(jnp.where(sub8 < 4, jnp.where(before, first - passed, last + passed), 0))

        mat[0] = every[edge]
        mat[1] = every[inner]
        outer = [jnp.broadcast_to(mat[0, j:j + 1, :], (SUB, LANES)) for j in range(12)]
        below = [jnp.broadcast_to(mat[1, j:j + 1, :], (SUB, LANES)) for j in range(12)]

        def rows_of(g):
            return slice(SUB * g, SUB * g + SUB)

        def lateral(ref, g, index, ends):
            values = spans(per_row, ref, *index, rows_of(g))
            aside = roll_columns(values)
            out = []
            for j in range(per_row):
                above = ref[index + (slice(SUB * g - 1, SUB * g), chunk(j))] if g > 0 else ends[0][j]
                under = ref[index + (slice(SUB * g + SUB, SUB * g + SUB + 1), chunk(j))] if g < total - 1 else ends[1][j]
                out.append(roll_rows(values[j], above, under) + aside[j])
            return out

        low_in = jnp.where(lat > 0, 1.0, 0.0)
        high_in = jnp.where(lat < lats - 1, 1.0, 0.0)
        weight = jnp.where(sub8 == 1, low_in, jnp.where(sub8 == 2, high_in, 0.0))

        def ends_of(ref, index, j):
            low = jnp.broadcast_to(ref[index + (slice(0, 1), chunk(j))], (SUB, LANES))
            high = jnp.broadcast_to(ref[index + (slice(rows - 1, rows), chunk(j))], (SUB, LANES))
            return jnp.where(sub8 == 1, low, jnp.where(sub8 == 2, high, 0.0))

        over = [[outer[3 + c] * ends_of(u, (c, edge), j) * weight for j in range(per_row)] for c in range(3)]
        over_inner = [below[3] * ends_of(u, (0, inner), j) * weight for j in range(per_row)]
        aside = roll_columns(over[0])
        spill = []
        for j in range(per_row):
            shifted = jnp.where(sub8 == 0, pltpu.roll(over[0][j], SUB - 1, 0),
                                jnp.where(sub8 == 3, pltpu.roll(over[0][j], 1, 0), 0.0))
            near = over_inner[j] + aside[j] + shifted + ends_of(s, (0, edge), j)
            value = relax(0, [over[c][j] for c in range(3)], near, zero, outer)
            spill.append(value * jnp.where(before, low_in, high_in))
        ends = [[over[0][j][1:2, :] for j in range(per_row)], [over[0][j][2:3, :] for j in range(per_row)]]

        met = (width - 2) // LEAST_COUNT + 2

        def window_of(values, cycles):
            start = jnp.broadcast_to(cycles[0][:, 0:1], (SUB, LANES))
            offsets = [cycle - start for cycle in cycles]
            window = zero
            for t in range(met):
                picked = [jnp.where(offset == t, value, 0.0) for offset, value in zip(offsets, values)]
                sum_t = jnp.sum(functools.reduce(jnp.add, picked), axis=1, keepdims=True)
                window = jnp.where(lane8 == t, jnp.broadcast_to(sum_t, (SUB, LANES)), window)
            return window, start

        windowed = [window_of(spill, spill_ids)]
        for g in range(total):
            here = rows_of(g)
            centers = [spans(per_row, s, c, edge, here) for c in range(3)]
            near = lateral(s, g, (0, edge), ends)
            inners = spans(per_row, s, 0, inner, here)
            force = spans(per_row, f, 0, edge, here)
            values = [
                relax(0, [center[j] for center in centers], near[j] + inners[j], force[j], outer)
                for j in range(per_row)
            ]
            windowed.append(window_of(values, spans(per_row, cyc, here)))
        for i, (window, start) in enumerate(windowed):
            windows[0, i] = window
            windows[1, i] = start.astype(jnp.float32)

        for copy in table:
            copy.wait()
        half = jnp.where(bottom, groups, 0)
        low_part = jnp.right_shift(jnp.maximum(first - reach, 0), 7)
        high_part = jnp.minimum(jnp.right_shift(last + reach, 7), chunks - 1)

        def batch(b, result):
            means = []
            parts = []
            for i in range(BATCH):
                q = low_part + b * BATCH + i
                part = jnp.minimum(q, chunks - 1)
                parts.append(part)
                acc = zero
                for w in range(total + 1):
                    at = q * LANES + lane8 - windows[1, w].astype(jnp.int32)
                    got = lane_gather(windows[0, w], jnp.bitwise_and(at, LANES - 1))
                    acc = acc + jnp.where(jnp.right_shift(at, 7) == 0, got, 0.0)
                mean = jnp.sum(acc, axis=0, keepdims=True) / num[pl.ds(part, 1), :].astype(jnp.float32)
                mean = jnp.where(q < chunks, mean, 0.0)
                means.append(jnp.broadcast_to(mean, (SUB, LANES)))
            for g in range(groups):
                acc = tab[parts[0], SUB * g:SUB * g + SUB, :] * means[0]
                for i in range(1, BATCH):
                    acc = acc + tab[parts[i], SUB * g:SUB * g + SUB, :] * means[i]
                column = jnp.broadcast_to(jnp.sum(acc, axis=1, keepdims=True), (SUB, LANES))
                result = jnp.where(lane8 == g + half, result + column, result)
            return result

        pay[0:SUB, 0:LANES] = lax.fori_loop(0, (high_part - low_part) // BATCH + 1, batch, zero)

    @pl.when(jnp.logical_not(at_end))
    def _():
        for copy in table:
            copy.wait()

    tall = 3 * layers

    def pack(ref, base, near, far):
        for c in range(3):
            for r in range(layers):
                at = base + c * layers + r
                ref[at:at + 1, :] = u[c, r, near:near + 1, :]
                ref[at + tall:at + tall + 1, :] = u[c, r, far:far + 1, :]
                ref[at + 2 * tall:at + 2 * tall + 1, :] = f[c, r, near:near + 1, :]

    @pl.when(lax.rem(lat, 2) == 0)
    def _():
        pack(pay, SUB, rows - 1, rows - 2)
        pack(held, 0, 0, 1)

    @pl.when(lax.rem(lat, 2) == 1)
    def _():
        pack(pay, SUB, 0, 1)
        pack(held, 0, rows - 1, rows - 2)


def sweep_kernel(
    disp, forc, first, lo, hi, got1, got2, got3, got4, every,
    out,
    s, f, face, fringe, rim, done, cf, in_sem, out_sem,
):
    layers, rows, width = disp.shape[1:]
    per_row = width // LANES
    total = rows // SUB
    tall = 3 * layers
    top = layers - 1
    loads = [
        pltpu.make_async_copy(disp.at[:, :, pl.ds(0, SUB)], fringe.at[0], in_sem.at[0]),
        pltpu.make_async_copy(disp.at[:, :, pl.ds(rows - SUB, SUB)], fringe.at[1], in_sem.at[1]),
        pltpu.make_async_copy(disp.at[:, 0], face.at[0], in_sem.at[2]),
        pltpu.make_async_copy(disp.at[:, top], face.at[1], in_sem.at[3]),
        pltpu.make_async_copy(first, s.at[:, pl.ds(1, layers)], in_sem.at[4]),
        pltpu.make_async_copy(forc, f, in_sem.at[5]),
    ]
    for copy in loads:
        copy.start()
    lat, lats = lax.axis_index("lat"), lax.axis_size("lat")
    rad, rads = lax.axis_index("rad"), lax.axis_size("rad")
    lat_odd, rad_odd = lax.rem(lat, 2) == 1, lax.rem(rad, 2) == 1
    low_in, high_in = lat > 0, lat < lats - 1
    sub8 = iota((SUB, LANES), 0)

    def side_rows(base, j):
        at = (slice(SUB + base, SUB + base + layers), chunk(j))
        one, two = got1[at], got2[at]
        low = jnp.where(low_in, jnp.where(lat_odd, one, two), 0.0)
        high = jnp.where(high_in, jnp.where(lat_odd, two, one), 0.0)
        return jnp.concatenate([low, high], axis=0)

    below = lambda at: jnp.where(rad > 0, jnp.where(rad_odd, got3[at], got4[at]), 0.0)
    above = lambda at: jnp.where(rad < rads - 1, jnp.where(rad_odd, got4[at], got3[at]), 0.0)
    cf[0] = below(slice(SUB, SUB + COEFS))
    cf[layers + 1] = above(slice(SUB, SUB + COEFS))
    for r in range(layers):
        cf[1 + r] = every[r]
    corner_low = [below(slice(SUB + COEFS + SUB * j, SUB + COEFS + SUB * j + SUB)) for j in range(per_row)]
    corner_high = [above(slice(SUB + COEFS + SUB * j, SUB + COEFS + SUB * j + SUB)) for j in range(per_row)]

    def coefficients(layer):
        return [jnp.broadcast_to(cf[layer, j:j + 1, :], (SUB, LANES)) for j in range(12)]

    near_rows = [[side_rows(c * layers, j) for j in range(per_row)] for c in range(3)]
    mixed = []
    for i in range(12):
        row = jnp.zeros((SUB, LANES), jnp.float32)
        for r in range(layers):
            here = jnp.broadcast_to(cf[1 + r, i:i + 1, :], (SUB, LANES))
            row = jnp.where(jnp.logical_or(sub8 == r, sub8 == layers + r), here, row)
        mixed.append(row)
    loads[0].wait()
    loads[1].wait()
    keep = jnp.where(sub8 < layers, jnp.where(low_in, 1.0, 0.0), jnp.where(high_in, 1.0, 0.0))
    for c in range(3):
        aside = roll_columns(near_rows[c])
        for j in range(per_row):
            value = near_rows[c][j]
            first_low, first_high = corner_low[j][c:c + 1, :], corner_low[j][3 + c:4 + c, :]
            last_low, last_high = corner_high[j][c:c + 1, :], corner_high[j][3 + c:4 + c, :]
            down = pltpu.roll(value, 1, 0)
            down = jnp.where(sub8 == 0, jnp.broadcast_to(first_low, down.shape), down)
            down = jnp.where(sub8 == layers, jnp.broadcast_to(first_high, down.shape), down)
            rise = pltpu.roll(value, SUB - 1, 0)
            rise = jnp.where(sub8 == layers - 1, jnp.broadcast_to(last_low, rise.shape), rise)
            rise = jnp.where(sub8 == SUB - 1, jnp.broadcast_to(last_high, rise.shape), rise)
            within = jnp.zeros((SUB, LANES), jnp.float32)
            for r in range(layers):
                head = jnp.broadcast_to(fringe[0, c, r, 0:1, chunk(j)], within.shape)
                tail = jnp.broadcast_to(fringe[1, c, r, SUB - 1:SUB, chunk(j)], within.shape)
                within = jnp.where(sub8 == r, head, jnp.where(sub8 == layers + r, tail, within))
            near = aside[j] + down + rise + within + side_rows(tall + c * layers, j)
            force = side_rows(2 * tall + c * layers, j)
            value = relax(c, [near_rows[d][j] for d in range(3)], near, force, mixed) * keep
            for i in range(2 * layers):
                rim[i, c, :, chunk(j)] = jnp.broadcast_to(value[i:i + 1, :], (SUB, LANES))

    def beyond(layer, side, c, j):
        if layer == 0:
            return corner_low[j][3 * side + c:3 * side + c + 1, :]
        if layer == layers + 1:
            return corner_high[j][3 * side + c:3 * side + c + 1, :]
        at = layers * side + layer - 1
        return near_rows[c][j][at:at + 1, :]

    for copy in loads[2:5]:
        copy.wait()
    for layer in range(layers + 2):
        for c in range(3):
            gain = jnp.broadcast_to(cf[layer, 3 + c:4 + c, :], (SUB, LANES))
            for j in range(per_row):
                for g in range(total):
                    at = (slice(SUB * g, SUB * g + SUB), chunk(j))
                    value = None
                    if layer == 0:
                        value = lo[(1, c) + at] + gain * face[(0, c) + at]
                    elif layer == layers + 1:
                        value = hi[(1, c) + at] + gain * face[(1, c) + at]
                    elif layer in (1, layers) or g in (0, total - 1):
                        value = s[(c, layer) + at]
                    if layer == 1:
                        value = value + gain * lo[(0, c) + at]
                    if layer == layers:
                        value = value + gain * hi[(0, c) + at]
                    if value is None:
                        continue
                    if g == 0:
                        row = jnp.broadcast_to(beyond(layer, 0, c, j), value.shape)
                        value = value + jnp.where(sub8 == 0, gain * row, 0.0)
                    if g == total - 1:
                        row = jnp.broadcast_to(beyond(layer, 1, c, j), value.shape)
                        value = value + jnp.where(sub8 == SUB - 1, gain * row, 0.0)
                    s[(c, layer) + at] = value

    loads[5].wait()
    stores = [pltpu.make_async_copy(done.at[:, r], out.at[:, r], out_sem.at[r]) for r in range(layers)]
    for r in range(layers):
        layer = r + 1
        coef = coefficients(layer)
        for g in range(total):
            here = slice(SUB * g, SUB * g + SUB)
            values = [spans(per_row, s, c, layer, here) for c in range(3)]
            for c in range(3):
                aside = roll_columns(values[c])
                for j in range(per_row):
                    at = (c, layer)
                    if g > 0:
                        before = s[at + (slice(SUB * g - 1, SUB * g), chunk(j))]
                    else:
                        before = rim[r, c, :, chunk(j)]
                    if g < total - 1:
                        after = s[at + (slice(SUB * g + SUB, SUB * g + SUB + 1), chunk(j))]
                    else:
                        after = rim[layers + r, c, :, chunk(j)]
                    near = roll_rows(values[c][j], before, after) + aside[j]
                    near = near + (s[c, layer - 1, here, chunk(j)] + s[c, layer + 1, here, chunk(j)])
                    done[c, r, here, chunk(j)] = relax(
                        c, [values[d][j] for d in range(3)], near, f[c, r, here, chunk(j)], coef
                    )
        stores[r].start()
    for copy in stores:
        copy.wait()


def synthesis_kernel(scale, coef, gain_a, gain_b, ids, tab, out, factors):
    rows, width = ids.shape
    chunks = tab.shape[0]
    groups = tab.shape[1] // SUB
    per_row = width // LANES
    lane8 = iota((SUB, LANES), 1)
    here = coef[...]
    other = pltpu.roll(here, groups, 1)
    left = lane8 < groups
    surface = jnp.where(left, here, other)
    core = jnp.where(left, other, here)
    modes = (gain_a[...] * surface + gain_b[...] * core) * scale
    zero = jnp.zeros((SUB, LANES), jnp.float32)
    for i in range(2 * groups):
        factors[i] = jnp.broadcast_to(modes[:, i:i + 1], (SUB, LANES))
    low_part = jnp.right_shift(jnp.min(ids[0:1, 0:LANES]), 7)
    high_part = jnp.right_shift(jnp.max(ids[rows - 1:rows, width - LANES:width]), 7)

    def batch(b, carry):
        parts = [low_part + b * BATCH + i for i in range(BATCH)]
        blocks = [jnp.minimum(part, chunks - 1) for part in parts]
        sums = [[zero] * BATCH for _ in range(2)]
        for g in range(groups):
            for i in range(BATCH):
                block = tab[blocks[i], SUB * g:SUB * g + SUB, :]
                for k in range(2):
                    sums[k][i] = sums[k][i] + factors[k * groups + g] * block
        for k in range(2):
            for i in range(BATCH):
                sums[k][i] = jnp.broadcast_to(jnp.sum(sums[k][i], axis=0, keepdims=True), (SUB, LANES))
        for a in range(rows // SUB):
            for j in range(per_row):
                spot = (slice(SUB * a, SUB * a + SUB), chunk(j))
                cycle = ids[spot]
                place, part = jnp.bitwise_and(cycle, LANES - 1), jnp.right_shift(cycle, 7)
                values = [jnp.where(b == 0, 0.0, out[(k,) + spot]) for k in range(2)]
                for i in range(BATCH):
                    chosen = part == parts[i]
                    for k in range(2):
                        values[k] = jnp.where(chosen, lane_gather(sums[k][i], place), values[k])
                for k in range(2):
                    out[(k,) + spot] = values[k]
        return carry

    lax.fori_loop(0, (high_part - low_part) // BATCH + 1, batch, 0)


def even_pairs(count):
    return [(i, i ^ 1) for i in range(count)]


def odd_pairs(count):
    pairs = []
    for i in range(1, count, 2):
        j = (i + 1) % count
        pairs += [(i, j), (j, i)]
    return pairs


def local(displacement, forcing, layer_id, stiffness, coupling, cycle_id, cycle_count, gravity):
    _, layers, rows, width = displacement.shape
    cycles, degrees = cycle_count.shape[0], gravity.shape[2]
    chunks, groups = cycles // LANES, degrees // SUB
    if 2 * groups != LANES or 2 * layers != SUB:
        raise ValueError("unsupported sizes")
    lat, lats = lax.axis_index("lat"), lax.axis_size("lat")
    rad, rads = lax.axis_index("rad"), lax.axis_size("rad")
    lat_odd, rad_odd = lat % 2 == 1, rad % 2 == 1
    f32 = jnp.float32
    table = jnp.asarray(basis_table(degrees, cycles))
    per_row = width // LANES
    tall = 3 * layers
    edge_rows = -(-3 * tall // SUB) * SUB
    face = jax.ShapeDtypeStruct((2, 3, rows, width), f32)

    whole = jax.ShapeDtypeStruct(displacement.shape, f32)
    pinned = [
        pltpu.with_memory_space_constraint(value, pltpu.HBM)
        for value in (
            displacement, forcing, layer_id, stiffness, jnp.transpose(coupling, (1, 2, 0)), cycle_id,
            cycle_count.reshape(chunks, LANES), table,
        )
    ]
    u, f, swept, kept, up, dn, every = pl.pallas_call(
        first_sweep_kernel,
        out_shape=(whole, whole, whole, whole, face, face, jax.ShapeDtypeStruct((layers, COEFS, LANES), f32)),
        in_specs=[HBM] * 5,
        out_specs=(VMEM,) * 3 + (HBM,) + (VMEM,) * 3,
        scratch_shapes=[
            pltpu.SMEM(layer_id.shape, jnp.int32),
            pltpu.SMEM(stiffness.shape, f32),
            pltpu.SMEM(coupling.shape[1:] + coupling.shape[:1], f32),
            pltpu.SemaphoreType.DMA((layers,)),
            pltpu.SemaphoreType.DMA((layers,)),
            pltpu.SemaphoreType.DMA((3,)),
            pltpu.SemaphoreType.DMA((4,)),
            pltpu.SemaphoreType.DMA((layers,)),
        ],
        compiler_params=pltpu.CompilerParams(vmem_limit_bytes=VMEM_LIMIT),
        name="first_sweep",
    )(*pinned[:5])

    low_far = lax.ppermute(up, "rad", [(i, i + 1) for i in range(rads - 1)])
    high_far = lax.ppermute(dn, "rad", [(i + 1, i) for i in range(rads - 1)])

    pay, held, mine1, mine2 = pl.pallas_call(
        analysis_kernel,
        out_shape=(
            jax.ShapeDtypeStruct((SUB + edge_rows, width), f32),
            jax.ShapeDtypeStruct((edge_rows, width), f32),
            jax.ShapeDtypeStruct((COEFS, LANES), f32),
            jax.ShapeDtypeStruct((COEFS, LANES), f32),
        ),
        in_specs=[VMEM] * 4 + [HBM] * 3,
        out_specs=(VMEM,) * 4,
        scratch_shapes=[
            pltpu.VMEM(cycle_id.shape, jnp.int32),
            pltpu.VMEM((chunks, LANES), jnp.int32),
            pltpu.VMEM((chunks, degrees, LANES), f32),
            pltpu.VMEM((2, COEFS, LANES), f32),
            pltpu.VMEM((2, rows // SUB + 1, SUB, LANES), f32),
            pltpu.SMEM((SUB, LANES), jnp.int32),
            pltpu.SMEM((SUB, LANES), jnp.int32),
            pltpu.SemaphoreType.DMA((4,)),
            pltpu.SemaphoreType.DMA((chunks,)),
        ],
        compiler_params=pltpu.CompilerParams(vmem_limit_bytes=VMEM_LIMIT),
        name="analysis",
    )(u, f, swept, every, *pinned[5:])

    butterfly = lats == 4 and rads == 8
    coef = pay[:SUB, :LANES]
    got1 = lax.ppermute(pay, "lat", even_pairs(lats))
    if butterfly:
        coef = coef + got1[:SUB, :LANES]
    else:
        coef = lax.psum(coef, ("lat", "rad"))
    strip = jnp.concatenate([coef, jnp.zeros((SUB, width - LANES), f32)], axis=1)
    ahead = jnp.concatenate([strip, held], axis=0)
    ahead, low_far, high_far = lax.optimization_barrier((ahead, low_far, high_far))
    got2 = lax.ppermute(ahead, "lat", odd_pairs(lats))
    if butterfly:
        coef = coef + got2[:SUB, :LANES]
    low = jnp.where(lat > 0, jnp.where(lat_odd, got1[SUB:SUB + tall], got2[SUB:SUB + tall]), 0.0)
    high = jnp.where(lat < lats - 1, jnp.where(lat_odd, got2[SUB:SUB + tall], got1[SUB:SUB + tall]), 0.0)

    def corners(layer):
        picks = [side[c * layers + layer][None] for side in (low, high) for c in range(3)]
        block = jnp.concatenate(picks + [jnp.zeros((SUB - 6, width), f32)], axis=0)
        return jnp.concatenate(jnp.split(block, per_row, axis=1), axis=0)

    corner_low, corner_high = corners(0), corners(layers - 1)
    send1 = jnp.where(rad_odd, corner_low, corner_high)
    send2 = jnp.where(rad_odd, corner_high, corner_low)
    got3 = lax.ppermute(jnp.concatenate([coef, mine1, send1], axis=0), "rad", even_pairs(rads))
    if butterfly:
        coef = coef + got3[:SUB]
    got4 = lax.ppermute(jnp.concatenate([coef, mine2, send2], axis=0), "rad", odd_pairs(rads))
    if butterfly:
        coef = coef + got4[:SUB]
        coef = coef + lax.ppermute(coef, "rad", [(0, 3), (7, 4), (2, 5), (5, 2), (1, 6), (6, 1)])

    smoothed = pl.pallas_call(
        sweep_kernel,
        out_shape=whole,
        in_specs=[HBM] * 3 + [VMEM] * 7,
        out_specs=HBM,
        scratch_shapes=[
            pltpu.VMEM((3, layers + 2, rows, width), f32),
            pltpu.VMEM((3, layers, rows, width), f32),
            pltpu.VMEM((2, 3, rows, width), f32),
            pltpu.VMEM((2, 3, layers, SUB, width), f32),
            pltpu.VMEM((2 * layers, 3, SUB, width), f32),
            pltpu.VMEM((3, layers, rows, width), f32),
            pltpu.VMEM((layers + 2, COEFS, LANES), f32),
            pltpu.SemaphoreType.DMA((6,)),
            pltpu.SemaphoreType.DMA((layers,)),
        ],
        compiler_params=pltpu.CompilerParams(vmem_limit_bytes=VMEM_LIMIT),
        name="sweeps",
    )(*pinned[:2], kept, low_far, high_far, got1, got2, got3, got4, every)
    coef, smoothed = lax.optimization_barrier((coef, smoothed))

    shaped = gravity.reshape(2, 2, SUB, groups)
    gain_a = jnp.concatenate([shaped[0, 0], shaped[1, 0]], axis=1)
    gain_b = jnp.concatenate([shaped[0, 1], shaped[1, 1]], axis=1)
    potential = pl.pallas_call(
        functools.partial(synthesis_kernel, 2.0 / cycles),
        out_shape=jax.ShapeDtypeStruct((2, rows, width), f32),
        in_specs=[VMEM] * 5,
        out_specs=VMEM,
        scratch_shapes=[pltpu.VMEM((2 * groups, SUB, LANES), f32)],
        compiler_params=pltpu.CompilerParams(vmem_limit_bytes=VMEM_LIMIT),
        name="synthesis",
    )(coef, gain_a, gain_b, cycle_id, table)
    return smoothed, potential


def solution(mesh):
    in_specs = (
        P(None, "rad", "lat", None),
        P(None, "rad", "lat", None),
        P("rad"),
        P(),
        P(),
        P("lat", None),
        P(),
        P(),
    )
    out_specs = (P(None, "rad", "lat", None), P(None, "lat", None))
    return jax.shard_map(local, mesh=mesh, in_specs=in_specs, out_specs=out_specs, check_vma=False)
```

```python
import functools
import math

import jax
import jax.numpy as jnp
import numpy as np
from jax import lax
from jax.experimental import pallas as pl
from jax.experimental.pallas import tpu as pltpu
from jax.sharding import PartitionSpec as P

SWEEPS = 2
OMEGA = 0.8
LEAST_COUNT = 32
LANES = 128
SUB = 8
PAD = 8
COEFS = 16
BATCH = 5
VMEM_LIMIT = 16 * 1024 * 1024

VMEM = pl.BlockSpec(memory_space=pltpu.VMEM)
SMEM = pl.BlockSpec(memory_space=pltpu.SMEM)
HBM = pl.BlockSpec(memory_space=pltpu.HBM)
ANY = pl.BlockSpec(memory_space=pl.ANY)


def basis_table(degrees, cycles):
    groups = degrees // SUB
    degree = np.arange(degrees, dtype=np.int64)[:, None]
    cycle = np.arange(cycles, dtype=np.int64)[None, :]
    phase = degree * (2 * cycle + 1) % (4 * cycles)
    table = np.cos(np.pi * phase / (2.0 * cycles)).astype(np.float32)
    table = table.reshape(SUB, groups, cycles // LANES, LANES).transpose(2, 1, 0, 3)
    return np.ascontiguousarray(table.reshape(cycles // LANES, degrees, LANES))


def iota(shape, dim):
    return lax.broadcasted_iota(jnp.int32, shape, dim)


def lane_gather(values, index):
    return jnp.take_along_axis(values, index, axis=1, mode="promise_in_bounds")


def layer_scalars(layer, lid, stiff, coup):
    material = lid[layer]
    mu = stiff[material]
    return mu, [[coup[c, d, material] for d in range(3)] for c in range(3)]


def coefficient_rows(mu, k, width=LANES):
    row = iota((COEFS, width), 0)
    top = jnp.zeros((COEFS, width), jnp.float32)
    below = jnp.ones((COEFS, width), jnp.float32)
    for c in range(3):
        diag = 6.0 * mu + k[c][c]
        others = [d for d in range(3) if d != c]
        entries = [(c, 1.0), (3 + c, mu), (6 + 2 * c, k[c][others[0]]), (7 + 2 * c, k[c][others[1]])]
        for at, value in entries:
            top = jnp.where(row == at, OMEGA * value, top)
            below = jnp.where(row == at, diag, below)
    return top / below


def roll_rows(value, before, after):
    sub = iota(value.shape, 0)
    up = jnp.where(sub == 0, jnp.broadcast_to(before, value.shape), pltpu.roll(value, 1, 0))
    down = jnp.where(sub == SUB - 1, jnp.broadcast_to(after, value.shape), pltpu.roll(value, SUB - 1, 0))
    return up + down


def roll_columns(values):
    lane = iota(values[0].shape, 1)
    right = [pltpu.roll(value, 1, 1) for value in values]
    left = [pltpu.roll(value, LANES - 1, 1) for value in values]
    last = len(values) - 1
    return [
        jnp.where(lane == 0, right[j - 1] if j > 0 else 0.0, right[j])
        + jnp.where(lane == LANES - 1, left[j + 1] if j < last else 0.0, left[j])
        for j in range(len(values))
    ]


def relax(c, centers, neighbours, force, rows):
    d0, d1 = [d for d in range(3) if d != c]
    value = rows[c] * force + rows[3 + c] * neighbours
    value = value - (rows[6 + 2 * c] * centers[d0] + rows[7 + 2 * c] * centers[d1])
    return value + (1.0 - OMEGA) * centers[c]


def chunk(j):
    return pl.ds(LANES * j, LANES)


def spans(per_row, ref, *index):
    return [ref[index + (chunk(j),)] for j in range(per_row)]


def lane_scan(values, steps):
    lane = iota(values.shape, 1)
    step = 1
    while step < steps:
        values = values + jnp.where(lane >= step, pltpu.roll(values, step, 1), 0)
        step *= 2
    return values


def analysis_kernel(
    disp, forc, lid, stiff, coup, ids, cnt, tbl,
    kept, face1, face2, pay, send1, send2, every,
    u, f, s, cyc, num, tab, mat, windows, lids, stiffs, coups, first_ids, last_ids,
    small_sem, near_sem, u_sem, f_sem, face_sem, kept_sem, tab_sem,
):
    layers, rows, width = disp.shape[1:]
    chunks = cnt.shape[0]
    groups = tbl.shape[1] // SUB
    per_row = width // LANES
    lat, lats = lax.axis_index("lat"), lax.axis_size("lat")
    rad, rads = lax.axis_index("rad"), lax.axis_size("rad")
    bottom = rad == 0
    at_end = jnp.logical_or(bottom, rad == rads - 1)
    edge = jnp.where(bottom, 0, layers - 1)
    inner = jnp.where(bottom, 1, layers - 2)
    total = rows // SUB

    top = layers - 1
    odd = lax.rem(rad, 2) == 1
    small = [
        pltpu.make_async_copy(lid, lids, small_sem.at[0]),
        pltpu.make_async_copy(stiff, stiffs, small_sem.at[1]),
        pltpu.make_async_copy(coup, coups, small_sem.at[2]),
    ]
    cycles = [
        pltpu.make_async_copy(ids.at[pl.ds(0, SUB), pl.ds(0, LANES)], first_ids, near_sem.at[0]),
        pltpu.make_async_copy(
            ids.at[pl.ds(rows - SUB, SUB), pl.ds(width - LANES, LANES)], last_ids, near_sem.at[1]
        ),
        pltpu.make_async_copy(cnt, num, near_sem.at[2]),
        pltpu.make_async_copy(ids, cyc, near_sem.at[3]),
    ]
    loads_u = [pltpu.make_async_copy(disp.at[:, r], u.at[:, r], u_sem.at[r]) for r in range(layers)]
    loads_f = [pltpu.make_async_copy(forc.at[:, r], f.at[:, r], f_sem.at[r]) for r in range(layers)]
    order = [0, 1, top] + list(range(top - 1, 1, -1))
    for copy in small:
        copy.start()
    for r in order:
        loads_u[r].start()
        loads_f[r].start()
    for copy in cycles:
        copy.start()
    for copy in small:
        copy.wait()

    for r in range(layers):
        every[r] = coefficient_rows(*layer_scalars(r, lids, stiffs, coups))
    send1[...] = every[jnp.where(odd, 0, top)]
    send2[...] = every[jnp.where(odd, top, 0)]

    def local_sweep(layer, lower, upper):
        coef = [jnp.broadcast_to(every[layer, j:j + 1, :], (SUB, LANES)) for j in range(12)]
        none = jnp.zeros((1, LANES), jnp.float32)
        for g in range(total):
            here = slice(SUB * g, SUB * g + SUB)
            values = [spans(per_row, u, c, layer, here) for c in range(3)]
            for c in range(3):
                aside = roll_columns(values[c])
                for j in range(per_row):
                    at = (c, layer)
                    above = u[at + (slice(SUB * g - 1, SUB * g), chunk(j))] if g > 0 else none
                    under = u[at + (slice(SUB * g + SUB, SUB * g + SUB + 1), chunk(j))] if g < total - 1 else none
                    near = roll_rows(values[c][j], above, under) + aside[j]
                    if lower is not None:
                        near = near + u[c, lower, here, chunk(j)]
                    if upper is not None:
                        near = near + u[c, upper, here, chunk(j)]
                    value = relax(c, [values[d][j] for d in range(3)], near, f[c, layer, here, chunk(j)], coef)
                    s[c, layer, here, chunk(j)] = value

    keeps = [pltpu.make_async_copy(s.at[:, r], kept.at[:, r], kept_sem.at[r]) for r in range(layers)]
    loads_u[0].wait()
    loads_f[0].wait()
    loads_u[1].wait()
    local_sweep(0, None, 1)
    keeps[0].start()
    for r in range(2, layers):
        loads_u[r].wait()
    loads_f[top].wait()
    faces = []
    for n, (face, layer) in enumerate(((face1, jnp.where(odd, 0, top)), (face2, jnp.where(odd, top, 0)))):
        faces.append(pltpu.make_async_copy(u.at[:, layer], face.at[0], face_sem.at[2 * n]))
        faces.append(pltpu.make_async_copy(s.at[:, layer], face.at[1], face_sem.at[2 * n + 1]))
    faces[0].start()
    faces[2].start()
    local_sweep(top, top - 1, None)
    keeps[top].start()
    faces[1].start()
    faces[3].start()
    for r in range(1, top):
        loads_f[r].wait()

    def middle(r, carry):
        local_sweep(r, r - 1, r + 1)
        pltpu.make_async_copy(s.at[:, r], kept.at[:, r], kept_sem.at[r]).start()
        return carry

    lax.fori_loop(1, top, middle, 0)

    sub8, lane8 = iota((SUB, LANES), 0), iota((SUB, LANES), 1)
    before = sub8 < 2
    zero = jnp.zeros((SUB, LANES), jnp.float32)
    reach = 2 * width // LEAST_COUNT + 2
    for copy in cycles:
        copy.wait()
    first, last = first_ids[0, 0], last_ids[SUB - 1, LANES - 1]
    low_part = jnp.right_shift(jnp.maximum(first - reach, 0), 7)
    high_part = jnp.minimum(jnp.right_shift(last + reach, 7), chunks - 1)
    pay[0:SUB, :] = jnp.zeros((SUB, width), jnp.float32)

    def table(b):
        return [
            pltpu.make_async_copy(tbl.at[jnp.minimum(low_part + b * BATCH + i, chunks - 1)], tab.at[i], tab_sem.at[i])
            for i in range(BATCH)
        ]

    @pl.when(at_end)
    def _():
        for copy in table(0):
            copy.start()

        own_first = jnp.zeros((SUB, LANES), jnp.int32)
        own_last = own_first
        for j in range(per_row):
            own_first = own_first + jnp.where(cyc[0:SUB, LANES * j:LANES * j + LANES] == first, 1, 0)
            own_last = own_last + jnp.where(cyc[rows - SUB:rows, LANES * j:LANES * j + LANES] == last, 1, 0)

        def total_of(count):
            count = jnp.sum(count.astype(jnp.float32), axis=1, keepdims=True)
            return jnp.broadcast_to(jnp.sum(count, axis=0, keepdims=True), (SUB, LANES)).astype(jnp.int32)

        held_here = jnp.where(before, total_of(own_first), total_of(own_last))
        index = jnp.where(before, first - lane8, last + lane8)
        place, part = jnp.bitwise_and(index, LANES - 1), jnp.right_shift(index, 7)
        lengths = jnp.full((SUB, LANES), 2 ** 20, jnp.int32)
        part_first, part_last = jnp.right_shift(first, 7), jnp.right_shift(last, 7)
        for q in (part_first - 1, part_first, part_last, part_last + 1):
            row = num[pl.ds(jnp.clip(q, 0, chunks - 1), 1), :]
            known = jnp.logical_and(part == q, jnp.logical_and(part >= 0, part < chunks))
            lengths = jnp.where(known, lane_gather(jnp.broadcast_to(row, (SUB, LANES)), place), lengths)
        lengths = lengths - jnp.where(lane8 == 0, held_here, 0)
        limits = lane_scan(lengths, reach)
        caps = [jnp.broadcast_to(limits[:, i:i + 1], (SUB, LANES)) for i in range(reach)]
        spill_ids = []
        for j in range(per_row):
            column = LANES * j + lane8
            away = jnp.where(before, (width - 1 - column) + jnp.where(sub8 == 0, width, 0),
                             column + jnp.where(sub8 == 3, width, 0))
            passed = jnp.zeros((SUB, LANES), jnp.int32)
            for i in range(reach):
                passed = passed + jnp.where(away >= caps[i], 1, 0)
            spill_ids.append(jnp.where(sub8 < 4, jnp.where(before, first - passed, last + passed), 0))

        mat[0] = every[edge]
        mat[1] = every[inner]
        outer = [jnp.broadcast_to(mat[0, j:j + 1, :], (SUB, LANES)) for j in range(12)]
        below = [jnp.broadcast_to(mat[1, j:j + 1, :], (SUB, LANES)) for j in range(12)]

        def rows_of(g):
            return slice(SUB * g, SUB * g + SUB)

        def lateral(ref, g, index, ends):
            values = spans(per_row, ref, *index, rows_of(g))
            aside = roll_columns(values)
            out = []
            for j in range(per_row):
                above = ref[index + (slice(SUB * g - 1, SUB * g), chunk(j))] if g > 0 else ends[0][j]
                under = ref[index + (slice(SUB * g + SUB, SUB * g + SUB + 1), chunk(j))] if g < total - 1 else ends[1][j]
                out.append(roll_rows(values[j], above, under) + aside[j])
            return out

        low_in = jnp.where(lat > 0, 1.0, 0.0)
        high_in = jnp.where(lat < lats - 1, 1.0, 0.0)
        weight = jnp.where(sub8 == 1, low_in, jnp.where(sub8 == 2, high_in, 0.0))

        def ends_of(ref, index, j):
            low = jnp.broadcast_to(ref[index + (slice(0, 1), chunk(j))], (SUB, LANES))
            high = jnp.broadcast_to(ref[index + (slice(rows - 1, rows), chunk(j))], (SUB, LANES))
            return jnp.where(sub8 == 1, low, jnp.where(sub8 == 2, high, 0.0))

        over = [[outer[3 + c] * ends_of(u, (c, edge), j) * weight for j in range(per_row)] for c in range(3)]
        over_inner = [below[3] * ends_of(u, (0, inner), j) * weight for j in range(per_row)]
        aside = roll_columns(over[0])
        spill = []
        for j in range(per_row):
            shifted = jnp.where(sub8 == 0, pltpu.roll(over[0][j], SUB - 1, 0),
                                jnp.where(sub8 == 3, pltpu.roll(over[0][j], 1, 0), 0.0))
            near = over_inner[j] + aside[j] + shifted + ends_of(s, (0, edge), j)
            value = relax(0, [over[c][j] for c in range(3)], near, zero, outer)
            spill.append(value * jnp.where(before, low_in, high_in))
        ends = [[over[0][j][1:2, :] for j in range(per_row)], [over[0][j][2:3, :] for j in range(per_row)]]

        met = (width - 2) // LEAST_COUNT + 2

        def window_of(values, cycles):
            start = jnp.broadcast_to(cycles[0][:, 0:1], (SUB, LANES))
            offsets = [cycle - start for cycle in cycles]
            window = zero
            for t in range(met):
                picked = [jnp.where(offset == t, value, 0.0) for offset, value in zip(offsets, values)]
                sum_t = jnp.sum(functools.reduce(jnp.add, picked), axis=1, keepdims=True)
                window = jnp.where(lane8 == t, jnp.broadcast_to(sum_t, (SUB, LANES)), window)
            return window, start

        windowed = [window_of(spill, spill_ids)]
        for g in range(total):
            here = rows_of(g)
            centers = [spans(per_row, s, c, edge, here) for c in range(3)]
            near = lateral(s, g, (0, edge), ends)
            inners = spans(per_row, s, 0, inner, here)
            force = spans(per_row, f, 0, edge, here)
            values = [
                relax(0, [center[j] for center in centers], near[j] + inners[j], force[j], outer)
                for j in range(per_row)
            ]
            windowed.append(window_of(values, spans(per_row, cyc, here)))
        for i, (window, start) in enumerate(windowed):
            windows[0, i] = window
            windows[1, i] = start.astype(jnp.float32)

        half = jnp.where(bottom, groups, 0)

        def batch(b, result):
            @pl.when(b > 0)
            def _():
                for copy in table(b):
                    copy.start()

            means = []
            for i in range(BATCH):
                q = low_part + b * BATCH + i
                part = jnp.minimum(q, chunks - 1)
                acc = zero
                for w in range(total + 1):
                    at = q * LANES + lane8 - windows[1, w].astype(jnp.int32)
                    got = lane_gather(windows[0, w], jnp.bitwise_and(at, LANES - 1))
                    acc = acc + jnp.where(jnp.right_shift(at, 7) == 0, got, 0.0)
                mean = jnp.sum(acc, axis=0, keepdims=True) / num[pl.ds(part, 1), :].astype(jnp.float32)
                mean = jnp.where(q < chunks, mean, 0.0)
                means.append(jnp.broadcast_to(mean, (SUB, LANES)))
            for copy in table(b):
                copy.wait()
            for g in range(groups):
                acc = tab[0, SUB * g:SUB * g + SUB, :] * means[0]
                for i in range(1, BATCH):
                    acc = acc + tab[i, SUB * g:SUB * g + SUB, :] * means[i]
                column = jnp.broadcast_to(jnp.sum(acc, axis=1, keepdims=True), (SUB, LANES))
                result = jnp.where(lane8 == g + half, result + column, result)
            return result

        pay[0:SUB, 0:LANES] = lax.fori_loop(0, (high_part - low_part) // BATCH + 1, batch, zero)

    tall = 3 * layers

    def pack(ref, base, near):
        for c in range(3):
            for r in range(layers):
                at = base + c * layers + r
                ref[at:at + 1, :] = u[c, r, near:near + 1, :]
                ref[at + tall:at + tall + 1, :] = s[c, r, near:near + 1, :]

    pack(pay, SUB, 0)
    pack(pay, SUB + 2 * tall, rows - 1)

    for copy in faces + keeps:
        copy.wait()


def sweep_kernel(
    disp, forc, first, face1, face2, ring, got3, got4, every,
    out,
    s, f, face, fringe, rim, done, cf, in_sem, out_sem,
):
    layers, rows, width = disp.shape[1:]
    per_row = width // LANES
    total = rows // SUB
    tall = 3 * layers
    top = layers - 1
    loads = [
        pltpu.make_async_copy(disp.at[:, :, pl.ds(0, SUB)], fringe.at[0], in_sem.at[0]),
        pltpu.make_async_copy(disp.at[:, :, pl.ds(rows - SUB, SUB)], fringe.at[1], in_sem.at[1]),
        pltpu.make_async_copy(disp.at[:, 0], face.at[0], in_sem.at[2]),
        pltpu.make_async_copy(disp.at[:, top], face.at[1], in_sem.at[3]),
        pltpu.make_async_copy(first, s.at[:, pl.ds(1, layers)], in_sem.at[4]),
        pltpu.make_async_copy(forc, f, in_sem.at[5]),
    ]
    for copy in loads:
        copy.start()
    lat, lats = lax.axis_index("lat"), lax.axis_size("lat")
    rad, rads = lax.axis_index("rad"), lax.axis_size("rad")
    rad_odd = lax.rem(rad, 2) == 1
    before, after = jnp.maximum(lat - 1, 0), jnp.minimum(lat + 1, lats - 1)
    low_in, high_in = lat > 0, lat < lats - 1
    sub8 = iota((SUB, LANES), 0)

    def side_rows(base, j):
        at = SUB + base
        low = ring[before, at + 2 * tall:at + 2 * tall + layers, chunk(j)]
        high = ring[after, at:at + layers, chunk(j)]
        low, high = jnp.where(low_in, low, 0.0), jnp.where(high_in, high, 0.0)
        return jnp.concatenate([low, high], axis=0)

    below = lambda at: jnp.where(rad > 0, jnp.where(rad_odd, got3[at], got4[at]), 0.0)
    above = lambda at: jnp.where(rad < rads - 1, jnp.where(rad_odd, got4[at], got3[at]), 0.0)
    cf[0] = below(slice(SUB, SUB + COEFS))
    cf[layers + 1] = above(slice(SUB, SUB + COEFS))
    for r in range(layers):
        cf[1 + r] = every[r]
    corner_low = [below(slice(SUB + COEFS + SUB * j, SUB + COEFS + SUB * j + SUB)) for j in range(per_row)]
    corner_high = [above(slice(SUB + COEFS + SUB * j, SUB + COEFS + SUB * j + SUB)) for j in range(per_row)]

    def coefficients(layer):
        return [jnp.broadcast_to(cf[layer, j:j + 1, :], (SUB, LANES)) for j in range(12)]

    near_rows = [[side_rows(c * layers, j) for j in range(per_row)] for c in range(3)]
    loads[0].wait()
    loads[1].wait()
    keep = jnp.where(sub8 < layers, jnp.where(low_in, 1.0, 0.0), jnp.where(high_in, 1.0, 0.0))
    for c in range(3):
        gain = jnp.zeros((SUB, LANES), jnp.float32)
        for r in range(layers):
            here = jnp.broadcast_to(cf[1 + r, 3 + c:4 + c, :], (SUB, LANES))
            gain = jnp.where(jnp.logical_or(sub8 == r, sub8 == layers + r), here, gain)
        for j in range(per_row):
            near = jnp.zeros((SUB, LANES), jnp.float32)
            for r in range(layers):
                head = jnp.broadcast_to(fringe[0, c, r, 0:1, chunk(j)], near.shape)
                tail = jnp.broadcast_to(fringe[1, c, r, SUB - 1:SUB, chunk(j)], near.shape)
                near = jnp.where(sub8 == r, head, jnp.where(sub8 == layers + r, tail, near))
            ends = (
                (0, corner_low[j][c:c + 1, :]), (layers, corner_low[j][3 + c:4 + c, :]),
                (layers - 1, corner_high[j][c:c + 1, :]), (SUB - 1, corner_high[j][3 + c:4 + c, :]),
            )
            for row, corner in ends:
                near = near + jnp.where(sub8 == row, jnp.broadcast_to(corner, near.shape), 0.0)
            value = (side_rows(tall + c * layers, j) + gain * near) * keep
            for i in range(2 * layers):
                rim[i, c, :, chunk(j)] = jnp.broadcast_to(value[i:i + 1, :], (SUB, LANES))

    def beyond(layer, side, c, j):
        if layer == 0:
            return corner_low[j][3 * side + c:3 * side + c + 1, :]
        if layer == layers + 1:
            return corner_high[j][3 * side + c:3 * side + c + 1, :]
        at = layers * side + layer - 1
        return near_rows[c][j][at:at + 1, :]

    def lo(index):
        return jnp.where(rad_odd, face1[index], face2[index])

    def hi(index):
        return jnp.where(rad_odd, face2[index], face1[index])

    for copy in loads[2:5]:
        copy.wait()
    for layer in range(layers + 2):
        for c in range(3):
            gain = jnp.broadcast_to(cf[layer, 3 + c:4 + c, :], (SUB, LANES))
            for j in range(per_row):
                for g in range(total):
                    at = (slice(SUB * g, SUB * g + SUB), chunk(j))
                    value = None
                    if layer == 0:
                        value = lo((1, c) + at) + gain * face[(0, c) + at]
                    elif layer == layers + 1:
                        value = hi((1, c) + at) + gain * face[(1, c) + at]
                    elif layer in (1, layers) or g in (0, total - 1):
                        value = s[(c, layer) + at]
                    if layer == 1:
                        value = value + gain * lo((0, c) + at)
                    if layer == layers:
                        value = value + gain * hi((0, c) + at)
                    if value is None:
                        continue
                    if g == 0:
                        row = jnp.broadcast_to(beyond(layer, 0, c, j), value.shape)
                        value = value + jnp.where(sub8 == 0, gain * row, 0.0)
                    if g == total - 1:
                        row = jnp.broadcast_to(beyond(layer, 1, c, j), value.shape)
                        value = value + jnp.where(sub8 == SUB - 1, gain * row, 0.0)
                    s[(c, layer) + at] = value

    loads[5].wait()
    stores = [pltpu.make_async_copy(done.at[:, r], out.at[:, r], out_sem.at[r]) for r in range(layers)]
    for r in range(layers):
        layer = r + 1
        coef = coefficients(layer)
        for g in range(total):
            here = slice(SUB * g, SUB * g + SUB)
            values = [spans(per_row, s, c, layer, here) for c in range(3)]
            for c in range(3):
                aside = roll_columns(values[c])
                for j in range(per_row):
                    at = (c, layer)
                    if g > 0:
                        above_row = s[at + (slice(SUB * g - 1, SUB * g), chunk(j))]
                    else:
                        above_row = rim[r, c, :, chunk(j)]
                    if g < total - 1:
                        under_row = s[at + (slice(SUB * g + SUB, SUB * g + SUB + 1), chunk(j))]
                    else:
                        under_row = rim[layers + r, c, :, chunk(j)]
                    near = roll_rows(values[c][j], above_row, under_row) + aside[j]
                    near = near + (s[c, layer - 1, here, chunk(j)] + s[c, layer + 1, here, chunk(j)])
                    done[c, r, here, chunk(j)] = relax(
                        c, [values[d][j] for d in range(3)], near, f[c, r, here, chunk(j)], coef
                    )
        stores[r].start()
    for copy in stores:
        copy.wait()


def synthesis_kernel(scale, coef, gain_a, gain_b, ids, tab, out, factors):
    rows, width = ids.shape
    chunks = tab.shape[0]
    groups = tab.shape[1] // SUB
    per_row = width // LANES
    lane8 = iota((SUB, LANES), 1)
    here = coef[...]
    other = pltpu.roll(here, groups, 1)
    left = lane8 < groups
    surface = jnp.where(left, here, other)
    core = jnp.where(left, other, here)
    modes = (gain_a[...] * surface + gain_b[...] * core) * scale
    zero = jnp.zeros((SUB, LANES), jnp.float32)
    for i in range(2 * groups):
        factors[i] = jnp.broadcast_to(modes[:, i:i + 1], (SUB, LANES))
    low_part = jnp.right_shift(jnp.min(ids[0:1, 0:LANES]), 7)
    high_part = jnp.right_shift(jnp.max(ids[rows - 1:rows, width - LANES:width]), 7)

    def batch(b, carry):
        parts = [low_part + b * BATCH + i for i in range(BATCH)]
        blocks = [jnp.minimum(part, chunks - 1) for part in parts]
        sums = [[zero] * BATCH for _ in range(2)]
        for g in range(groups):
            for i in range(BATCH):
                block = tab[blocks[i], SUB * g:SUB * g + SUB, :]
                for k in range(2):
                    sums[k][i] = sums[k][i] + factors[k * groups + g] * block
        for k in range(2):
            for i in range(BATCH):
                sums[k][i] = jnp.broadcast_to(jnp.sum(sums[k][i], axis=0, keepdims=True), (SUB, LANES))
        for a in range(rows // SUB):
            for j in range(per_row):
                spot = (slice(SUB * a, SUB * a + SUB), chunk(j))
                cycle = ids[spot]
                place, part = jnp.bitwise_and(cycle, LANES - 1), jnp.right_shift(cycle, 7)
                values = [jnp.where(b == 0, 0.0, out[(k,) + spot]) for k in range(2)]
                for i in range(BATCH):
                    chosen = part == parts[i]
                    for k in range(2):
                        values[k] = jnp.where(chosen, lane_gather(sums[k][i], place), values[k])
                for k in range(2):
                    out[(k,) + spot] = values[k]
        return carry

    lax.fori_loop(0, (high_part - low_part) // BATCH + 1, batch, 0)


def even_pairs(count):
    return [(i, i ^ 1) for i in range(count)]


def odd_pairs(count):
    pairs = []
    for i in range(1, count, 2):
        j = (i + 1) % count
        pairs += [(i, j), (j, i)]
    return pairs


def local(displacement, forcing, layer_id, stiffness, coupling, cycle_id, cycle_count, gravity):
    _, layers, rows, width = displacement.shape
    cycles, degrees = cycle_count.shape[0], gravity.shape[2]
    chunks, groups = cycles // LANES, degrees // SUB
    if 2 * groups != LANES or 2 * layers != SUB:
        raise ValueError("unsupported sizes")
    lat, lats = lax.axis_index("lat"), lax.axis_size("lat")
    rad, rads = lax.axis_index("rad"), lax.axis_size("rad")
    rad_odd = rad % 2 == 1
    f32 = jnp.float32
    table = jnp.asarray(basis_table(degrees, cycles))
    per_row = width // LANES
    tall = 3 * layers
    face = jax.ShapeDtypeStruct((2, 3, rows, width), f32)

    whole = jax.ShapeDtypeStruct(displacement.shape, f32)
    pinned = [
        pltpu.with_memory_space_constraint(value, pltpu.HBM)
        for value in (
            displacement, forcing, layer_id, stiffness, jnp.transpose(coupling, (1, 2, 0)), cycle_id,
            cycle_count.reshape(chunks, LANES), table,
        )
    ]
    kept, face1, face2, pay, mine1, mine2, every = pl.pallas_call(
        analysis_kernel,
        out_shape=(
            whole, face, face,
            jax.ShapeDtypeStruct((SUB + 4 * tall, width), f32),
            jax.ShapeDtypeStruct((COEFS, LANES), f32),
            jax.ShapeDtypeStruct((COEFS, LANES), f32),
            jax.ShapeDtypeStruct((layers, COEFS, LANES), f32),
        ),
        in_specs=[HBM] * 8,
        out_specs=(HBM,) + (VMEM,) * 6,
        scratch_shapes=[
            pltpu.VMEM(displacement.shape, f32),
            pltpu.VMEM(displacement.shape, f32),
            pltpu.VMEM(displacement.shape, f32),
            pltpu.VMEM(cycle_id.shape, jnp.int32),
            pltpu.VMEM((chunks, LANES), jnp.int32),
            pltpu.VMEM((BATCH, degrees, LANES), f32),
            pltpu.VMEM((2, COEFS, LANES), f32),
            pltpu.VMEM((2, rows // SUB + 1, SUB, LANES), f32),
            pltpu.SMEM(layer_id.shape, jnp.int32),
            pltpu.SMEM(stiffness.shape, f32),
            pltpu.SMEM(coupling.shape[1:] + coupling.shape[:1], f32),
            pltpu.SMEM((SUB, LANES), jnp.int32),
            pltpu.SMEM((SUB, LANES), jnp.int32),
            pltpu.SemaphoreType.DMA((3,)),
            pltpu.SemaphoreType.DMA((4,)),
            pltpu.SemaphoreType.DMA((layers,)),
            pltpu.SemaphoreType.DMA((layers,)),
            pltpu.SemaphoreType.DMA((4,)),
            pltpu.SemaphoreType.DMA((layers,)),
            pltpu.SemaphoreType.DMA((BATCH,)),
        ],
        compiler_params=pltpu.CompilerParams(vmem_limit_bytes=VMEM_LIMIT),
        name="analysis",
    )(*pinned)

    beside2 = lax.ppermute(face2, "rad", odd_pairs(rads)[:-2])
    beside1 = lax.ppermute(face1, "rad", even_pairs(rads))

    ring = lax.all_gather(pay, "lat")
    coef = jnp.sum(ring[:, :SUB, :LANES], axis=0)
    butterfly = rads == 8
    if not butterfly:
        coef = lax.psum(coef, "rad")
    low = lax.dynamic_index_in_dim(ring, jnp.maximum(lat - 1, 0), keepdims=False)[SUB + 2 * tall:SUB + 3 * tall]
    high = lax.dynamic_index_in_dim(ring, jnp.minimum(lat + 1, lats - 1), keepdims=False)[SUB:SUB + tall]
    low, high = jnp.where(lat > 0, low, 0.0), jnp.where(lat < lats - 1, high, 0.0)

    def corners(layer):
        picks = [side[c * layers + layer][None] for side in (low, high) for c in range(3)]
        block = jnp.concatenate(picks + [jnp.zeros((SUB - 6, width), f32)], axis=0)
        return jnp.concatenate(jnp.split(block, per_row, axis=1), axis=0)

    corner_low, corner_high = corners(0), corners(layers - 1)
    send1 = jnp.where(rad_odd, corner_low, corner_high)
    send2 = jnp.where(rad_odd, corner_high, corner_low)
    first = jnp.concatenate([coef, mine1, send1], axis=0)
    first, beside1, beside2 = lax.optimization_barrier((first, beside1, beside2))
    got3 = lax.ppermute(first, "rad", even_pairs(rads))
    if butterfly:
        coef = coef + got3[:SUB]
    got4 = lax.ppermute(jnp.concatenate([coef, mine2, send2], axis=0), "rad", odd_pairs(rads))
    if butterfly:
        coef = coef + got4[:SUB]
        coef = coef + lax.ppermute(coef, "rad", [(0, 3), (7, 4), (2, 5), (5, 2), (1, 6), (6, 1)])

    smoothed = pl.pallas_call(
        sweep_kernel,
        out_shape=whole,
        in_specs=[HBM] * 3 + [VMEM] * 6,
        out_specs=HBM,
        scratch_shapes=[
            pltpu.VMEM((3, layers + 2, rows, width), f32),
            pltpu.VMEM((3, layers, rows, width), f32),
            pltpu.VMEM((2, 3, rows, width), f32),
            pltpu.VMEM((2, 3, layers, SUB, width), f32),
            pltpu.VMEM((2 * layers, 3, SUB, width), f32),
            pltpu.VMEM((3, layers, rows, width), f32),
            pltpu.VMEM((layers + 2, COEFS, LANES), f32),
            pltpu.SemaphoreType.DMA((6,)),
            pltpu.SemaphoreType.DMA((layers,)),
        ],
        compiler_params=pltpu.CompilerParams(vmem_limit_bytes=VMEM_LIMIT),
        name="sweeps",
    )(*pinned[:2], kept, beside1, beside2, ring, got3, got4, every)
    coef, smoothed = lax.optimization_barrier((coef, smoothed))

    shaped = gravity.reshape(2, 2, SUB, groups)
    gain_a = jnp.concatenate([shaped[0, 0], shaped[1, 0]], axis=1)
    gain_b = jnp.concatenate([shaped[0, 1], shaped[1, 1]], axis=1)
    potential = pl.pallas_call(
        functools.partial(synthesis_kernel, 2.0 / cycles),
        out_shape=jax.ShapeDtypeStruct((2, rows, width), f32),
        in_specs=[VMEM] * 5,
        out_specs=VMEM,
        scratch_shapes=[pltpu.VMEM((2 * groups, SUB, LANES), f32)],
        compiler_params=pltpu.CompilerParams(vmem_limit_bytes=VMEM_LIMIT),
        name="synthesis",
    )(coef, gain_a, gain_b, cycle_id, table)
    return smoothed, potential


def solution(mesh):
    in_specs = (
        P(None, "rad", "lat", None),
        P(None, "rad", "lat", None),
        P("rad"),
        P(),
        P(),
        P("lat", None),
        P(),
        P(),
    )
    out_specs = (P(None, "rad", "lat", None), P(None, "lat", None))
    return jax.shard_map(local, mesh=mesh, in_specs=in_specs, out_specs=out_specs, check_vma=False)
```

```python
import functools
import math

import jax
import jax.numpy as jnp
import numpy as np
from jax import lax
from jax.experimental import pallas as pl
from jax.experimental.pallas import tpu as pltpu
from jax.sharding import PartitionSpec as P

SWEEPS = 2
OMEGA = 0.8
LEAST_COUNT = 32
LANES = 128
SUB = 8
PAD = 8
COEFS = 16
BATCH = 5
VMEM_LIMIT = 16 * 1024 * 1024

VMEM = pl.BlockSpec(memory_space=pltpu.VMEM)
SMEM = pl.BlockSpec(memory_space=pltpu.SMEM)
HBM = pl.BlockSpec(memory_space=pltpu.HBM)
ANY = pl.BlockSpec(memory_space=pl.ANY)


def basis_table(degrees, cycles):
    groups = degrees // SUB
    degree = np.arange(degrees, dtype=np.int64)[:, None]
    cycle = np.arange(cycles, dtype=np.int64)[None, :]
    phase = degree * (2 * cycle + 1) % (4 * cycles)
    table = np.cos(np.pi * phase / (2.0 * cycles)).astype(np.float32)
    table = table.reshape(SUB, groups, cycles // LANES, LANES).transpose(2, 1, 0, 3)
    return np.ascontiguousarray(table.reshape(cycles // LANES, degrees, LANES))


def iota(shape, dim):
    return lax.broadcasted_iota(jnp.int32, shape, dim)


def lane_gather(values, index):
    return jnp.take_along_axis(values, index, axis=1, mode="promise_in_bounds")


def layer_scalars(layer, lid, stiff, coup):
    material = lid[layer]
    mu = stiff[material]
    return mu, [[coup[c, d, material] for d in range(3)] for c in range(3)]


def coefficient_rows(mu, k, width=LANES):
    row = iota((COEFS, width), 0)
    top = jnp.zeros((COEFS, width), jnp.float32)
    below = jnp.ones((COEFS, width), jnp.float32)
    for c in range(3):
        diag = 6.0 * mu + k[c][c]
        others = [d for d in range(3) if d != c]
        entries = [(c, 1.0), (3 + c, mu), (6 + 2 * c, k[c][others[0]]), (7 + 2 * c, k[c][others[1]])]
        for at, value in entries:
            top = jnp.where(row == at, OMEGA * value, top)
            below = jnp.where(row == at, diag, below)
    return top / below


def roll_rows(value, before, after):
    sub = iota(value.shape, 0)
    up = jnp.where(sub == 0, jnp.broadcast_to(before, value.shape), pltpu.roll(value, 1, 0))
    down = jnp.where(sub == SUB - 1, jnp.broadcast_to(after, value.shape), pltpu.roll(value, SUB - 1, 0))
    return up + down


def roll_columns(values):
    lane = iota(values[0].shape, 1)
    right = [pltpu.roll(value, 1, 1) for value in values]
    left = [pltpu.roll(value, LANES - 1, 1) for value in values]
    last = len(values) - 1
    return [
        jnp.where(lane == 0, right[j - 1] if j > 0 else 0.0, right[j])
        + jnp.where(lane == LANES - 1, left[j + 1] if j < last else 0.0, left[j])
        for j in range(len(values))
    ]


def relax(c, centers, neighbours, force, rows):
    d0, d1 = [d for d in range(3) if d != c]
    value = rows[c] * force + rows[3 + c] * neighbours
    value = value - (rows[6 + 2 * c] * centers[d0] + rows[7 + 2 * c] * centers[d1])
    return value + (1.0 - OMEGA) * centers[c]


def chunk(j):
    return pl.ds(LANES * j, LANES)


def spans(per_row, ref, *index):
    return [ref[index + (chunk(j),)] for j in range(per_row)]


def lane_scan(values, steps):
    lane = iota(values.shape, 1)
    step = 1
    while step < steps:
        values = values + jnp.where(lane >= step, pltpu.roll(values, step, 1), 0)
        step *= 2
    return values


def analysis_kernel(
    disp, forc, lid, stiff, coup, ids, cnt, grav, tbl,
    u, f, s, face1, face2, pay, send, every, gains,
    cyc, num, tab, mat, windows, gain_in, lids, stiffs, coups, first_ids, last_ids,
    small_sem, near_sem, u_sem, f_sem, face_sem, tab_sem,
):
    layers, rows, width = disp.shape[1:]
    chunks = cnt.shape[0]
    groups = tbl.shape[1] // SUB
    per_row = width // LANES
    lat, lats = lax.axis_index("lat"), lax.axis_size("lat")
    rad, rads = lax.axis_index("rad"), lax.axis_size("rad")
    bottom = rad == 0
    at_end = jnp.logical_or(bottom, rad == rads - 1)
    edge = jnp.where(bottom, 0, layers - 1)
    inner = jnp.where(bottom, 1, layers - 2)
    total = rows // SUB

    top = layers - 1
    odd = lax.rem(rad, 2) == 1
    small = [
        pltpu.make_async_copy(lid, lids, small_sem.at[0]),
        pltpu.make_async_copy(stiff, stiffs, small_sem.at[1]),
        pltpu.make_async_copy(coup, coups, small_sem.at[2]),
    ]
    cycles = [
        pltpu.make_async_copy(ids.at[pl.ds(0, SUB), pl.ds(0, LANES)], first_ids, near_sem.at[0]),
        pltpu.make_async_copy(
            ids.at[pl.ds(rows - SUB, SUB), pl.ds(width - LANES, LANES)], last_ids, near_sem.at[1]
        ),
        pltpu.make_async_copy(cnt, num, near_sem.at[2]),
        pltpu.make_async_copy(ids, cyc, near_sem.at[3]),
        pltpu.make_async_copy(grav, gain_in, near_sem.at[4]),
    ]
    loads_u = [pltpu.make_async_copy(disp.at[:, r], u.at[:, r], u_sem.at[r]) for r in range(layers)]
    loads_f = [pltpu.make_async_copy(forc.at[:, r], f.at[:, r], f_sem.at[r]) for r in range(layers)]
    order = [0, 1, top] + list(range(top - 1, 1, -1))
    for copy in small:
        copy.start()
    for r in order:
        loads_u[r].start()
        loads_f[r].start()
    for copy in cycles:
        copy.start()
    for copy in small:
        copy.wait()

    for r in range(layers):
        every[r] = coefficient_rows(*layer_scalars(r, lids, stiffs, coups))
    send[...] = every[jnp.where(odd, top, 0)]
    at_core = every[jnp.where(odd, 0, top)]

    def local_sweep(layer, lower, upper):
        coef = [jnp.broadcast_to(every[layer, j:j + 1, :], (SUB, LANES)) for j in range(12)]
        none = jnp.zeros((1, LANES), jnp.float32)
        for g in range(total):
            here = slice(SUB * g, SUB * g + SUB)
            values = [spans(per_row, u, c, layer, here) for c in range(3)]
            for c in range(3):
                aside = roll_columns(values[c])
                for j in range(per_row):
                    at = (c, layer)
                    above = u[at + (slice(SUB * g - 1, SUB * g), chunk(j))] if g > 0 else none
                    under = u[at + (slice(SUB * g + SUB, SUB * g + SUB + 1), chunk(j))] if g < total - 1 else none
                    near = roll_rows(values[c][j], above, under) + aside[j]
                    if lower is not None:
                        near = near + u[c, lower, here, chunk(j)]
                    if upper is not None:
                        near = near + u[c, upper, here, chunk(j)]
                    value = relax(c, [values[d][j] for d in range(3)], near, f[c, layer, here, chunk(j)], coef)
                    s[c, layer, here, chunk(j)] = value

    loads_u[0].wait()
    loads_f[0].wait()
    loads_u[1].wait()
    local_sweep(0, None, 1)
    for r in range(2, layers):
        loads_u[r].wait()
    loads_f[top].wait()
    faces = []
    for n, (face, layer) in enumerate(((face1, jnp.where(odd, 0, top)), (face2, jnp.where(odd, top, 0)))):
        faces.append(pltpu.make_async_copy(u.at[:, layer], face.at[0], face_sem.at[2 * n]))
        faces.append(pltpu.make_async_copy(s.at[:, layer], face.at[1], face_sem.at[2 * n + 1]))
    faces[0].start()
    faces[2].start()
    local_sweep(top, top - 1, None)
    faces[1].start()
    faces[3].start()
    for r in range(1, top):
        loads_f[r].wait()

    def middle(r, carry):
        local_sweep(r, r - 1, r + 1)
        return carry

    lax.fori_loop(1, top, middle, 0)

    sub8, lane8 = iota((SUB, LANES), 0), iota((SUB, LANES), 1)
    before = sub8 < 2
    zero = jnp.zeros((SUB, LANES), jnp.float32)
    reach = 2 * width // LEAST_COUNT + 2
    for copy in cycles:
        copy.wait()
    first, last = first_ids[0, 0], last_ids[SUB - 1, LANES - 1]
    low_part = jnp.right_shift(jnp.maximum(first - reach, 0), 7)
    high_part = jnp.minimum(jnp.right_shift(last + reach, 7), chunks - 1)
    pay[0:SUB, 0:LANES] = jnp.zeros((SUB, LANES), jnp.float32)
    pay[0:SUB, LANES:2 * LANES] = at_core[0:SUB]
    pay[0:SUB, 2 * LANES:3 * LANES] = at_core[SUB:]

    lane1 = iota((1, LANES), 1)
    for load in range(2):
        for m in range(groups * SUB // LANES):
            one, two = gain_in[0, load:load + 1, chunk(m)], gain_in[1, load:load + 1, chunk(m)]
            gains[load, 2 * m:2 * m + 1, :] = jnp.where(lane1 < groups, one, pltpu.roll(two, groups, 1))
            gains[load, 2 * m + 1:2 * m + 2, :] = jnp.where(lane1 < groups, pltpu.roll(one, groups, 1), two)

    def table(b):
        return [
            pltpu.make_async_copy(tbl.at[jnp.minimum(low_part + b * BATCH + i, chunks - 1)], tab.at[i], tab_sem.at[i])
            for i in range(BATCH)
        ]

    @pl.when(at_end)
    def _():
        for copy in table(0):
            copy.start()

        own_first = jnp.zeros((SUB, LANES), jnp.int32)
        own_last = own_first
        for j in range(per_row):
            own_first = own_first + jnp.where(cyc[0:SUB, LANES * j:LANES * j + LANES] == first, 1, 0)
            own_last = own_last + jnp.where(cyc[rows - SUB:rows, LANES * j:LANES * j + LANES] == last, 1, 0)

        def total_of(count):
            count = jnp.sum(count.astype(jnp.float32), axis=1, keepdims=True)
            return jnp.broadcast_to(jnp.sum(count, axis=0, keepdims=True), (SUB, LANES)).astype(jnp.int32)

        held_here = jnp.where(before, total_of(own_first), total_of(own_last))
        index = jnp.where(before, first - lane8, last + lane8)
        place, part = jnp.bitwise_and(index, LANES - 1), jnp.right_shift(index, 7)
        lengths = jnp.full((SUB, LANES), 2 ** 20, jnp.int32)
        part_first, part_last = jnp.right_shift(first, 7), jnp.right_shift(last, 7)
        for q in (part_first - 1, part_first, part_last, part_last + 1):
            row = num[pl.ds(jnp.clip(q, 0, chunks - 1), 1), :]
            known = jnp.logical_and(part == q, jnp.logical_and(part >= 0, part < chunks))
            lengths = jnp.where(known, lane_gather(jnp.broadcast_to(row, (SUB, LANES)), place), lengths)
        lengths = lengths - jnp.where(lane8 == 0, held_here, 0)
        limits = lane_scan(lengths, reach)
        caps = [jnp.broadcast_to(limits[:, i:i + 1], (SUB, LANES)) for i in range(reach)]
        spill_ids = []
        for j in range(per_row):
            column = LANES * j + lane8
            away = jnp.where(before, (width - 1 - column) + jnp.where(sub8 == 0, width, 0),
                             column + jnp.where(sub8 == 3, width, 0))
            passed = jnp.zeros((SUB, LANES), jnp.int32)
            for i in range(reach):
                passed = passed + jnp.where(away >= caps[i], 1, 0)
            spill_ids.append(jnp.where(sub8 < 4, jnp.where(before, first - passed, last + passed), 0))

        mat[0] = every[edge]
        mat[1] = every[inner]
        outer = [jnp.broadcast_to(mat[0, j:j + 1, :], (SUB, LANES)) for j in range(12)]
        below = [jnp.broadcast_to(mat[1, j:j + 1, :], (SUB, LANES)) for j in range(12)]

        def rows_of(g):
            return slice(SUB * g, SUB * g + SUB)

        def lateral(ref, g, index, ends):
            values = spans(per_row, ref, *index, rows_of(g))
            aside = roll_columns(values)
            out = []
            for j in range(per_row):
                above = ref[index + (slice(SUB * g - 1, SUB * g), chunk(j))] if g > 0 else ends[0][j]
                under = ref[index + (slice(SUB * g + SUB, SUB * g + SUB + 1), chunk(j))] if g < total - 1 else ends[1][j]
                out.append(roll_rows(values[j], above, under) + aside[j])
            return out

        low_in = jnp.where(lat > 0, 1.0, 0.0)
        high_in = jnp.where(lat < lats - 1, 1.0, 0.0)
        weight = jnp.where(sub8 == 1, low_in, jnp.where(sub8 == 2, high_in, 0.0))

        def ends_of(ref, index, j):
            low = jnp.broadcast_to(ref[index + (slice(0, 1), chunk(j))], (SUB, LANES))
            high = jnp.broadcast_to(ref[index + (slice(rows - 1, rows), chunk(j))], (SUB, LANES))
            return jnp.where(sub8 == 1, low, jnp.where(sub8 == 2, high, 0.0))

        over = [[outer[3 + c] * ends_of(u, (c, edge), j) * weight for j in range(per_row)] for c in range(3)]
        over_inner = [below[3] * ends_of(u, (0, inner), j) * weight for j in range(per_row)]
        aside = roll_columns(over[0])
        spill = []
        for j in range(per_row):
            shifted = jnp.where(sub8 == 0, pltpu.roll(over[0][j], SUB - 1, 0),
                                jnp.where(sub8 == 3, pltpu.roll(over[0][j], 1, 0), 0.0))
            near = over_inner[j] + aside[j] + shifted + ends_of(s, (0, edge), j)
            value = relax(0, [over[c][j] for c in range(3)], near, zero, outer)
            spill.append(value * jnp.where(before, low_in, high_in))
        ends = [[over[0][j][1:2, :] for j in range(per_row)], [over[0][j][2:3, :] for j in range(per_row)]]

        met = (width - 2) // LEAST_COUNT + 2

        def window_of(values, cycles):
            start = jnp.broadcast_to(cycles[0][:, 0:1], (SUB, LANES))
            offsets = [cycle - start for cycle in cycles]
            window = zero
            for t in range(met):
                picked = [jnp.where(offset == t, value, 0.0) for offset, value in zip(offsets, values)]
                sum_t = jnp.sum(functools.reduce(jnp.add, picked), axis=1, keepdims=True)
                window = jnp.where(lane8 == t, jnp.broadcast_to(sum_t, (SUB, LANES)), window)
            return window, start

        windowed = [window_of(spill, spill_ids)]
        for g in range(total):
            here = rows_of(g)
            centers = [spans(per_row, s, c, edge, here) for c in range(3)]
            near = lateral(s, g, (0, edge), ends)
            inners = spans(per_row, s, 0, inner, here)
            force = spans(per_row, f, 0, edge, here)
            values = [
                relax(0, [center[j] for center in centers], near[j] + inners[j], force[j], outer)
                for j in range(per_row)
            ]
            windowed.append(window_of(values, spans(per_row, cyc, here)))
        for i, (window, start) in enumerate(windowed):
            windows[0, i] = window
            windows[1, i] = start.astype(jnp.float32)

        half = jnp.where(bottom, groups, 0)

        def batch(b, result):
            @pl.when(b > 0)
            def _():
                for copy in table(b):
                    copy.start()

            means = []
            for i in range(BATCH):
                q = low_part + b * BATCH + i
                part = jnp.minimum(q, chunks - 1)
                acc = zero
                for w in range(total + 1):
                    at = q * LANES + lane8 - windows[1, w].astype(jnp.int32)
                    got = lane_gather(windows[0, w], jnp.bitwise_and(at, LANES - 1))
                    acc = acc + jnp.where(jnp.right_shift(at, 7) == 0, got, 0.0)
                mean = jnp.sum(acc, axis=0, keepdims=True) / num[pl.ds(part, 1), :].astype(jnp.float32)
                mean = jnp.where(q < chunks, mean, 0.0)
                means.append(jnp.broadcast_to(mean, (SUB, LANES)))
            for copy in table(b):
                copy.wait()
            for g in range(groups):
                acc = tab[0, SUB * g:SUB * g + SUB, :] * means[0]
                for i in range(1, BATCH):
                    acc = acc + tab[i, SUB * g:SUB * g + SUB, :] * means[i]
                column = jnp.broadcast_to(jnp.sum(acc, axis=1, keepdims=True), (SUB, LANES))
                result = jnp.where(lane8 == g + half, result + column, result)
            return result

        pay[0:SUB, 0:LANES] = lax.fori_loop(0, (high_part - low_part) // BATCH + 1, batch, zero)

    tall = 3 * layers

    def pack(ref, base, near):
        for c in range(3):
            for r in range(layers):
                at = base + c * layers + r
                ref[at:at + 1, :] = u[c, r, near:near + 1, :]
                ref[at + tall:at + tall + 1, :] = s[c, r, near:near + 1, :]

    pack(pay, SUB, 0)
    pack(pay, SUB + 2 * tall, rows - 1)

    for copy in faces:
        copy.wait()


def relay_kernel(ring, send, out):
    cores = 2
    lat, lats = lax.axis_index("lat"), lax.axis_size("lat")
    core = lax.rem(lax.axis_index("rad"), cores)
    members, _, width = ring.shape
    tall = (ring.shape[1] - SUB) // 4
    layers = tall // 3
    coef = ring[0, 0:SUB, 0:LANES]
    for i in range(1, members):
        coef = coef + ring[i, 0:SUB, 0:LANES]
    out[0:SUB, :] = coef
    out[SUB:SUB + COEFS, :] = send[...]
    before, after = cores * jnp.maximum(lat - 1, 0) + core, cores * jnp.minimum(lat + 1, lats - 1) + core
    low_in, high_in = lat > 0, lat < lats - 1
    for j in range(width // LANES):
        base = SUB + COEFS + SUB * j
        out[base:base + SUB, :] = jnp.zeros((SUB, LANES), jnp.float32)
        for c in range(3):
            for at, member, valid, start in ((c, before, low_in, 2 * tall), (3 + c, after, high_in, 0)):
                row = SUB + start + c * layers
                bottom, top = ring[member, row:row + 1, chunk(j)], ring[member, row + layers - 1:row + layers, chunk(j)]
                out[base + at:base + at + 1, :] = jnp.where(valid, jnp.where(core == 1, top, bottom), 0.0)


def sweep_kernel(
    u, f, first, face1, face2, ring, got, every,
    out,
    s, rim, done, cf, out_sem,
):
    layers, rows, width = u.shape[1:]
    per_row = width // LANES
    total = rows // SUB
    tall = 3 * layers
    top = layers - 1
    lat, lats = lax.axis_index("lat"), lax.axis_size("lat")
    rad, rads = lax.axis_index("rad"), lax.axis_size("rad")
    rad_odd = lax.rem(rad, 2) == 1
    cores = 2
    core = lax.rem(rad, cores)
    lower, upper = cores * jnp.maximum(lat - 1, 0), cores * jnp.minimum(lat + 1, lats - 1)
    low_in, high_in = lat > 0, lat < lats - 1
    sub8 = iota((SUB, LANES), 0)

    def side_rows(base, j):
        at = SUB + base
        low = ring[lower + core, at + 2 * tall:at + 2 * tall + layers, chunk(j)]
        high = ring[upper + core, at:at + layers, chunk(j)]
        low, high = jnp.where(low_in, low, 0.0), jnp.where(high_in, high, 0.0)
        return jnp.concatenate([low, high], axis=0)

    mate = 1 - core
    own_chip = jnp.concatenate(
        [ring[cores * lat + mate, 0:SUB, LANES:2 * LANES], ring[cores * lat + mate, 0:SUB, 2 * LANES:3 * LANES]], axis=0
    )
    other_chip = got[SUB:SUB + COEFS, :]
    lowest, highest = rad == 0, rad == rads - 1
    cf[0] = jnp.where(rad_odd, own_chip, jnp.where(lowest, 0.0, other_chip))
    cf[layers + 1] = jnp.where(rad_odd, jnp.where(highest, 0.0, other_chip), own_chip)
    for r in range(layers):
        cf[1 + r] = every[r]
    corner_low, corner_high = [], []
    for j in range(per_row):
        base = SUB + COEFS + SUB * j
        other = got[base:base + SUB, :]
        rows_own = []
        for member, valid, start in ((lower + mate, low_in, 2 * tall), (upper + mate, high_in, 0)):
            for c in range(3):
                row = SUB + start + c * layers
                near_end, far_end = ring[member, row:row + 1, chunk(j)], ring[member, row + top:row + top + 1, chunk(j)]
                rows_own.append(jnp.where(valid, jnp.where(rad_odd, far_end, near_end), 0.0))
        rows_own.append(jnp.zeros((SUB - 6, LANES), jnp.float32))
        own = jnp.concatenate(rows_own, axis=0)
        corner_low.append(jnp.where(rad_odd, own, jnp.where(lowest, 0.0, other)))
        corner_high.append(jnp.where(rad_odd, jnp.where(highest, 0.0, other), own))

    def coefficients(layer):
        return [jnp.broadcast_to(cf[layer, j:j + 1, :], (SUB, LANES)) for j in range(12)]

    near_rows = [[side_rows(c * layers, j) for j in range(per_row)] for c in range(3)]
    keep = jnp.where(sub8 < layers, jnp.where(low_in, 1.0, 0.0), jnp.where(high_in, 1.0, 0.0))
    for c in range(3):
        gain = jnp.zeros((SUB, LANES), jnp.float32)
        for r in range(layers):
            here = jnp.broadcast_to(cf[1 + r, 3 + c:4 + c, :], (SUB, LANES))
            gain = jnp.where(jnp.logical_or(sub8 == r, sub8 == layers + r), here, gain)
        for j in range(per_row):
            near = jnp.zeros((SUB, LANES), jnp.float32)
            for r in range(layers):
                head = jnp.broadcast_to(u[c, r, 0:1, chunk(j)], near.shape)
                tail = jnp.broadcast_to(u[c, r, rows - 1:rows, chunk(j)], near.shape)
                near = jnp.where(sub8 == r, head, jnp.where(sub8 == layers + r, tail, near))
            ends = (
                (0, corner_low[j][c:c + 1, :]), (layers, corner_low[j][3 + c:4 + c, :]),
                (layers - 1, corner_high[j][c:c + 1, :]), (SUB - 1, corner_high[j][3 + c:4 + c, :]),
            )
            for row, corner in ends:
                near = near + jnp.where(sub8 == row, jnp.broadcast_to(corner, near.shape), 0.0)
            value = (side_rows(tall + c * layers, j) + gain * near) * keep
            for i in range(2 * layers):
                rim[i, c, :, chunk(j)] = jnp.broadcast_to(value[i:i + 1, :], (SUB, LANES))

    def beyond(layer, side, c, j):
        if layer == 0:
            return corner_low[j][3 * side + c:3 * side + c + 1, :]
        if layer == layers + 1:
            return corner_high[j][3 * side + c:3 * side + c + 1, :]
        at = layers * side + layer - 1
        return near_rows[c][j][at:at + 1, :]

    def lo(index):
        return jnp.where(rad_odd, face1[index], face2[index])

    def hi(index):
        return jnp.where(rad_odd, face2[index], face1[index])

    for layer in range(layers + 2):
        for c in range(3):
            gain = jnp.broadcast_to(cf[layer, 3 + c:4 + c, :], (SUB, LANES))
            for j in range(per_row):
                for g in range(total):
                    at = (slice(SUB * g, SUB * g + SUB), chunk(j))
                    if layer == 0:
                        value = lo((1, c) + at) + gain * u[(c, 0) + at]
                    elif layer == layers + 1:
                        value = hi((1, c) + at) + gain * u[(c, top) + at]
                    else:
                        value = first[(c, layer - 1) + at]
                    if layer == 1:
                        value = value + gain * lo((0, c) + at)
                    if layer == layers:
                        value = value + gain * hi((0, c) + at)
                    if g == 0:
                        row = jnp.broadcast_to(beyond(layer, 0, c, j), value.shape)
                        value = value + jnp.where(sub8 == 0, gain * row, 0.0)
                    if g == total - 1:
                        row = jnp.broadcast_to(beyond(layer, 1, c, j), value.shape)
                        value = value + jnp.where(sub8 == SUB - 1, gain * row, 0.0)
                    s[(c, layer) + at] = value

    stores = [pltpu.make_async_copy(done.at[:, r], out.at[:, r], out_sem.at[r]) for r in range(layers)]
    for r in range(layers):
        layer = r + 1
        coef = coefficients(layer)
        for g in range(total):
            here = slice(SUB * g, SUB * g + SUB)
            values = [spans(per_row, s, c, layer, here) for c in range(3)]
            for c in range(3):
                aside = roll_columns(values[c])
                for j in range(per_row):
                    at = (c, layer)
                    if g > 0:
                        above_row = s[at + (slice(SUB * g - 1, SUB * g), chunk(j))]
                    else:
                        above_row = rim[r, c, :, chunk(j)]
                    if g < total - 1:
                        under_row = s[at + (slice(SUB * g + SUB, SUB * g + SUB + 1), chunk(j))]
                    else:
                        under_row = rim[layers + r, c, :, chunk(j)]
                    near = roll_rows(values[c][j], above_row, under_row) + aside[j]
                    near = near + (s[c, layer - 1, here, chunk(j)] + s[c, layer + 1, here, chunk(j)])
                    done[c, r, here, chunk(j)] = relax(
                        c, [values[d][j] for d in range(3)], near, f[c, r, here, chunk(j)], coef
                    )
        stores[r].start()
    for copy in stores:
        copy.wait()


def synthesis_kernel(scale, coef, rest, gains, ids, tab, out, factors):
    rows, width = ids.shape
    chunks = tab.shape[0]
    groups = tab.shape[1] // SUB
    per_row = width // LANES
    lane8 = iota((SUB, LANES), 1)
    here = coef[...] + rest[...]
    other = pltpu.roll(here, groups, 1)
    left = lane8 < groups
    surface = jnp.where(left, here, other)
    core = jnp.where(left, other, here)
    modes = (gains[0] * surface + gains[1] * core) * scale
    zero = jnp.zeros((SUB, LANES), jnp.float32)
    for i in range(2 * groups):
        factors[i] = jnp.broadcast_to(modes[:, i:i + 1], (SUB, LANES))
    low_part = jnp.right_shift(jnp.min(ids[0:1, 0:LANES]), 7)
    high_part = jnp.right_shift(jnp.max(ids[rows - 1:rows, width - LANES:width]), 7)

    def batch(b, carry):
        parts = [low_part + b * BATCH + i for i in range(BATCH)]
        blocks = [jnp.minimum(part, chunks - 1) for part in parts]
        sums = [[zero] * BATCH for _ in range(2)]
        for g in range(groups):
            for i in range(BATCH):
                block = tab[blocks[i], SUB * g:SUB * g + SUB, :]
                for k in range(2):
                    sums[k][i] = sums[k][i] + factors[k * groups + g] * block
        for k in range(2):
            for i in range(BATCH):
                sums[k][i] = jnp.broadcast_to(jnp.sum(sums[k][i], axis=0, keepdims=True), (SUB, LANES))
        for a in range(rows // SUB):
            for j in range(per_row):
                spot = (slice(SUB * a, SUB * a + SUB), chunk(j))
                cycle = ids[spot]
                place, part = jnp.bitwise_and(cycle, LANES - 1), jnp.right_shift(cycle, 7)
                values = [jnp.where(b == 0, 0.0, out[(k,) + spot]) for k in range(2)]
                for i in range(BATCH):
                    chosen = part == parts[i]
                    for k in range(2):
                        values[k] = jnp.where(chosen, lane_gather(sums[k][i], place), values[k])
                for k in range(2):
                    out[(k,) + spot] = values[k]
        return carry

    lax.fori_loop(0, (high_part - low_part) // BATCH + 1, batch, 0)


def even_pairs(count):
    return [(i, i ^ 1) for i in range(count)]


def odd_pairs(count):
    pairs = []
    for i in range(1, count, 2):
        j = (i + 1) % count
        pairs += [(i, j), (j, i)]
    return pairs


def local(displacement, forcing, layer_id, stiffness, coupling, cycle_id, cycle_count, gravity):
    _, layers, rows, width = displacement.shape
    cycles, degrees = cycle_count.shape[0], gravity.shape[2]
    chunks, groups = cycles // LANES, degrees // SUB
    lats, rads, cores = lax.axis_size("lat"), lax.axis_size("rad"), 2
    if 2 * groups != LANES or 2 * layers != SUB or rads % cores or width < 3 * LANES:
        raise ValueError("unsupported sizes")
    f32 = jnp.float32
    table = jnp.asarray(basis_table(degrees, cycles))
    per_row = width // LANES
    tall = 3 * layers
    face = jax.ShapeDtypeStruct((2, 3, rows, width), f32)

    whole = jax.ShapeDtypeStruct(displacement.shape, f32)
    pinned = [
        pltpu.with_memory_space_constraint(value, pltpu.HBM)
        for value in (
            displacement, forcing, layer_id, stiffness, jnp.transpose(coupling, (1, 2, 0)), cycle_id,
            cycle_count.reshape(chunks, LANES), gravity, table,
        )
    ]
    u, f, swept, face1, face2, pay, mine, every, gains = pl.pallas_call(
        analysis_kernel,
        out_shape=(
            whole, whole, whole, face, face,
            jax.ShapeDtypeStruct((SUB + 4 * tall, width), f32),
            jax.ShapeDtypeStruct((COEFS, LANES), f32),
            jax.ShapeDtypeStruct((layers, COEFS, LANES), f32),
            jax.ShapeDtypeStruct((2, SUB, LANES), f32),
        ),
        in_specs=[HBM] * 9,
        out_specs=(VMEM,) * 9,
        scratch_shapes=[
            pltpu.VMEM(cycle_id.shape, jnp.int32),
            pltpu.VMEM((chunks, LANES), jnp.int32),
            pltpu.VMEM((BATCH, degrees, LANES), f32),
            pltpu.VMEM((2, COEFS, LANES), f32),
            pltpu.VMEM((2, rows // SUB + 1, SUB, LANES), f32),
            pltpu.VMEM(gravity.shape, f32),
            pltpu.SMEM(layer_id.shape, jnp.int32),
            pltpu.SMEM(stiffness.shape, f32),
            pltpu.SMEM(coupling.shape[1:] + coupling.shape[:1], f32),
            pltpu.SMEM((SUB, LANES), jnp.int32),
            pltpu.SMEM((SUB, LANES), jnp.int32),
            pltpu.SemaphoreType.DMA((3,)),
            pltpu.SemaphoreType.DMA((5,)),
            pltpu.SemaphoreType.DMA((layers,)),
            pltpu.SemaphoreType.DMA((layers,)),
            pltpu.SemaphoreType.DMA((4,)),
            pltpu.SemaphoreType.DMA((BATCH,)),
        ],
        compiler_params=pltpu.CompilerParams(vmem_limit_bytes=VMEM_LIMIT),
        name="analysis",
    )(*pinned)

    beside2 = lax.ppermute(face2, "rad", odd_pairs(rads)[:-2])
    beside1 = lax.ppermute(face1, "rad", even_pairs(rads))

    chips = [[a * rads + b + c for a in range(lats) for c in range(cores)] for b in range(0, rads, cores)]
    ring = lax.all_gather(pay, ("lat", "rad"), axis_index_groups=chips)
    outward = pl.pallas_call(
        relay_kernel,
        out_shape=jax.ShapeDtypeStruct((SUB + COEFS + SUB * per_row, LANES), f32),
        in_specs=[VMEM] * 2,
        out_specs=VMEM,
        compiler_params=pltpu.CompilerParams(vmem_limit_bytes=VMEM_LIMIT),
        name="relay",
    )(ring, mine)
    outward, beside1, beside2 = lax.optimization_barrier((outward, beside1, beside2))
    got = lax.ppermute(outward, "rad", odd_pairs(rads))
    coef = outward[:SUB]
    if rads == 8:
        coef = coef + got[:SUB]
        rest = lax.ppermute(coef, "rad", [(0, 3), (7, 4), (2, 5), (5, 2), (1, 6), (6, 1)])
    else:
        coef = lax.psum(coef, "rad") * (1.0 / cores)
        rest = jnp.zeros_like(coef)

    smoothed = pl.pallas_call(
        sweep_kernel,
        out_shape=whole,
        in_specs=[VMEM] * 8,
        out_specs=HBM,
        scratch_shapes=[
            pltpu.VMEM((3, layers + 2, rows, width), f32),
            pltpu.VMEM((2 * layers, 3, SUB, width), f32),
            pltpu.VMEM((3, layers, rows, width), f32),
            pltpu.VMEM((layers + 2, COEFS, LANES), f32),
            pltpu.SemaphoreType.DMA((layers,)),
        ],
        compiler_params=pltpu.CompilerParams(vmem_limit_bytes=VMEM_LIMIT),
        name="sweeps",
    )(u, f, swept, beside1, beside2, ring, got, every)
    coef, smoothed = lax.optimization_barrier((coef, smoothed))

    potential = pl.pallas_call(
        functools.partial(synthesis_kernel, 2.0 / cycles),
        out_shape=jax.ShapeDtypeStruct((2, rows, width), f32),
        in_specs=[VMEM] * 5,
        out_specs=VMEM,
        scratch_shapes=[pltpu.VMEM((2 * groups, SUB, LANES), f32)],
        compiler_params=pltpu.CompilerParams(vmem_limit_bytes=VMEM_LIMIT),
        name="synthesis",
    )(coef, rest, gains, cycle_id, table)
    return smoothed, potential


def solution(mesh):
    in_specs = (
        P(None, "rad", "lat", None),
        P(None, "rad", "lat", None),
        P("rad"),
        P(),
        P(),
        P("lat", None),
        P(),
        P(),
    )
    out_specs = (P(None, "rad", "lat", None), P(None, "lat", None))
    return jax.shard_map(local, mesh=mesh, in_specs=in_specs, out_specs=out_specs, check_vma=False)
```

```python
import functools
import math

import jax
import jax.numpy as jnp
import numpy as np
from jax import lax
from jax.experimental import pallas as pl
from jax.experimental.pallas import tpu as pltpu
from jax.sharding import PartitionSpec as P

SWEEPS = 2
OMEGA = 0.8
LEAST_COUNT = 32
LANES = 128
SUB = 8
PAD = 8
COEFS = 16
BATCH = 5
VMEM_LIMIT = 16 * 1024 * 1024

VMEM = pl.BlockSpec(memory_space=pltpu.VMEM)
SMEM = pl.BlockSpec(memory_space=pltpu.SMEM)
HBM = pl.BlockSpec(memory_space=pltpu.HBM)
ANY = pl.BlockSpec(memory_space=pl.ANY)


def basis_table(degrees, cycles):
    groups = degrees // SUB
    degree = np.arange(degrees, dtype=np.int64)[:, None]
    cycle = np.arange(cycles, dtype=np.int64)[None, :]
    phase = degree * (2 * cycle + 1) % (4 * cycles)
    table = np.cos(np.pi * phase / (2.0 * cycles)).astype(np.float32)
    table = table.reshape(SUB, groups, cycles // LANES, LANES).transpose(2, 1, 0, 3)
    return np.ascontiguousarray(table.reshape(cycles // LANES, degrees, LANES))


def iota(shape, dim):
    return lax.broadcasted_iota(jnp.int32, shape, dim)


def lane_gather(values, index):
    return jnp.take_along_axis(values, index, axis=1, mode="promise_in_bounds")


def layer_scalars(layer, lid, stiff, coup):
    material = lid[layer]
    mu = stiff[material]
    return mu, [[coup[c, d, material] for d in range(3)] for c in range(3)]


def coefficient_rows(mu, k, width=LANES):
    row = iota((COEFS, width), 0)
    top = jnp.zeros((COEFS, width), jnp.float32)
    below = jnp.ones((COEFS, width), jnp.float32)
    for c in range(3):
        diag = 6.0 * mu + k[c][c]
        others = [d for d in range(3) if d != c]
        entries = [(c, 1.0), (3 + c, mu), (6 + 2 * c, k[c][others[0]]), (7 + 2 * c, k[c][others[1]])]
        for at, value in entries:
            top = jnp.where(row == at, OMEGA * value, top)
            below = jnp.where(row == at, diag, below)
    return top / below


def roll_rows(value, before, after):
    sub = iota(value.shape, 0)
    up = jnp.where(sub == 0, jnp.broadcast_to(before, value.shape), pltpu.roll(value, 1, 0))
    down = jnp.where(sub == SUB - 1, jnp.broadcast_to(after, value.shape), pltpu.roll(value, SUB - 1, 0))
    return up + down


def roll_columns(values):
    lane = iota(values[0].shape, 1)
    right = [pltpu.roll(value, 1, 1) for value in values]
    left = [pltpu.roll(value, LANES - 1, 1) for value in values]
    last = len(values) - 1
    return [
        jnp.where(lane == 0, right[j - 1] if j > 0 else 0.0, right[j])
        + jnp.where(lane == LANES - 1, left[j + 1] if j < last else 0.0, left[j])
        for j in range(len(values))
    ]


def relax(c, centers, neighbours, force, rows):
    d0, d1 = [d for d in range(3) if d != c]
    value = rows[c] * force + rows[3 + c] * neighbours
    value = value - (rows[6 + 2 * c] * centers[d0] + rows[7 + 2 * c] * centers[d1])
    return value + (1.0 - OMEGA) * centers[c]


def chunk(j):
    return pl.ds(LANES * j, LANES)


def spans(per_row, ref, *index):
    return [ref[index + (chunk(j),)] for j in range(per_row)]


def lane_scan(values, steps):
    lane = iota(values.shape, 1)
    step = 1
    while step < steps:
        values = values + jnp.where(lane >= step, pltpu.roll(values, step, 1), 0)
        step *= 2
    return values


def local_sweep(u, f, every, layer, lower, upper, result, at_layer):
    rows, width = u.shape[2:]
    per_row, total = width // LANES, rows // SUB
    coef = [jnp.broadcast_to(every[layer, j:j + 1, :], (SUB, LANES)) for j in range(12)]
    none = jnp.zeros((1, LANES), jnp.float32)
    for g in range(total):
        here = slice(SUB * g, SUB * g + SUB)
        values = [spans(per_row, u, c, layer, here) for c in range(3)]
        for c in range(3):
            aside = roll_columns(values[c])
            for j in range(per_row):
                at = (c, layer)
                above = u[at + (slice(SUB * g - 1, SUB * g), chunk(j))] if g > 0 else none
                under = u[at + (slice(SUB * g + SUB, SUB * g + SUB + 1), chunk(j))] if g < total - 1 else none
                near = roll_rows(values[c][j], above, under) + aside[j]
                if lower is not None:
                    near = near + u[c, lower, here, chunk(j)]
                if upper is not None:
                    near = near + u[c, upper, here, chunk(j)]
                value = relax(c, [values[d][j] for d in range(3)], near, f[c, layer, here, chunk(j)], coef)
                result[c, at_layer, here, chunk(j)] = value


def faces_kernel(
    disp, forc, lid, stiff, coup, ids, cnt,
    u, f, outer_s, face1, face2, send, every, cyc, num,
    lids, stiffs, coups, small_sem, near_sem, u_sem, f_sem, face_sem,
):
    layers = disp.shape[1]
    top = layers - 1
    odd = lax.rem(lax.axis_index("rad"), 2) == 1
    small = [
        pltpu.make_async_copy(lid, lids, small_sem.at[0]),
        pltpu.make_async_copy(stiff, stiffs, small_sem.at[1]),
        pltpu.make_async_copy(coup, coups, small_sem.at[2]),
    ]
    cycles = [
        pltpu.make_async_copy(cnt, num, near_sem.at[0]),
        pltpu.make_async_copy(ids, cyc, near_sem.at[1]),
    ]
    loads_u = [pltpu.make_async_copy(disp.at[:, r], u.at[:, r], u_sem.at[r]) for r in range(layers)]
    loads_f = [pltpu.make_async_copy(forc.at[:, r], f.at[:, r], f_sem.at[r]) for r in range(layers)]
    for copy in small:
        copy.start()
    for r in [0, 1, top] + list(range(top - 1, 1, -1)):
        loads_u[r].start()
        if r in (0, top):
            loads_f[r].start()
    for r in range(1, top):
        loads_f[r].start()
    for copy in cycles:
        copy.start()
    for copy in small:
        copy.wait()
    for r in range(layers):
        every[r] = coefficient_rows(*layer_scalars(r, lids, stiffs, coups))
    send[...] = every[jnp.where(odd, top, 0)]

    loads_u[0].wait()
    loads_f[0].wait()
    loads_u[1].wait()
    local_sweep(u, f, every, 0, None, 1, outer_s, 0)
    for r in range(2, layers):
        loads_u[r].wait()
    loads_f[top].wait()
    faces = []
    for n, (face, high) in enumerate(((face1, jnp.logical_not(odd)), (face2, odd))):
        source = jnp.where(high, top, 0)
        swept = jnp.where(high, 1, 0)
        faces.append(pltpu.make_async_copy(u.at[:, source], face.at[0], face_sem.at[2 * n]))
        faces.append(pltpu.make_async_copy(outer_s.at[:, swept], face.at[1], face_sem.at[2 * n + 1]))
    faces[0].start()
    faces[2].start()
    local_sweep(u, f, every, top, top - 1, None, outer_s, 1)
    faces[1].start()
    faces[3].start()
    for copy in loads_f[1:top] + cycles + faces:
        copy.wait()


def analysis_kernel(
    u, f, outer_s, every, cyc, num, ids, grav, tbl,
    inner_s, pay, gains,
    tab, mat, windows, gain_in, first_ids, last_ids, near_sem, tab_sem,
):
    layers, rows, width = u.shape[1:]
    chunks = num.shape[0]
    groups = tbl.shape[1] // SUB
    per_row = width // LANES
    lat, lats = lax.axis_index("lat"), lax.axis_size("lat")
    rad, rads = lax.axis_index("rad"), lax.axis_size("rad")
    bottom = rad == 0
    at_end = jnp.logical_or(bottom, rad == rads - 1)
    top = layers - 1
    edge, inner = jnp.where(bottom, 0, top), jnp.where(bottom, 1, top - 1)
    edge_s, inner_at = jnp.where(bottom, 0, 1), jnp.where(bottom, 0, top - 2)
    total = rows // SUB
    at_core = every[jnp.where(lax.rem(rad, 2) == 1, 0, top)]
    cycles = [
        pltpu.make_async_copy(ids.at[pl.ds(0, SUB), pl.ds(0, LANES)], first_ids, near_sem.at[0]),
        pltpu.make_async_copy(
            ids.at[pl.ds(rows - SUB, SUB), pl.ds(width - LANES, LANES)], last_ids, near_sem.at[1]
        ),
        pltpu.make_async_copy(grav, gain_in, near_sem.at[2]),
    ]
    for copy in cycles:
        copy.start()

    def middle(r, carry):
        local_sweep(u, f, every, r, r - 1, r + 1, inner_s, r - 1)
        return carry

    lax.fori_loop(1, top, middle, 0)

    sub8, lane8 = iota((SUB, LANES), 0), iota((SUB, LANES), 1)
    before = sub8 < 2
    zero = jnp.zeros((SUB, LANES), jnp.float32)
    reach = 2 * width // LEAST_COUNT + 2
    for copy in cycles:
        copy.wait()
    first, last = first_ids[0, 0], last_ids[SUB - 1, LANES - 1]
    low_part = jnp.right_shift(jnp.maximum(first - reach, 0), 7)
    high_part = jnp.minimum(jnp.right_shift(last + reach, 7), chunks - 1)
    pay[0:SUB, 0:LANES] = jnp.zeros((SUB, LANES), jnp.float32)
    pay[0:SUB, LANES:2 * LANES] = at_core[0:SUB]
    pay[0:SUB, 2 * LANES:3 * LANES] = at_core[SUB:]

    lane1 = iota((1, LANES), 1)
    for load in range(2):
        for m in range(groups * SUB // LANES):
            one, two = gain_in[0, load:load + 1, chunk(m)], gain_in[1, load:load + 1, chunk(m)]
            gains[load, 2 * m:2 * m + 1, :] = jnp.where(lane1 < groups, one, pltpu.roll(two, groups, 1))
            gains[load, 2 * m + 1:2 * m + 2, :] = jnp.where(lane1 < groups, pltpu.roll(one, groups, 1), two)

    def table(b):
        return [
            pltpu.make_async_copy(tbl.at[jnp.minimum(low_part + b * BATCH + i, chunks - 1)], tab.at[i], tab_sem.at[i])
            for i in range(BATCH)
        ]

    @pl.when(at_end)
    def _():
        for copy in table(0):
            copy.start()

        own_first = jnp.zeros((SUB, LANES), jnp.int32)
        own_last = own_first
        for j in range(per_row):
            own_first = own_first + jnp.where(cyc[0:SUB, LANES * j:LANES * j + LANES] == first, 1, 0)
            own_last = own_last + jnp.where(cyc[rows - SUB:rows, LANES * j:LANES * j + LANES] == last, 1, 0)

        def total_of(count):
            count = jnp.sum(count.astype(jnp.float32), axis=1, keepdims=True)
            return jnp.broadcast_to(jnp.sum(count, axis=0, keepdims=True), (SUB, LANES)).astype(jnp.int32)

        held_here = jnp.where(before, total_of(own_first), total_of(own_last))
        index = jnp.where(before, first - lane8, last + lane8)
        place, part = jnp.bitwise_and(index, LANES - 1), jnp.right_shift(index, 7)
        lengths = jnp.full((SUB, LANES), 2 ** 20, jnp.int32)
        part_first, part_last = jnp.right_shift(first, 7), jnp.right_shift(last, 7)
        for q in (part_first - 1, part_first, part_last, part_last + 1):
            row = num[pl.ds(jnp.clip(q, 0, chunks - 1), 1), :]
            known = jnp.logical_and(part == q, jnp.logical_and(part >= 0, part < chunks))
            lengths = jnp.where(known, lane_gather(jnp.broadcast_to(row, (SUB, LANES)), place), lengths)
        lengths = lengths - jnp.where(lane8 == 0, held_here, 0)
        limits = lane_scan(lengths, reach)
        caps = [jnp.broadcast_to(limits[:, i:i + 1], (SUB, LANES)) for i in range(reach)]
        spill_ids = []
        for j in range(per_row):
            column = LANES * j + lane8
            away = jnp.where(before, (width - 1 - column) + jnp.where(sub8 == 0, width, 0),
                             column + jnp.where(sub8 == 3, width, 0))
            passed = jnp.zeros((SUB, LANES), jnp.int32)
            for i in range(reach):
                passed = passed + jnp.where(away >= caps[i], 1, 0)
            spill_ids.append(jnp.where(sub8 < 4, jnp.where(before, first - passed, last + passed), 0))

        mat[0] = every[edge]
        mat[1] = every[inner]
        outer = [jnp.broadcast_to(mat[0, j:j + 1, :], (SUB, LANES)) for j in range(12)]
        below = [jnp.broadcast_to(mat[1, j:j + 1, :], (SUB, LANES)) for j in range(12)]

        def rows_of(g):
            return slice(SUB * g, SUB * g + SUB)

        def lateral(ref, g, index, ends):
            values = spans(per_row, ref, *index, rows_of(g))
            aside = roll_columns(values)
            out = []
            for j in range(per_row):
                above = ref[index + (slice(SUB * g - 1, SUB * g), chunk(j))] if g > 0 else ends[0][j]
                under = ref[index + (slice(SUB * g + SUB, SUB * g + SUB + 1), chunk(j))] if g < total - 1 else ends[1][j]
                out.append(roll_rows(values[j], above, under) + aside[j])
            return out

        low_in = jnp.where(lat > 0, 1.0, 0.0)
        high_in = jnp.where(lat < lats - 1, 1.0, 0.0)
        weight = jnp.where(sub8 == 1, low_in, jnp.where(sub8 == 2, high_in, 0.0))

        def ends_of(ref, index, j):
            low = jnp.broadcast_to(ref[index + (slice(0, 1), chunk(j))], (SUB, LANES))
            high = jnp.broadcast_to(ref[index + (slice(rows - 1, rows), chunk(j))], (SUB, LANES))
            return jnp.where(sub8 == 1, low, jnp.where(sub8 == 2, high, 0.0))

        over = [[outer[3 + c] * ends_of(u, (c, edge), j) * weight for j in range(per_row)] for c in range(3)]
        over_inner = [below[3] * ends_of(u, (0, inner), j) * weight for j in range(per_row)]
        aside = roll_columns(over[0])
        spill = []
        for j in range(per_row):
            shifted = jnp.where(sub8 == 0, pltpu.roll(over[0][j], SUB - 1, 0),
                                jnp.where(sub8 == 3, pltpu.roll(over[0][j], 1, 0), 0.0))
            near = over_inner[j] + aside[j] + shifted + ends_of(outer_s, (0, edge_s), j)
            value = relax(0, [over[c][j] for c in range(3)], near, zero, outer)
            spill.append(value * jnp.where(before, low_in, high_in))
        ends = [[over[0][j][1:2, :] for j in range(per_row)], [over[0][j][2:3, :] for j in range(per_row)]]

        met = (width - 2) // LEAST_COUNT + 2

        def window_of(values, cycles):
            start = jnp.broadcast_to(cycles[0][:, 0:1], (SUB, LANES))
            offsets = [cycle - start for cycle in cycles]
            window = zero
            for t in range(met):
                picked = [jnp.where(offset == t, value, 0.0) for offset, value in zip(offsets, values)]
                sum_t = jnp.sum(functools.reduce(jnp.add, picked), axis=1, keepdims=True)
                window = jnp.where(lane8 == t, jnp.broadcast_to(sum_t, (SUB, LANES)), window)
            return window, start

        windowed = [window_of(spill, spill_ids)]
        for g in range(total):
            here = rows_of(g)
            centers = [spans(per_row, outer_s, c, edge_s, here) for c in range(3)]
            near = lateral(outer_s, g, (0, edge_s), ends)
            inners = spans(per_row, inner_s, 0, inner_at, here)
            force = spans(per_row, f, 0, edge, here)
            values = [
                relax(0, [center[j] for center in centers], near[j] + inners[j], force[j], outer)
                for j in range(per_row)
            ]
            windowed.append(window_of(values, spans(per_row, cyc, here)))
        for i, (window, start) in enumerate(windowed):
            windows[0, i] = window
            windows[1, i] = start.astype(jnp.float32)

        half = jnp.where(bottom, groups, 0)

        def batch(b, result):
            @pl.when(b > 0)
            def _():
                for copy in table(b):
                    copy.start()

            means = []
            for i in range(BATCH):
                q = low_part + b * BATCH + i
                part = jnp.minimum(q, chunks - 1)
                acc = zero
                for w in range(total + 1):
                    at = q * LANES + lane8 - windows[1, w].astype(jnp.int32)
                    got = lane_gather(windows[0, w], jnp.bitwise_and(at, LANES - 1))
                    acc = acc + jnp.where(jnp.right_shift(at, 7) == 0, got, 0.0)
                mean = jnp.sum(acc, axis=0, keepdims=True) / num[pl.ds(part, 1), :].astype(jnp.float32)
                mean = jnp.where(q < chunks, mean, 0.0)
                means.append(jnp.broadcast_to(mean, (SUB, LANES)))
            for copy in table(b):
                copy.wait()
            for g in range(groups):
                acc = tab[0, SUB * g:SUB * g + SUB, :] * means[0]
                for i in range(1, BATCH):
                    acc = acc + tab[i, SUB * g:SUB * g + SUB, :] * means[i]
                column = jnp.broadcast_to(jnp.sum(acc, axis=1, keepdims=True), (SUB, LANES))
                result = jnp.where(lane8 == g + half, result + column, result)
            return result

        pay[0:SUB, 0:LANES] = lax.fori_loop(0, (high_part - low_part) // BATCH + 1, batch, zero)

    tall = 3 * layers

    def pack(ref, base, near):
        for c in range(3):
            for r in range(layers):
                at = base + c * layers + r
                ref[at:at + 1, :] = u[c, r, near:near + 1, :]
                source, layer = (outer_s, r // top) if r in (0, top) else (inner_s, r - 1)
                ref[at + tall:at + tall + 1, :] = source[c, layer, near:near + 1, :]

    pack(pay, SUB, 0)
    pack(pay, SUB + 2 * tall, rows - 1)


def relay_kernel(ring, send, out):
    cores = 2
    lat, lats = lax.axis_index("lat"), lax.axis_size("lat")
    core = lax.rem(lax.axis_index("rad"), cores)
    members, _, width = ring.shape
    tall = (ring.shape[1] - SUB) // 4
    layers = tall // 3
    coef = ring[0, 0:SUB, 0:LANES]
    for i in range(1, members):
        coef = coef + ring[i, 0:SUB, 0:LANES]
    out[0:SUB, :] = coef
    out[SUB:SUB + COEFS, :] = send[...]
    before, after = cores * jnp.maximum(lat - 1, 0) + core, cores * jnp.minimum(lat + 1, lats - 1) + core
    low_in, high_in = lat > 0, lat < lats - 1
    for j in range(width // LANES):
        base = SUB + COEFS + SUB * j
        out[base:base + SUB, :] = jnp.zeros((SUB, LANES), jnp.float32)
        for c in range(3):
            for at, member, valid, start in ((c, before, low_in, 2 * tall), (3 + c, after, high_in, 0)):
                row = SUB + start + c * layers
                bottom, top = ring[member, row:row + 1, chunk(j)], ring[member, row + layers - 1:row + layers, chunk(j)]
                out[base + at:base + at + 1, :] = jnp.where(valid, jnp.where(core == 1, top, bottom), 0.0)


def sweep_kernel(
    u, f, outer_s, inner_s, face1, face2, ring, got, every,
    out,
    s, rim, done, cf, out_sem,
):
    layers, rows, width = u.shape[1:]
    per_row = width // LANES
    total = rows // SUB
    tall = 3 * layers
    top = layers - 1
    lat, lats = lax.axis_index("lat"), lax.axis_size("lat")
    rad, rads = lax.axis_index("rad"), lax.axis_size("rad")
    rad_odd = lax.rem(rad, 2) == 1
    cores = 2
    core = lax.rem(rad, cores)
    lower, upper = cores * jnp.maximum(lat - 1, 0), cores * jnp.minimum(lat + 1, lats - 1)
    low_in, high_in = lat > 0, lat < lats - 1
    sub8 = iota((SUB, LANES), 0)

    def side_rows(base, j):
        at = SUB + base
        low = ring[lower + core, at + 2 * tall:at + 2 * tall + layers, chunk(j)]
        high = ring[upper + core, at:at + layers, chunk(j)]
        low, high = jnp.where(low_in, low, 0.0), jnp.where(high_in, high, 0.0)
        return jnp.concatenate([low, high], axis=0)

    mate = 1 - core
    own_chip = jnp.concatenate(
        [ring[cores * lat + mate, 0:SUB, LANES:2 * LANES], ring[cores * lat + mate, 0:SUB, 2 * LANES:3 * LANES]], axis=0
    )
    other_chip = got[SUB:SUB + COEFS, :]
    lowest, highest = rad == 0, rad == rads - 1
    cf[0] = jnp.where(rad_odd, own_chip, jnp.where(lowest, 0.0, other_chip))
    cf[layers + 1] = jnp.where(rad_odd, jnp.where(highest, 0.0, other_chip), own_chip)
    for r in range(layers):
        cf[1 + r] = every[r]
    corner_low, corner_high = [], []
    for j in range(per_row):
        base = SUB + COEFS + SUB * j
        other = got[base:base + SUB, :]
        rows_own = []
        for member, valid, start in ((lower + mate, low_in, 2 * tall), (upper + mate, high_in, 0)):
            for c in range(3):
                row = SUB + start + c * layers
                near_end, far_end = ring[member, row:row + 1, chunk(j)], ring[member, row + top:row + top + 1, chunk(j)]
                rows_own.append(jnp.where(valid, jnp.where(rad_odd, far_end, near_end), 0.0))
        rows_own.append(jnp.zeros((SUB - 6, LANES), jnp.float32))
        own = jnp.concatenate(rows_own, axis=0)
        corner_low.append(jnp.where(rad_odd, own, jnp.where(lowest, 0.0, other)))
        corner_high.append(jnp.where(rad_odd, jnp.where(highest, 0.0, other), own))

    def coefficients(layer):
        return [jnp.broadcast_to(cf[layer, j:j + 1, :], (SUB, LANES)) for j in range(12)]

    near_rows = [[side_rows(c * layers, j) for j in range(per_row)] for c in range(3)]
    keep = jnp.where(sub8 < layers, jnp.where(low_in, 1.0, 0.0), jnp.where(high_in, 1.0, 0.0))
    for c in range(3):
        gain = jnp.zeros((SUB, LANES), jnp.float32)
        for r in range(layers):
            here = jnp.broadcast_to(cf[1 + r, 3 + c:4 + c, :], (SUB, LANES))
            gain = jnp.where(jnp.logical_or(sub8 == r, sub8 == layers + r), here, gain)
        for j in range(per_row):
            near = jnp.zeros((SUB, LANES), jnp.float32)
            for r in range(layers):
                head = jnp.broadcast_to(u[c, r, 0:1, chunk(j)], near.shape)
                tail = jnp.broadcast_to(u[c, r, rows - 1:rows, chunk(j)], near.shape)
                near = jnp.where(sub8 == r, head, jnp.where(sub8 == layers + r, tail, near))
            ends = (
                (0, corner_low[j][c:c + 1, :]), (layers, corner_low[j][3 + c:4 + c, :]),
                (layers - 1, corner_high[j][c:c + 1, :]), (SUB - 1, corner_high[j][3 + c:4 + c, :]),
            )
            for row, corner in ends:
                near = near + jnp.where(sub8 == row, jnp.broadcast_to(corner, near.shape), 0.0)
            value = (side_rows(tall + c * layers, j) + gain * near) * keep
            for i in range(2 * layers):
                rim[i, c, :, chunk(j)] = jnp.broadcast_to(value[i:i + 1, :], (SUB, LANES))

    def beyond(layer, side, c, j):
        if layer == 0:
            return corner_low[j][3 * side + c:3 * side + c + 1, :]
        if layer == layers + 1:
            return corner_high[j][3 * side + c:3 * side + c + 1, :]
        at = layers * side + layer - 1
        return near_rows[c][j][at:at + 1, :]

    def lo(index):
        return jnp.where(rad_odd, face1[index], face2[index])

    def hi(index):
        return jnp.where(rad_odd, face2[index], face1[index])

    for layer in range(layers + 2):
        for c in range(3):
            gain = jnp.broadcast_to(cf[layer, 3 + c:4 + c, :], (SUB, LANES))
            for j in range(per_row):
                for g in range(total):
                    at = (slice(SUB * g, SUB * g + SUB), chunk(j))
                    if layer == 0:
                        value = lo((1, c) + at) + gain * u[(c, 0) + at]
                    elif layer == layers + 1:
                        value = hi((1, c) + at) + gain * u[(c, top) + at]
                    elif layer in (1, layers):
                        value = outer_s[(c, layer // layers) + at]
                    else:
                        value = inner_s[(c, layer - 2) + at]
                    if layer == 1:
                        value = value + gain * lo((0, c) + at)
                    if layer == layers:
                        value = value + gain * hi((0, c) + at)
                    if g == 0:
                        row = jnp.broadcast_to(beyond(layer, 0, c, j), value.shape)
                        value = value + jnp.where(sub8 == 0, gain * row, 0.0)
                    if g == total - 1:
                        row = jnp.broadcast_to(beyond(layer, 1, c, j), value.shape)
                        value = value + jnp.where(sub8 == SUB - 1, gain * row, 0.0)
                    s[(c, layer) + at] = value

    stores = [pltpu.make_async_copy(done.at[:, r], out.at[:, r], out_sem.at[r]) for r in range(layers)]
    for r in range(layers):
        layer = r + 1
        coef = coefficients(layer)
        for g in range(total):
            here = slice(SUB * g, SUB * g + SUB)
            values = [spans(per_row, s, c, layer, here) for c in range(3)]
            for c in range(3):
                aside = roll_columns(values[c])
                for j in range(per_row):
                    at = (c, layer)
                    if g > 0:
                        above_row = s[at + (slice(SUB * g - 1, SUB * g), chunk(j))]
                    else:
                        above_row = rim[r, c, :, chunk(j)]
                    if g < total - 1:
                        under_row = s[at + (slice(SUB * g + SUB, SUB * g + SUB + 1), chunk(j))]
                    else:
                        under_row = rim[layers + r, c, :, chunk(j)]
                    near = roll_rows(values[c][j], above_row, under_row) + aside[j]
                    near = near + (s[c, layer - 1, here, chunk(j)] + s[c, layer + 1, here, chunk(j)])
                    done[c, r, here, chunk(j)] = relax(
                        c, [values[d][j] for d in range(3)], near, f[c, r, here, chunk(j)], coef
                    )
        stores[r].start()
    for copy in stores:
        copy.wait()


def synthesis_kernel(scale, coef, rest, gains, ids, tab, out, factors):
    rows, width = ids.shape
    chunks = tab.shape[0]
    groups = tab.shape[1] // SUB
    per_row = width // LANES
    lane8 = iota((SUB, LANES), 1)
    here = coef[...] + rest[...]
    other = pltpu.roll(here, groups, 1)
    left = lane8 < groups
    surface = jnp.where(left, here, other)
    core = jnp.where(left, other, here)
    modes = (gains[0] * surface + gains[1] * core) * scale
    zero = jnp.zeros((SUB, LANES), jnp.float32)
    for i in range(2 * groups):
        factors[i] = jnp.broadcast_to(modes[:, i:i + 1], (SUB, LANES))
    low_part = jnp.right_shift(jnp.min(ids[0:1, 0:LANES]), 7)
    high_part = jnp.right_shift(jnp.max(ids[rows - 1:rows, width - LANES:width]), 7)

    def batch(b, carry):
        parts = [low_part + b * BATCH + i for i in range(BATCH)]
        blocks = [jnp.minimum(part, chunks - 1) for part in parts]
        sums = [[zero] * BATCH for _ in range(2)]
        for g in range(groups):
            for i in range(BATCH):
                block = tab[blocks[i], SUB * g:SUB * g + SUB, :]
                for k in range(2):
                    sums[k][i] = sums[k][i] + factors[k * groups + g] * block
        for k in range(2):
            for i in range(BATCH):
                sums[k][i] = jnp.broadcast_to(jnp.sum(sums[k][i], axis=0, keepdims=True), (SUB, LANES))
        for a in range(rows // SUB):
            for j in range(per_row):
                spot = (slice(SUB * a, SUB * a + SUB), chunk(j))
                cycle = ids[spot]
                place, part = jnp.bitwise_and(cycle, LANES - 1), jnp.right_shift(cycle, 7)
                values = [jnp.where(b == 0, 0.0, out[(k,) + spot]) for k in range(2)]
                for i in range(BATCH):
                    chosen = part == parts[i]
                    for k in range(2):
                        values[k] = jnp.where(chosen, lane_gather(sums[k][i], place), values[k])
                for k in range(2):
                    out[(k,) + spot] = values[k]
        return carry

    lax.fori_loop(0, (high_part - low_part) // BATCH + 1, batch, 0)


def even_pairs(count):
    return [(i, i ^ 1) for i in range(count)]


def odd_pairs(count):
    pairs = []
    for i in range(1, count, 2):
        j = (i + 1) % count
        pairs += [(i, j), (j, i)]
    return pairs


def local(displacement, forcing, layer_id, stiffness, coupling, cycle_id, cycle_count, gravity):
    _, layers, rows, width = displacement.shape
    cycles, degrees = cycle_count.shape[0], gravity.shape[2]
    chunks, groups = cycles // LANES, degrees // SUB
    lats, rads, cores = lax.axis_size("lat"), lax.axis_size("rad"), 2
    if 2 * groups != LANES or 2 * layers != SUB or rads % cores or width < 3 * LANES:
        raise ValueError("unsupported sizes")
    f32 = jnp.float32
    table = jnp.asarray(basis_table(degrees, cycles))
    per_row = width // LANES
    tall = 3 * layers
    face = jax.ShapeDtypeStruct((2, 3, rows, width), f32)

    whole = jax.ShapeDtypeStruct(displacement.shape, f32)
    pinned = [
        pltpu.with_memory_space_constraint(value, pltpu.HBM)
        for value in (
            displacement, forcing, layer_id, stiffness, jnp.transpose(coupling, (1, 2, 0)), cycle_id,
            cycle_count.reshape(chunks, LANES), gravity, table,
        )
    ]
    u, f, outer_s, face1, face2, mine, every, cyc, num = pl.pallas_call(
        faces_kernel,
        out_shape=(
            whole, whole,
            jax.ShapeDtypeStruct((3, 2, rows, width), f32),
            face, face,
            jax.ShapeDtypeStruct((COEFS, LANES), f32),
            jax.ShapeDtypeStruct((layers, COEFS, LANES), f32),
            jax.ShapeDtypeStruct(cycle_id.shape, jnp.int32),
            jax.ShapeDtypeStruct((chunks, LANES), jnp.int32),
        ),
        in_specs=[HBM] * 7,
        out_specs=(VMEM,) * 9,
        scratch_shapes=[
            pltpu.SMEM(layer_id.shape, jnp.int32),
            pltpu.SMEM(stiffness.shape, f32),
            pltpu.SMEM(coupling.shape[1:] + coupling.shape[:1], f32),
            pltpu.SemaphoreType.DMA((3,)),
            pltpu.SemaphoreType.DMA((2,)),
            pltpu.SemaphoreType.DMA((layers,)),
            pltpu.SemaphoreType.DMA((layers,)),
            pltpu.SemaphoreType.DMA((4,)),
        ],
        compiler_params=pltpu.CompilerParams(vmem_limit_bytes=VMEM_LIMIT),
        name="faces",
    )(*pinned[:7])

    beside2 = lax.ppermute(face2, "rad", odd_pairs(rads)[:-2])
    beside1 = lax.ppermute(face1, "rad", even_pairs(rads))

    inner_s, pay, gains = pl.pallas_call(
        analysis_kernel,
        out_shape=(
            jax.ShapeDtypeStruct((3, layers - 2, rows, width), f32),
            jax.ShapeDtypeStruct((SUB + 4 * tall, width), f32),
            jax.ShapeDtypeStruct((2, SUB, LANES), f32),
        ),
        in_specs=[VMEM] * 6 + [HBM] * 3,
        out_specs=(VMEM,) * 3,
        scratch_shapes=[
            pltpu.VMEM((BATCH, degrees, LANES), f32),
            pltpu.VMEM((2, COEFS, LANES), f32),
            pltpu.VMEM((2, rows // SUB + 1, SUB, LANES), f32),
            pltpu.VMEM(gravity.shape, f32),
            pltpu.SMEM((SUB, LANES), jnp.int32),
            pltpu.SMEM((SUB, LANES), jnp.int32),
            pltpu.SemaphoreType.DMA((3,)),
            pltpu.SemaphoreType.DMA((BATCH,)),
        ],
        compiler_params=pltpu.CompilerParams(vmem_limit_bytes=VMEM_LIMIT),
        name="analysis",
    )(u, f, outer_s, every, cyc, num, pinned[5], *pinned[7:])

    chips = [[a * rads + b + c for a in range(lats) for c in range(cores)] for b in range(0, rads, cores)]
    ring = lax.all_gather(pay, ("lat", "rad"), axis_index_groups=chips)
    outward = pl.pallas_call(
        relay_kernel,
        out_shape=jax.ShapeDtypeStruct((SUB + COEFS + SUB * per_row, LANES), f32),
        in_specs=[VMEM] * 2,
        out_specs=VMEM,
        compiler_params=pltpu.CompilerParams(vmem_limit_bytes=VMEM_LIMIT),
        name="relay",
    )(ring, mine)
    outward, beside1, beside2 = lax.optimization_barrier((outward, beside1, beside2))
    got = lax.ppermute(outward, "rad", odd_pairs(rads))
    coef = outward[:SUB]
    if rads == 8:
        coef = coef + got[:SUB]
        rest = lax.ppermute(coef, "rad", [(0, 3), (3, 0), (7, 4), (4, 7), (2, 5), (5, 2), (1, 6), (6, 1)])
    else:
        coef = lax.psum(coef, "rad") * (1.0 / cores)
        rest = jnp.zeros_like(coef)

    smoothed = pl.pallas_call(
        sweep_kernel,
        out_shape=whole,
        in_specs=[VMEM] * 9,
        out_specs=HBM,
        scratch_shapes=[
            pltpu.VMEM((3, layers + 2, rows, width), f32),
            pltpu.VMEM((2 * layers, 3, SUB, width), f32),
            pltpu.VMEM((3, layers, rows, width), f32),
            pltpu.VMEM((layers + 2, COEFS, LANES), f32),
            pltpu.SemaphoreType.DMA((layers,)),
        ],
        compiler_params=pltpu.CompilerParams(vmem_limit_bytes=VMEM_LIMIT),
        name="sweeps",
    )(u, f, outer_s, inner_s, beside1, beside2, ring, got, every)
    coef, smoothed = lax.optimization_barrier((coef, smoothed))

    potential = pl.pallas_call(
        functools.partial(synthesis_kernel, 2.0 / cycles),
        out_shape=jax.ShapeDtypeStruct((2, rows, width), f32),
        in_specs=[VMEM] * 5,
        out_specs=VMEM,
        scratch_shapes=[pltpu.VMEM((2 * groups, SUB, LANES), f32)],
        compiler_params=pltpu.CompilerParams(vmem_limit_bytes=VMEM_LIMIT),
        name="synthesis",
    )(coef, rest, gains, cyc, table)
    return smoothed, potential


def solution(mesh):
    in_specs = (
        P(None, "rad", "lat", None),
        P(None, "rad", "lat", None),
        P("rad"),
        P(),
        P(),
        P("lat", None),
        P(),
        P(),
    )
    out_specs = (P(None, "rad", "lat", None), P(None, "lat", None))
    return jax.shard_map(local, mesh=mesh, in_specs=in_specs, out_specs=out_specs, check_vma=False)
```

```python
import functools
import math

import jax
import jax.numpy as jnp
import numpy as np
from jax import lax
from jax.experimental import pallas as pl
from jax.experimental.pallas import tpu as pltpu
from jax.sharding import PartitionSpec as P

SWEEPS = 2
OMEGA = 0.8
LEAST_COUNT = 32
LANES = 128
SUB = 8
PAD = 8
COEFS = 16
BATCH = 5
VMEM_LIMIT = 16 * 1024 * 1024

VMEM = pl.BlockSpec(memory_space=pltpu.VMEM)
SMEM = pl.BlockSpec(memory_space=pltpu.SMEM)
HBM = pl.BlockSpec(memory_space=pltpu.HBM)
ANY = pl.BlockSpec(memory_space=pl.ANY)


def basis_table(degrees, cycles):
    groups = degrees // SUB
    degree = np.arange(degrees, dtype=np.int64)[:, None]
    cycle = np.arange(cycles, dtype=np.int64)[None, :]
    phase = degree * (2 * cycle + 1) % (4 * cycles)
    table = np.cos(np.pi * phase / (2.0 * cycles)).astype(np.float32)
    table = table.reshape(SUB, groups, cycles // LANES, LANES).transpose(2, 1, 0, 3)
    return np.ascontiguousarray(table.reshape(cycles // LANES, degrees, LANES))


def iota(shape, dim):
    return lax.broadcasted_iota(jnp.int32, shape, dim)


def lane_gather(values, index):
    return jnp.take_along_axis(values, index, axis=1, mode="promise_in_bounds")


def layer_scalars(layer, lid, stiff, coup):
    material = lid[layer]
    mu = stiff[material]
    return mu, [[coup[c, d, material] for d in range(3)] for c in range(3)]


def coefficient_rows(mu, k, width=LANES):
    row = iota((COEFS, width), 0)
    top = jnp.zeros((COEFS, width), jnp.float32)
    below = jnp.ones((COEFS, width), jnp.float32)
    for c in range(3):
        diag = 6.0 * mu + k[c][c]
        others = [d for d in range(3) if d != c]
        entries = [(c, 1.0), (3 + c, mu), (6 + 2 * c, k[c][others[0]]), (7 + 2 * c, k[c][others[1]])]
        for at, value in entries:
            top = jnp.where(row == at, OMEGA * value, top)
            below = jnp.where(row == at, diag, below)
    return top / below


def roll_rows(value, before, after):
    sub = iota(value.shape, 0)
    up = jnp.where(sub == 0, jnp.broadcast_to(before, value.shape), pltpu.roll(value, 1, 0))
    down = jnp.where(sub == SUB - 1, jnp.broadcast_to(after, value.shape), pltpu.roll(value, SUB - 1, 0))
    return up + down


def roll_columns(values):
    lane = iota(values[0].shape, 1)
    right = [pltpu.roll(value, 1, 1) for value in values]
    left = [pltpu.roll(value, LANES - 1, 1) for value in values]
    last = len(values) - 1
    return [
        jnp.where(lane == 0, right[j - 1] if j > 0 else 0.0, right[j])
        + jnp.where(lane == LANES - 1, left[j + 1] if j < last else 0.0, left[j])
        for j in range(len(values))
    ]


def relax(c, centers, neighbours, force, rows):
    d0, d1 = [d for d in range(3) if d != c]
    value = rows[c] * force + rows[3 + c] * neighbours
    value = value - (rows[6 + 2 * c] * centers[d0] + rows[7 + 2 * c] * centers[d1])
    return value + (1.0 - OMEGA) * centers[c]


def chunk(j):
    return pl.ds(LANES * j, LANES)


def spans(per_row, ref, *index):
    return [ref[index + (chunk(j),)] for j in range(per_row)]


def lane_scan(values, steps):
    lane = iota(values.shape, 1)
    step = 1
    while step < steps:
        values = values + jnp.where(lane >= step, pltpu.roll(values, step, 1), 0)
        step *= 2
    return values


def local_sweep(u, f, every, layer, beside, store, groups=None, parts=(0, 1, 2)):
    rows, width = u.shape[2:]
    per_row, total = width // LANES, rows // SUB
    coef = [jnp.broadcast_to(every[layer, j:j + 1, :], (SUB, LANES)) for j in range(12)]
    none = jnp.zeros((1, LANES), jnp.float32)
    for g in range(total) if groups is None else groups:
        here = slice(SUB * g, SUB * g + SUB)
        values = [spans(per_row, u, c, layer, here) for c in range(3)]
        for c in parts:
            aside = roll_columns(values[c])
            for j in range(per_row):
                at = (c, layer)
                above = u[at + (slice(SUB * g - 1, SUB * g), chunk(j))] if g > 0 else none
                under = u[at + (slice(SUB * g + SUB, SUB * g + SUB + 1), chunk(j))] if g < total - 1 else none
                near = roll_rows(values[c][j], above, under) + aside[j]
                for other in beside:
                    near = near + u[c, other, here, chunk(j)]
                value = relax(c, [values[d][j] for d in range(3)], near, f[c, layer, here, chunk(j)], coef)
                store(c, g, j, values[c][j], value)


def faces_kernel(
    disp, forc, lid, stiff, coup, ids, cnt,
    u, f, face1, face2, send, every, cyc, num,
    lids, stiffs, coups, small_sem, near_sem, u_sem, f_sem,
):
    layers = disp.shape[1]
    top = layers - 1
    odd = lax.rem(lax.axis_index("rad"), 2) == 1
    small = [
        pltpu.make_async_copy(lid, lids, small_sem.at[0]),
        pltpu.make_async_copy(stiff, stiffs, small_sem.at[1]),
        pltpu.make_async_copy(coup, coups, small_sem.at[2]),
    ]
    cycles = [
        pltpu.make_async_copy(cnt, num, near_sem.at[0]),
        pltpu.make_async_copy(ids, cyc, near_sem.at[1]),
    ]
    loads_u = [pltpu.make_async_copy(disp.at[:, r], u.at[:, r], u_sem.at[r]) for r in range(layers)]
    loads_f = [pltpu.make_async_copy(forc.at[:, r], f.at[:, r], f_sem.at[r]) for r in range(layers)]
    for copy in small:
        copy.start()
    for r in [0, 1, top] + list(range(top - 1, 1, -1)):
        loads_u[r].start()
        if r in (0, top):
            loads_f[r].start()
    for r in range(1, top):
        loads_f[r].start()
    for copy in cycles:
        copy.start()
    for copy in small:
        copy.wait()
    for r in range(layers):
        every[r] = coefficient_rows(*layer_scalars(r, lids, stiffs, coups))
    send[...] = every[jnp.where(odd, top, 0)]

    for copy in loads_u + [loads_f[0], loads_f[top]]:
        copy.wait()
    for face, layer in ((face1, jnp.where(odd, 0, top)), (face2, jnp.where(odd, top, 0))):
        def store(c, g, j, value, swept, face=face):
            at = (c, slice(SUB * g, SUB * g + SUB), chunk(j))
            face[(0,) + at] = value
            face[(1,) + at] = swept

        local_sweep(u, f, every, layer, (jnp.where(layer == 0, 1, top - 1),), store)
    for copy in loads_f[1:top] + cycles:
        copy.wait()


def inner_kernel(u, f, every, grav, inner_s, gains, gain_in, gain_sem):
    groups = gain_in.shape[2] // SUB
    load_gains = pltpu.make_async_copy(grav, gain_in, gain_sem.at[0])
    load_gains.start()

    def middle(r, carry):
        def store(c, g, j, value, swept):
            inner_s[c, r - 1, SUB * g:SUB * g + SUB, chunk(j)] = swept

        local_sweep(u, f, every, r, (r - 1, r + 1), store)
        return carry

    lax.fori_loop(1, u.shape[1] - 1, middle, 0)
    load_gains.wait()

    lane1 = iota((1, LANES), 1)
    for load in range(2):
        for m in range(groups * SUB // LANES):
            one, two = gain_in[0, load:load + 1, chunk(m)], gain_in[1, load:load + 1, chunk(m)]
            gains[load, 2 * m:2 * m + 1, :] = jnp.where(lane1 < groups, one, pltpu.roll(two, groups, 1))
            gains[load, 2 * m + 1:2 * m + 2, :] = jnp.where(lane1 < groups, pltpu.roll(one, groups, 1), two)


def analysis_kernel(
    u, f, face1, face2, every, cyc, num, tbl,
    pay,
    plane, rims, tab, mat, windows, first_ids, last_ids, near_sem, tab_sem,
):
    layers, rows, width = u.shape[1:]
    chunks = num.shape[0]
    groups = tbl.shape[1] // SUB
    per_row = width // LANES
    lat, lats = lax.axis_index("lat"), lax.axis_size("lat")
    rad, rads = lax.axis_index("rad"), lax.axis_size("rad")
    bottom = rad == 0
    at_end = jnp.logical_or(bottom, rad == rads - 1)
    top = layers - 1
    edge, inner = jnp.where(bottom, 0, top), jnp.where(bottom, 1, top - 1)
    total = rows // SUB
    odd = lax.rem(rad, 2) == 1
    at_core = every[jnp.where(odd, 0, top)]
    cycles = [
        pltpu.make_async_copy(cyc.at[pl.ds(0, SUB), pl.ds(0, LANES)], first_ids, near_sem.at[0]),
        pltpu.make_async_copy(
            cyc.at[pl.ds(rows - SUB, SUB), pl.ds(width - LANES, LANES)], last_ids, near_sem.at[1]
        ),
    ]

    table = pltpu.make_async_copy(tbl, tab, tab_sem.at[0])

    @pl.when(at_end)
    def _():
        for copy in cycles + [table]:
            copy.start()

    for r in range(1, top):
        def store(c, g, j, value, swept, r=r):
            rims[c, r - 1, 0 if g == 0 else 1, :, chunk(j)] = swept

        local_sweep(u, f, every, r, (r - 1, r + 1), store, groups=(0, total - 1))

    sub8, lane8 = iota((SUB, LANES), 0), iota((SUB, LANES), 1)
    before = sub8 < 2
    zero = jnp.zeros((SUB, LANES), jnp.float32)
    reach = 2 * width // LEAST_COUNT + 2
    pay[0:SUB, 0:LANES] = jnp.zeros((SUB, LANES), jnp.float32)
    pay[0:SUB, LANES:2 * LANES] = at_core[0:SUB]
    pay[0:SUB, 2 * LANES:3 * LANES] = at_core[SUB:]

    @pl.when(at_end)
    def _():
        def keep_plane(c, g, j, value, swept):
            plane[SUB * g:SUB * g + SUB, chunk(j)] = swept

        local_sweep(u, f, every, inner, (inner - 1, inner + 1), keep_plane, parts=(0,))
        first = jnp.broadcast_to(cyc[0:1, 0:1], (SUB, LANES))
        last = jnp.broadcast_to(cyc[rows - 1:rows, width - 1:width], (SUB, LANES))
        own_first = jnp.zeros((SUB, LANES), jnp.int32)
        own_last = own_first
        for j in range(per_row):
            own_first = own_first + jnp.where(cyc[0:SUB, LANES * j:LANES * j + LANES] == first, 1, 0)
            own_last = own_last + jnp.where(cyc[rows - SUB:rows, LANES * j:LANES * j + LANES] == last, 1, 0)

        def total_of(count):
            count = jnp.sum(count.astype(jnp.float32), axis=1, keepdims=True)
            return jnp.broadcast_to(jnp.sum(count, axis=0, keepdims=True), (SUB, LANES)).astype(jnp.int32)

        held_here = jnp.where(before, total_of(own_first), total_of(own_last))
        index = jnp.where(before, first - lane8, last + lane8)
        place, part = jnp.bitwise_and(index, LANES - 1), jnp.right_shift(index, 7)
        lengths = jnp.full((SUB, LANES), 2 ** 20, jnp.int32)
        for q in range(chunks):
            row = jnp.broadcast_to(num[q:q + 1, :], (SUB, LANES))
            lengths = jnp.where(part == q, lane_gather(row, place), lengths)
        lengths = lengths - jnp.where(lane8 == 0, held_here, 0)
        limits = lane_scan(lengths, reach)
        caps = [jnp.broadcast_to(limits[:, i:i + 1], (SUB, LANES)) for i in range(reach)]
        spill_ids = []
        for j in range(per_row):
            column = LANES * j + lane8
            away = jnp.where(before, (width - 1 - column) + jnp.where(sub8 == 0, width, 0),
                             column + jnp.where(sub8 == 3, width, 0))
            passed = jnp.zeros((SUB, LANES), jnp.int32)
            for i in range(reach):
                passed = passed + jnp.where(away >= caps[i], 1, 0)
            spill_ids.append(jnp.where(sub8 < 4, jnp.where(before, first - passed, last + passed), 0))

        mat[0] = every[edge]
        mat[1] = every[inner]
        outer = [jnp.broadcast_to(mat[0, j:j + 1, :], (SUB, LANES)) for j in range(12)]
        below = [jnp.broadcast_to(mat[1, j:j + 1, :], (SUB, LANES)) for j in range(12)]

        def rows_of(g):
            return slice(SUB * g, SUB * g + SUB)

        def lateral(ref, g, index, ends):
            values = spans(per_row, ref, *index, rows_of(g))
            aside = roll_columns(values)
            out = []
            for j in range(per_row):
                above = ref[index + (slice(SUB * g - 1, SUB * g), chunk(j))] if g > 0 else ends[0][j]
                under = ref[index + (slice(SUB * g + SUB, SUB * g + SUB + 1), chunk(j))] if g < total - 1 else ends[1][j]
                out.append(roll_rows(values[j], above, under) + aside[j])
            return out

        low_in = jnp.where(lat > 0, 1.0, 0.0)
        high_in = jnp.where(lat < lats - 1, 1.0, 0.0)
        weight = jnp.where(sub8 == 1, low_in, jnp.where(sub8 == 2, high_in, 0.0))

        def ends_of(ref, index, j):
            low = jnp.broadcast_to(ref[index + (slice(0, 1), chunk(j))], (SUB, LANES))
            high = jnp.broadcast_to(ref[index + (slice(rows - 1, rows), chunk(j))], (SUB, LANES))
            return jnp.where(sub8 == 1, low, jnp.where(sub8 == 2, high, 0.0))

        over = [[outer[3 + c] * ends_of(u, (c, edge), j) * weight for j in range(per_row)] for c in range(3)]
        over_inner = [below[3] * ends_of(u, (0, inner), j) * weight for j in range(per_row)]
        aside = roll_columns(over[0])
        spill = []
        for j in range(per_row):
            shifted = jnp.where(sub8 == 0, pltpu.roll(over[0][j], SUB - 1, 0),
                                jnp.where(sub8 == 3, pltpu.roll(over[0][j], 1, 0), 0.0))
            near = over_inner[j] + aside[j] + shifted + ends_of(face2, (1, 0), j)
            value = relax(0, [over[c][j] for c in range(3)], near, zero, outer)
            spill.append(value * jnp.where(before, low_in, high_in))
        ends = [[over[0][j][1:2, :] for j in range(per_row)], [over[0][j][2:3, :] for j in range(per_row)]]

        met = (width - 2) // LEAST_COUNT + 2

        def window_of(values, cycles):
            start = jnp.broadcast_to(cycles[0][:, 0:1], (SUB, LANES))
            offsets = [cycle - start for cycle in cycles]
            window = zero
            for t in range(met):
                picked = [jnp.where(offset == t, value, 0.0) for offset, value in zip(offsets, values)]
                sum_t = jnp.sum(functools.reduce(jnp.add, picked), axis=1, keepdims=True)
                window = jnp.where(lane8 == t, jnp.broadcast_to(sum_t, (SUB, LANES)), window)
            return window, start

        windowed = [window_of(spill, spill_ids)]
        for g in range(total):
            here = rows_of(g)
            centers = [spans(per_row, face2, 1, c, here) for c in range(3)]
            near = lateral(face2, g, (1, 0), ends)
            inners = spans(per_row, plane, here)
            force = spans(per_row, f, 0, edge, here)
            values = [
                relax(0, [center[j] for center in centers], near[j] + inners[j], force[j], outer)
                for j in range(per_row)
            ]
            windowed.append(window_of(values, spans(per_row, cyc, here)))
        for i, (window, start) in enumerate(windowed):
            windows[0, i] = window
            windows[1, i] = start.astype(jnp.float32)

        for copy in cycles:
            copy.wait()
        low_part = jnp.right_shift(jnp.maximum(first_ids[0, 0] - reach, 0), 7)
        high_part = jnp.minimum(jnp.right_shift(last_ids[SUB - 1, LANES - 1] + reach, 7), chunks - 1)
        half = jnp.where(bottom, groups, 0)

        table.wait()

        def batch(b, result):
            means, blocks = [], []
            for i in range(BATCH):
                q = low_part + b * BATCH + i
                part = jnp.minimum(q, chunks - 1)
                blocks.append(part)
                acc = zero
                for w in range(total + 1):
                    at = q * LANES + lane8 - windows[1, w].astype(jnp.int32)
                    got = lane_gather(windows[0, w], jnp.bitwise_and(at, LANES - 1))
                    acc = acc + jnp.where(jnp.right_shift(at, 7) == 0, got, 0.0)
                mean = jnp.sum(acc, axis=0, keepdims=True) / num[pl.ds(part, 1), :].astype(jnp.float32)
                mean = jnp.where(q < chunks, mean, 0.0)
                means.append(jnp.broadcast_to(mean, (SUB, LANES)))
            for g in range(groups):
                acc = tab[blocks[0], SUB * g:SUB * g + SUB, :] * means[0]
                for i in range(1, BATCH):
                    acc = acc + tab[blocks[i], SUB * g:SUB * g + SUB, :] * means[i]
                column = jnp.broadcast_to(jnp.sum(acc, axis=1, keepdims=True), (SUB, LANES))
                result = jnp.where(lane8 == g + half, result + column, result)
            return result

        pay[0:SUB, 0:LANES] = lax.fori_loop(0, (high_part - low_part) // BATCH + 1, batch, zero)

    tall = 3 * layers

    def pack(ref, base, near):
        for c in range(3):
            for r in range(layers):
                at = base + c * layers + r
                ref[at:at + 1, :] = u[c, r, near:near + 1, :]
                if r == 0:
                    row = jnp.where(odd, face1[1, c, near:near + 1, :], face2[1, c, near:near + 1, :])
                elif r == top:
                    row = jnp.where(odd, face2[1, c, near:near + 1, :], face1[1, c, near:near + 1, :])
                else:
                    row = rims[c, r - 1, near // (rows - 1), near % SUB:near % SUB + 1, :]
                ref[at + tall:at + tall + 1, :] = row

    pack(pay, SUB, 0)
    pack(pay, SUB + 2 * tall, rows - 1)


def relay_kernel(ring, send, out):
    cores = 2
    lat, lats = lax.axis_index("lat"), lax.axis_size("lat")
    core = lax.rem(lax.axis_index("rad"), cores)
    members, _, width = ring.shape
    tall = (ring.shape[1] - SUB) // 4
    layers = tall // 3
    coef = ring[0, 0:SUB, 0:LANES]
    for i in range(1, members):
        coef = coef + ring[i, 0:SUB, 0:LANES]
    out[0:SUB, :] = coef
    out[SUB:SUB + COEFS, :] = send[...]
    before, after = cores * jnp.maximum(lat - 1, 0) + core, cores * jnp.minimum(lat + 1, lats - 1) + core
    low_in, high_in = lat > 0, lat < lats - 1
    for j in range(width // LANES):
        base = SUB + COEFS + SUB * j
        out[base:base + SUB, :] = jnp.zeros((SUB, LANES), jnp.float32)
        for c in range(3):
            for at, member, valid, start in ((c, before, low_in, 2 * tall), (3 + c, after, high_in, 0)):
                row = SUB + start + c * layers
                bottom, top = ring[member, row:row + 1, chunk(j)], ring[member, row + layers - 1:row + layers, chunk(j)]
                out[base + at:base + at + 1, :] = jnp.where(valid, jnp.where(core == 1, top, bottom), 0.0)


def sweep_kernel(
    u, f, own1, own2, inner_s, face1, face2, ring, got, every,
    out,
    s, rim, done, cf, out_sem,
):
    layers, rows, width = u.shape[1:]
    per_row = width // LANES
    total = rows // SUB
    tall = 3 * layers
    top = layers - 1
    lat, lats = lax.axis_index("lat"), lax.axis_size("lat")
    rad, rads = lax.axis_index("rad"), lax.axis_size("rad")
    rad_odd = lax.rem(rad, 2) == 1
    cores = 2
    core = lax.rem(rad, cores)
    lower, upper = cores * jnp.maximum(lat - 1, 0), cores * jnp.minimum(lat + 1, lats - 1)
    low_in, high_in = lat > 0, lat < lats - 1
    sub8 = iota((SUB, LANES), 0)

    def side_rows(base, j):
        at = SUB + base
        low = ring[lower + core, at + 2 * tall:at + 2 * tall + layers, chunk(j)]
        high = ring[upper + core, at:at + layers, chunk(j)]
        low, high = jnp.where(low_in, low, 0.0), jnp.where(high_in, high, 0.0)
        return jnp.concatenate([low, high], axis=0)

    mate = 1 - core
    own_chip = jnp.concatenate(
        [ring[cores * lat + mate, 0:SUB, LANES:2 * LANES], ring[cores * lat + mate, 0:SUB, 2 * LANES:3 * LANES]], axis=0
    )
    other_chip = got[SUB:SUB + COEFS, :]
    lowest, highest = rad == 0, rad == rads - 1
    cf[0] = jnp.where(rad_odd, own_chip, jnp.where(lowest, 0.0, other_chip))
    cf[layers + 1] = jnp.where(rad_odd, jnp.where(highest, 0.0, other_chip), own_chip)
    for r in range(layers):
        cf[1 + r] = every[r]
    corner_low, corner_high = [], []
    for j in range(per_row):
        base = SUB + COEFS + SUB * j
        other = got[base:base + SUB, :]
        rows_own = []
        for member, valid, start in ((lower + mate, low_in, 2 * tall), (upper + mate, high_in, 0)):
            for c in range(3):
                row = SUB + start + c * layers
                near_end, far_end = ring[member, row:row + 1, chunk(j)], ring[member, row + top:row + top + 1, chunk(j)]
                rows_own.append(jnp.where(valid, jnp.where(rad_odd, far_end, near_end), 0.0))
        rows_own.append(jnp.zeros((SUB - 6, LANES), jnp.float32))
        own = jnp.concatenate(rows_own, axis=0)
        corner_low.append(jnp.where(rad_odd, own, jnp.where(lowest, 0.0, other)))
        corner_high.append(jnp.where(rad_odd, jnp.where(highest, 0.0, other), own))

    def coefficients(layer):
        return [jnp.broadcast_to(cf[layer, j:j + 1, :], (SUB, LANES)) for j in range(12)]

    near_rows = [[side_rows(c * layers, j) for j in range(per_row)] for c in range(3)]
    keep = jnp.where(sub8 < layers, jnp.where(low_in, 1.0, 0.0), jnp.where(high_in, 1.0, 0.0))
    for c in range(3):
        gain = jnp.zeros((SUB, LANES), jnp.float32)
        for r in range(layers):
            here = jnp.broadcast_to(cf[1 + r, 3 + c:4 + c, :], (SUB, LANES))
            gain = jnp.where(jnp.logical_or(sub8 == r, sub8 == layers + r), here, gain)
        for j in range(per_row):
            near = jnp.zeros((SUB, LANES), jnp.float32)
            for r in range(layers):
                head = jnp.broadcast_to(u[c, r, 0:1, chunk(j)], near.shape)
                tail = jnp.broadcast_to(u[c, r, rows - 1:rows, chunk(j)], near.shape)
                near = jnp.where(sub8 == r, head, jnp.where(sub8 == layers + r, tail, near))
            ends = (
                (0, corner_low[j][c:c + 1, :]), (layers, corner_low[j][3 + c:4 + c, :]),
                (layers - 1, corner_high[j][c:c + 1, :]), (SUB - 1, corner_high[j][3 + c:4 + c, :]),
            )
            for row, corner in ends:
                near = near + jnp.where(sub8 == row, jnp.broadcast_to(corner, near.shape), 0.0)
            value = (side_rows(tall + c * layers, j) + gain * near) * keep
            for i in range(2 * layers):
                rim[i, c, :, chunk(j)] = jnp.broadcast_to(value[i:i + 1, :], (SUB, LANES))

    def beyond(layer, side, c, j):
        if layer == 0:
            return corner_low[j][3 * side + c:3 * side + c + 1, :]
        if layer == layers + 1:
            return corner_high[j][3 * side + c:3 * side + c + 1, :]
        at = layers * side + layer - 1
        return near_rows[c][j][at:at + 1, :]

    def lo(index):
        return jnp.where(rad_odd, face1[index], face2[index])

    def hi(index):
        return jnp.where(rad_odd, face2[index], face1[index])

    for layer in range(layers + 2):
        for c in range(3):
            gain = jnp.broadcast_to(cf[layer, 3 + c:4 + c, :], (SUB, LANES))
            for j in range(per_row):
                for g in range(total):
                    at = (slice(SUB * g, SUB * g + SUB), chunk(j))
                    if layer == 0:
                        value = lo((1, c) + at) + gain * u[(c, 0) + at]
                    elif layer == layers + 1:
                        value = hi((1, c) + at) + gain * u[(c, top) + at]
                    elif layer in (1, layers):
                        here1, here2 = own1[(1, c) + at], own2[(1, c) + at]
                        value = jnp.where(rad_odd, here1, here2) if layer == 1 else jnp.where(rad_odd, here2, here1)
                    else:
                        value = inner_s[(c, layer - 2) + at]
                    if layer == 1:
                        value = value + gain * lo((0, c) + at)
                    if layer == layers:
                        value = value + gain * hi((0, c) + at)
                    if g == 0:
                        row = jnp.broadcast_to(beyond(layer, 0, c, j), value.shape)
                        value = value + jnp.where(sub8 == 0, gain * row, 0.0)
                    if g == total - 1:
                        row = jnp.broadcast_to(beyond(layer, 1, c, j), value.shape)
                        value = value + jnp.where(sub8 == SUB - 1, gain * row, 0.0)
                    s[(c, layer) + at] = value

    stores = [pltpu.make_async_copy(done.at[:, r], out.at[:, r], out_sem.at[r]) for r in range(layers)]
    for r in range(layers):
        layer = r + 1
        coef = coefficients(layer)
        for g in range(total):
            here = slice(SUB * g, SUB * g + SUB)
            values = [spans(per_row, s, c, layer, here) for c in range(3)]
            for c in range(3):
                aside = roll_columns(values[c])
                for j in range(per_row):
                    at = (c, layer)
                    if g > 0:
                        above_row = s[at + (slice(SUB * g - 1, SUB * g), chunk(j))]
                    else:
                        above_row = rim[r, c, :, chunk(j)]
                    if g < total - 1:
                        under_row = s[at + (slice(SUB * g + SUB, SUB * g + SUB + 1), chunk(j))]
                    else:
                        under_row = rim[layers + r, c, :, chunk(j)]
                    near = roll_rows(values[c][j], above_row, under_row) + aside[j]
                    near = near + (s[c, layer - 1, here, chunk(j)] + s[c, layer + 1, here, chunk(j)])
                    done[c, r, here, chunk(j)] = relax(
                        c, [values[d][j] for d in range(3)], near, f[c, r, here, chunk(j)], coef
                    )
        stores[r].start()
    for copy in stores:
        copy.wait()


def synthesis_kernel(scale, coef, rest, gains, ids, tab, out, factors):
    rows, width = ids.shape
    chunks = tab.shape[0]
    groups = tab.shape[1] // SUB
    per_row = width // LANES
    lane8 = iota((SUB, LANES), 1)
    here = coef[...] + rest[...]
    other = pltpu.roll(here, groups, 1)
    left = lane8 < groups
    surface = jnp.where(left, here, other)
    core = jnp.where(left, other, here)
    modes = (gains[0] * surface + gains[1] * core) * scale
    zero = jnp.zeros((SUB, LANES), jnp.float32)
    for i in range(2 * groups):
        factors[i] = jnp.broadcast_to(modes[:, i:i + 1], (SUB, LANES))
    low_part = jnp.right_shift(jnp.min(ids[0:1, 0:LANES]), 7)
    high_part = jnp.right_shift(jnp.max(ids[rows - 1:rows, width - LANES:width]), 7)

    def batch(b, carry):
        parts = [low_part + b * BATCH + i for i in range(BATCH)]
        blocks = [jnp.minimum(part, chunks - 1) for part in parts]
        sums = [[zero] * BATCH for _ in range(2)]
        for g in range(groups):
            for i in range(BATCH):
                block = tab[blocks[i], SUB * g:SUB * g + SUB, :]
                for k in range(2):
                    sums[k][i] = sums[k][i] + factors[k * groups + g] * block
        for k in range(2):
            for i in range(BATCH):
                sums[k][i] = jnp.broadcast_to(jnp.sum(sums[k][i], axis=0, keepdims=True), (SUB, LANES))
        for a in range(rows // SUB):
            for j in range(per_row):
                spot = (slice(SUB * a, SUB * a + SUB), chunk(j))
                cycle = ids[spot]
                place, part = jnp.bitwise_and(cycle, LANES - 1), jnp.right_shift(cycle, 7)
                values = [zero if isinstance(b, int) else out[(k,) + spot] for k in range(2)]
                for i in range(BATCH):
                    chosen = part == parts[i]
                    for k in range(2):
                        values[k] = jnp.where(chosen, lane_gather(sums[k][i], place), values[k])
                for k in range(2):
                    out[(k,) + spot] = values[k]
        return carry

    batch(0, 0)
    lax.fori_loop(1, (high_part - low_part) // BATCH + 1, batch, 0)


def even_pairs(count):
    return [(i, i ^ 1) for i in range(count)]


def odd_pairs(count):
    pairs = []
    for i in range(1, count, 2):
        j = (i + 1) % count
        pairs += [(i, j), (j, i)]
    return pairs


def local(displacement, forcing, layer_id, stiffness, coupling, cycle_id, cycle_count, gravity):
    _, layers, rows, width = displacement.shape
    cycles, degrees = cycle_count.shape[0], gravity.shape[2]
    chunks, groups = cycles // LANES, degrees // SUB
    lats, rads, cores = lax.axis_size("lat"), lax.axis_size("rad"), 2
    if 2 * groups != LANES or 2 * layers != SUB or rads % cores or width < 3 * LANES:
        raise ValueError("unsupported sizes")
    f32 = jnp.float32
    table = jnp.asarray(basis_table(degrees, cycles))
    per_row = width // LANES
    tall = 3 * layers
    face = jax.ShapeDtypeStruct((2, 3, rows, width), f32)

    whole = jax.ShapeDtypeStruct(displacement.shape, f32)
    pinned = [
        pltpu.with_memory_space_constraint(value, pltpu.HBM)
        for value in (
            displacement, forcing, layer_id, stiffness, jnp.transpose(coupling, (1, 2, 0)), cycle_id,
            cycle_count.reshape(chunks, LANES), gravity, table,
        )
    ]
    u, f, face1, face2, mine, every, cyc, num = pl.pallas_call(
        faces_kernel,
        out_shape=(
            whole, whole,
            face, face,
            jax.ShapeDtypeStruct((COEFS, LANES), f32),
            jax.ShapeDtypeStruct((layers, COEFS, LANES), f32),
            jax.ShapeDtypeStruct(cycle_id.shape, jnp.int32),
            jax.ShapeDtypeStruct((chunks, LANES), jnp.int32),
        ),
        in_specs=[HBM] * 7,
        out_specs=(VMEM,) * 8,
        scratch_shapes=[
            pltpu.SMEM(layer_id.shape, jnp.int32),
            pltpu.SMEM(stiffness.shape, f32),
            pltpu.SMEM(coupling.shape[1:] + coupling.shape[:1], f32),
            pltpu.SemaphoreType.DMA((3,)),
            pltpu.SemaphoreType.DMA((2,)),
            pltpu.SemaphoreType.DMA((layers,)),
            pltpu.SemaphoreType.DMA((layers,)),
        ],
        compiler_params=pltpu.CompilerParams(vmem_limit_bytes=VMEM_LIMIT),
        name="faces",
    )(*pinned[:7])

    beside2 = lax.ppermute(face2, "rad", odd_pairs(rads)[:-2])
    beside1 = lax.ppermute(face1, "rad", even_pairs(rads))

    pay = pl.pallas_call(
        analysis_kernel,
        out_shape=jax.ShapeDtypeStruct((SUB + 4 * tall, width), f32),
        in_specs=[VMEM] * 7 + [HBM],
        out_specs=VMEM,
        scratch_shapes=[
            pltpu.VMEM((rows, width), f32),
            pltpu.VMEM((3, layers - 2, 2, SUB, width), f32),
            pltpu.VMEM(table.shape, f32),
            pltpu.VMEM((2, COEFS, LANES), f32),
            pltpu.VMEM((2, rows // SUB + 1, SUB, LANES), f32),
            pltpu.SMEM((SUB, LANES), jnp.int32),
            pltpu.SMEM((SUB, LANES), jnp.int32),
            pltpu.SemaphoreType.DMA((2,)),
            pltpu.SemaphoreType.DMA((1,)),
        ],
        compiler_params=pltpu.CompilerParams(vmem_limit_bytes=VMEM_LIMIT),
        name="analysis",
    )(u, f, face1, face2, every, cyc, num, pinned[8])

    chips = [[a * rads + b + c for a in range(lats) for c in range(cores)] for b in range(0, rads, cores)]
    ring = lax.all_gather(pay, ("lat", "rad"), axis_index_groups=chips)
    outward = pl.pallas_call(
        relay_kernel,
        out_shape=jax.ShapeDtypeStruct((SUB + COEFS + SUB * per_row, LANES), f32),
        in_specs=[VMEM] * 2,
        out_specs=VMEM,
        compiler_params=pltpu.CompilerParams(vmem_limit_bytes=VMEM_LIMIT),
        name="relay",
    )(ring, mine)
    outward, beside1, beside2 = lax.optimization_barrier((outward, beside1, beside2))
    got = lax.ppermute(outward, "rad", odd_pairs(rads))
    inner_s, gains = pl.pallas_call(
        inner_kernel,
        out_shape=(
            jax.ShapeDtypeStruct((3, layers - 2, rows, width), f32),
            jax.ShapeDtypeStruct((2, SUB, LANES), f32),
        ),
        in_specs=[VMEM] * 3 + [HBM],
        out_specs=(VMEM,) * 2,
        scratch_shapes=[pltpu.VMEM(gravity.shape, f32), pltpu.SemaphoreType.DMA((1,))],
        compiler_params=pltpu.CompilerParams(vmem_limit_bytes=VMEM_LIMIT),
        name="inner",
    )(u, f, every, pinned[7])
    got, inner_s = lax.optimization_barrier((got, inner_s))
    coef = outward[:SUB]
    if rads == 8:
        coef = coef + got[:SUB]
        rest = lax.ppermute(coef, "rad", [(0, 3), (3, 0), (7, 4), (4, 7), (1, 5), (5, 1), (2, 6), (6, 2)])
    else:
        coef = lax.psum(coef, "rad") * (1.0 / cores)
        rest = jnp.zeros_like(coef)

    smoothed = pl.pallas_call(
        sweep_kernel,
        out_shape=whole,
        in_specs=[VMEM] * 10,
        out_specs=HBM,
        scratch_shapes=[
            pltpu.VMEM((3, layers + 2, rows, width), f32),
            pltpu.VMEM((2 * layers, 3, SUB, width), f32),
            pltpu.VMEM((3, layers, rows, width), f32),
            pltpu.VMEM((layers + 2, COEFS, LANES), f32),
            pltpu.SemaphoreType.DMA((layers,)),
        ],
        compiler_params=pltpu.CompilerParams(vmem_limit_bytes=VMEM_LIMIT),
        name="sweeps",
    )(u, f, face1, face2, inner_s, beside1, beside2, ring, got, every)
    coef, smoothed = lax.optimization_barrier((coef, smoothed))

    potential = pl.pallas_call(
        functools.partial(synthesis_kernel, 2.0 / cycles),
        out_shape=jax.ShapeDtypeStruct((2, rows, width), f32),
        in_specs=[VMEM] * 5,
        out_specs=VMEM,
        scratch_shapes=[pltpu.VMEM((2 * groups, SUB, LANES), f32)],
        compiler_params=pltpu.CompilerParams(vmem_limit_bytes=VMEM_LIMIT),
        name="synthesis",
    )(coef, rest, gains, cyc, table)
    return smoothed, potential


def solution(mesh):
    in_specs = (
        P(None, "rad", "lat", None),
        P(None, "rad", "lat", None),
        P("rad"),
        P(),
        P(),
        P("lat", None),
        P(),
        P(),
    )
    out_specs = (P(None, "rad", "lat", None), P(None, "lat", None))
    return jax.shard_map(local, mesh=mesh, in_specs=in_specs, out_specs=out_specs, check_vma=False)
```

```python
import functools
import math

import jax
import jax.numpy as jnp
import numpy as np
from jax import lax
from jax.experimental import pallas as pl
from jax.experimental.pallas import tpu as pltpu
from jax.sharding import PartitionSpec as P

SWEEPS = 2
OMEGA = 0.8
LEAST_COUNT = 32
LANES = 128
SUB = 8
PAD = 8
COEFS = 16
BATCH = 5
VMEM_LIMIT = 16 * 1024 * 1024

VMEM = pl.BlockSpec(memory_space=pltpu.VMEM)
SMEM = pl.BlockSpec(memory_space=pltpu.SMEM)
HBM = pl.BlockSpec(memory_space=pltpu.HBM)
ANY = pl.BlockSpec(memory_space=pl.ANY)


def basis_table(degrees, cycles):
    groups = degrees // SUB
    degree = np.arange(degrees, dtype=np.int64)[:, None]
    cycle = np.arange(cycles, dtype=np.int64)[None, :]
    phase = degree * (2 * cycle + 1) % (4 * cycles)
    table = np.cos(np.pi * phase / (2.0 * cycles)).astype(np.float32)
    table = table.reshape(SUB, groups, cycles // LANES, LANES).transpose(2, 1, 0, 3)
    return np.ascontiguousarray(table.reshape(cycles // LANES, degrees, LANES))


def iota(shape, dim):
    return lax.broadcasted_iota(jnp.int32, shape, dim)


def lane_gather(values, index):
    return jnp.take_along_axis(values, index, axis=1, mode="promise_in_bounds")


def layer_scalars(layer, lid, stiff, coup):
    material = lid[layer]
    mu = stiff[material]
    return mu, [[coup[c, d, material] for d in range(3)] for c in range(3)]


def coefficient_rows(mu, k, width=LANES):
    row = iota((COEFS, width), 0)
    top = jnp.zeros((COEFS, width), jnp.float32)
    below = jnp.ones((COEFS, width), jnp.float32)
    for c in range(3):
        diag = 6.0 * mu + k[c][c]
        others = [d for d in range(3) if d != c]
        entries = [(c, 1.0), (3 + c, mu), (6 + 2 * c, k[c][others[0]]), (7 + 2 * c, k[c][others[1]])]
        for at, value in entries:
            top = jnp.where(row == at, OMEGA * value, top)
            below = jnp.where(row == at, diag, below)
    return top / below


def roll_rows(value, before, after):
    sub = iota(value.shape, 0)
    up = jnp.where(sub == 0, jnp.broadcast_to(before, value.shape), pltpu.roll(value, 1, 0))
    down = jnp.where(sub == SUB - 1, jnp.broadcast_to(after, value.shape), pltpu.roll(value, SUB - 1, 0))
    return up + down


def roll_columns(values):
    lane = iota(values[0].shape, 1)
    right = [pltpu.roll(value, 1, 1) for value in values]
    left = [pltpu.roll(value, LANES - 1, 1) for value in values]
    last = len(values) - 1
    return [
        jnp.where(lane == 0, right[j - 1] if j > 0 else 0.0, right[j])
        + jnp.where(lane == LANES - 1, left[j + 1] if j < last else 0.0, left[j])
        for j in range(len(values))
    ]


def relax(c, centers, neighbours, force, rows):
    d0, d1 = [d for d in range(3) if d != c]
    value = rows[c] * force + rows[3 + c] * neighbours
    value = value - (rows[6 + 2 * c] * centers[d0] + rows[7 + 2 * c] * centers[d1])
    return value + (1.0 - OMEGA) * centers[c]


def chunk(j):
    return pl.ds(LANES * j, LANES)


def spans(per_row, ref, *index):
    return [ref[index + (chunk(j),)] for j in range(per_row)]


def lane_scan(values, steps):
    lane = iota(values.shape, 1)
    step = 1
    while step < steps:
        values = values + jnp.where(lane >= step, pltpu.roll(values, step, 1), 0)
        step *= 2
    return values


def local_sweep(u, f, every, layer, beside, store, groups=None, parts=(0, 1, 2)):
    rows, width = u.shape[2:]
    per_row, total = width // LANES, rows // SUB
    coef = [jnp.broadcast_to(every[layer, j:j + 1, :], (SUB, LANES)) for j in range(12)]
    none = jnp.zeros((1, LANES), jnp.float32)
    for g in range(total) if groups is None else groups:
        here = slice(SUB * g, SUB * g + SUB)
        values = [spans(per_row, u, c, layer, here) for c in range(3)]
        for c in parts:
            aside = roll_columns(values[c])
            for j in range(per_row):
                at = (c, layer)
                above = u[at + (slice(SUB * g - 1, SUB * g), chunk(j))] if g > 0 else none
                under = u[at + (slice(SUB * g + SUB, SUB * g + SUB + 1), chunk(j))] if g < total - 1 else none
                near = roll_rows(values[c][j], above, under) + aside[j]
                for other in beside:
                    near = near + u[c, other, here, chunk(j)]
                value = relax(c, [values[d][j] for d in range(3)], near, f[c, layer, here, chunk(j)], coef)
                store(c, g, j, values[c][j], value)


def faces_kernel(
    disp, forc, lid, stiff, coup, ids, cnt, grav,
    u, f, face1, face2, send, every, cyc, num, gain_in,
    lids, stiffs, coups, small_sem, near_sem, u_sem, f_sem,
):
    layers = disp.shape[1]
    top = layers - 1
    odd = lax.rem(lax.axis_index("rad"), 2) == 1
    small = [
        pltpu.make_async_copy(lid, lids, small_sem.at[0]),
        pltpu.make_async_copy(stiff, stiffs, small_sem.at[1]),
        pltpu.make_async_copy(coup, coups, small_sem.at[2]),
    ]
    cycles = [
        pltpu.make_async_copy(cnt, num, near_sem.at[0]),
        pltpu.make_async_copy(ids, cyc, near_sem.at[1]),
        pltpu.make_async_copy(grav, gain_in, near_sem.at[2]),
    ]
    loads_u = [pltpu.make_async_copy(disp.at[:, r], u.at[:, r], u_sem.at[r]) for r in range(layers)]
    loads_f = [pltpu.make_async_copy(forc.at[:, r], f.at[:, r], f_sem.at[r]) for r in range(layers)]
    for copy in small:
        copy.start()
    for r in [0, 1, top] + list(range(top - 1, 1, -1)):
        loads_u[r].start()
        if r in (0, top):
            loads_f[r].start()
    for r in range(1, top):
        loads_f[r].start()
    for copy in cycles:
        copy.start()
    for copy in small:
        copy.wait()
    for r in range(layers):
        every[r] = coefficient_rows(*layer_scalars(r, lids, stiffs, coups))
    send[...] = every[jnp.where(odd, top, 0)]

    for copy in loads_u + [loads_f[0], loads_f[top]]:
        copy.wait()
    for face, layer in ((face1, jnp.where(odd, 0, top)), (face2, jnp.where(odd, top, 0))):
        def store(c, g, j, value, swept, face=face):
            at = (c, slice(SUB * g, SUB * g + SUB), chunk(j))
            face[(0,) + at] = value
            face[(1,) + at] = swept

        local_sweep(u, f, every, layer, (jnp.where(layer == 0, 1, top - 1),), store)
    for copy in loads_f[1:top] + cycles:
        copy.wait()


def inner_kernel(u, f, every, gain_in, inner_s, gains):
    groups = gain_in.shape[2] // SUB

    def middle(r, carry):
        def store(c, g, j, value, swept):
            inner_s[c, r - 1, SUB * g:SUB * g + SUB, chunk(j)] = swept

        local_sweep(u, f, every, r, (r - 1, r + 1), store)
        return carry

    lax.fori_loop(1, u.shape[1] - 1, middle, 0)

    lane1 = iota((1, LANES), 1)
    for load in range(2):
        for m in range(groups * SUB // LANES):
            one, two = gain_in[0, load:load + 1, chunk(m)], gain_in[1, load:load + 1, chunk(m)]
            gains[load, 2 * m:2 * m + 1, :] = jnp.where(lane1 < groups, one, pltpu.roll(two, groups, 1))
            gains[load, 2 * m + 1:2 * m + 2, :] = jnp.where(lane1 < groups, pltpu.roll(one, groups, 1), two)


def analysis_kernel(
    u, f, face1, face2, every, cyc, num, tbl,
    pay,
    plane, rims, tab, mat, windows, tab_sem,
):
    layers, rows, width = u.shape[1:]
    chunks = num.shape[0]
    groups = tbl.shape[1] // SUB
    per_row = width // LANES
    lat, lats = lax.axis_index("lat"), lax.axis_size("lat")
    rad, rads = lax.axis_index("rad"), lax.axis_size("rad")
    bottom = rad == 0
    at_end = jnp.logical_or(bottom, rad == rads - 1)
    top = layers - 1
    edge, inner = jnp.where(bottom, 0, top), jnp.where(bottom, 1, top - 1)
    total = rows // SUB
    odd = lax.rem(rad, 2) == 1
    at_core = every[jnp.where(odd, 0, top)]
    reach = 2 * width // LEAST_COUNT + 2
    low_part = jnp.right_shift(jnp.maximum(jnp.min(cyc[0:1, 0:LANES]) - reach, 0), 7)
    high_part = jnp.right_shift(jnp.max(cyc[rows - 1:rows, width - LANES:width]) + reach, 7)
    high_part = jnp.minimum(high_part, chunks - 1)

    def table(b):
        return [
            pltpu.make_async_copy(
                tbl.at[jnp.minimum(low_part + b * BATCH + i, chunks - 1)], tab.at[i], tab_sem.at[i]
            )
            for i in range(BATCH)
        ]

    @pl.when(at_end)
    def _():
        for copy in table(0):
            copy.start()

    for r in range(1, top):
        def store(c, g, j, value, swept, r=r):
            rims[c, r - 1, 0 if g == 0 else 1, :, chunk(j)] = swept

        local_sweep(u, f, every, r, (r - 1, r + 1), store, groups=(0, total - 1))

    sub8, lane8 = iota((SUB, LANES), 0), iota((SUB, LANES), 1)
    before = sub8 < 2
    zero = jnp.zeros((SUB, LANES), jnp.float32)
    pay[0:SUB, 0:LANES] = jnp.zeros((SUB, LANES), jnp.float32)
    pay[0:SUB, LANES:2 * LANES] = at_core[0:SUB]
    pay[0:SUB, 2 * LANES:3 * LANES] = at_core[SUB:]

    @pl.when(at_end)
    def _():
        def keep_plane(c, g, j, value, swept):
            plane[SUB * g:SUB * g + SUB, chunk(j)] = swept

        local_sweep(u, f, every, inner, (inner - 1, inner + 1), keep_plane, parts=(0,))
        first = jnp.broadcast_to(cyc[0:1, 0:1], (SUB, LANES))
        last = jnp.broadcast_to(cyc[rows - 1:rows, width - 1:width], (SUB, LANES))
        own_first = jnp.zeros((SUB, LANES), jnp.int32)
        own_last = own_first
        for j in range(per_row):
            own_first = own_first + jnp.where(cyc[0:SUB, LANES * j:LANES * j + LANES] == first, 1, 0)
            own_last = own_last + jnp.where(cyc[rows - SUB:rows, LANES * j:LANES * j + LANES] == last, 1, 0)

        def total_of(count):
            count = jnp.sum(count.astype(jnp.float32), axis=1, keepdims=True)
            return jnp.broadcast_to(jnp.sum(count, axis=0, keepdims=True), (SUB, LANES)).astype(jnp.int32)

        held_here = jnp.where(before, total_of(own_first), total_of(own_last))
        index = jnp.where(before, first - lane8, last + lane8)
        place, part = jnp.bitwise_and(index, LANES - 1), jnp.right_shift(index, 7)
        lengths = jnp.full((SUB, LANES), 2 ** 20, jnp.int32)
        for q in range(chunks):
            row = jnp.broadcast_to(num[q:q + 1, :], (SUB, LANES))
            lengths = jnp.where(part == q, lane_gather(row, place), lengths)
        lengths = lengths - jnp.where(lane8 == 0, held_here, 0)
        limits = lane_scan(lengths, reach)
        caps = [jnp.broadcast_to(limits[:, i:i + 1], (SUB, LANES)) for i in range(reach)]
        spill_ids = []
        for j in range(per_row):
            column = LANES * j + lane8
            away = jnp.where(before, (width - 1 - column) + jnp.where(sub8 == 0, width, 0),
                             column + jnp.where(sub8 == 3, width, 0))
            passed = jnp.zeros((SUB, LANES), jnp.int32)
            for i in range(reach):
                passed = passed + jnp.where(away >= caps[i], 1, 0)
            spill_ids.append(jnp.where(sub8 < 4, jnp.where(before, first - passed, last + passed), 0))

        mat[0] = every[edge]
        mat[1] = every[inner]
        outer = [jnp.broadcast_to(mat[0, j:j + 1, :], (SUB, LANES)) for j in range(12)]
        below = [jnp.broadcast_to(mat[1, j:j + 1, :], (SUB, LANES)) for j in range(12)]

        def rows_of(g):
            return slice(SUB * g, SUB * g + SUB)

        def lateral(ref, g, index, ends):
            values = spans(per_row, ref, *index, rows_of(g))
            aside = roll_columns(values)
            out = []
            for j in range(per_row):
                above = ref[index + (slice(SUB * g - 1, SUB * g), chunk(j))] if g > 0 else ends[0][j]
                under = ref[index + (slice(SUB * g + SUB, SUB * g + SUB + 1), chunk(j))] if g < total - 1 else ends[1][j]
                out.append(roll_rows(values[j], above, under) + aside[j])
            return out

        low_in = jnp.where(lat > 0, 1.0, 0.0)
        high_in = jnp.where(lat < lats - 1, 1.0, 0.0)
        weight = jnp.where(sub8 == 1, low_in, jnp.where(sub8 == 2, high_in, 0.0))

        def ends_of(ref, index, j):
            low = jnp.broadcast_to(ref[index + (slice(0, 1), chunk(j))], (SUB, LANES))
            high = jnp.broadcast_to(ref[index + (slice(rows - 1, rows), chunk(j))], (SUB, LANES))
            return jnp.where(sub8 == 1, low, jnp.where(sub8 == 2, high, 0.0))

        over = [[outer[3 + c] * ends_of(u, (c, edge), j) * weight for j in range(per_row)] for c in range(3)]
        over_inner = [below[3] * ends_of(u, (0, inner), j) * weight for j in range(per_row)]
        aside = roll_columns(over[0])
        spill = []
        for j in range(per_row):
            shifted = jnp.where(sub8 == 0, pltpu.roll(over[0][j], SUB - 1, 0),
                                jnp.where(sub8 == 3, pltpu.roll(over[0][j], 1, 0), 0.0))
            near = over_inner[j] + aside[j] + shifted + ends_of(face2, (1, 0), j)
            value = relax(0, [over[c][j] for c in range(3)], near, zero, outer)
            spill.append(value * jnp.where(before, low_in, high_in))
        ends = [[over[0][j][1:2, :] for j in range(per_row)], [over[0][j][2:3, :] for j in range(per_row)]]

        met = (width - 2) // LEAST_COUNT + 2

        def window_of(values, cycles):
            start = jnp.broadcast_to(cycles[0][:, 0:1], (SUB, LANES))
            offsets = [cycle - start for cycle in cycles]
            window = zero
            for t in range(met):
                picked = [jnp.where(offset == t, value, 0.0) for offset, value in zip(offsets, values)]
                sum_t = jnp.sum(functools.reduce(jnp.add, picked), axis=1, keepdims=True)
                window = jnp.where(lane8 == t, jnp.broadcast_to(sum_t, (SUB, LANES)), window)
            return window, start

        windowed = [window_of(spill, spill_ids)]
        for g in range(total):
            here = rows_of(g)
            centers = [spans(per_row, face2, 1, c, here) for c in range(3)]
            near = lateral(face2, g, (1, 0), ends)
            inners = spans(per_row, plane, here)
            force = spans(per_row, f, 0, edge, here)
            values = [
                relax(0, [center[j] for center in centers], near[j] + inners[j], force[j], outer)
                for j in range(per_row)
            ]
            windowed.append(window_of(values, spans(per_row, cyc, here)))
        for i, (window, start) in enumerate(windowed):
            windows[0, i] = window
            windows[1, i] = start.astype(jnp.float32)

        half = jnp.where(bottom, groups, 0)


        def batch(b, result):
            @pl.when(b > 0)
            def _():
                for copy in table(b):
                    copy.start()

            means = []
            for i in range(BATCH):
                q = low_part + b * BATCH + i
                part = jnp.minimum(q, chunks - 1)
                acc = zero
                for w in range(total + 1):
                    at = q * LANES + lane8 - windows[1, w].astype(jnp.int32)
                    got = lane_gather(windows[0, w], jnp.bitwise_and(at, LANES - 1))
                    acc = acc + jnp.where(jnp.right_shift(at, 7) == 0, got, 0.0)
                mean = jnp.sum(acc, axis=0, keepdims=True) / num[pl.ds(part, 1), :].astype(jnp.float32)
                mean = jnp.where(q < chunks, mean, 0.0)
                means.append(jnp.broadcast_to(mean, (SUB, LANES)))
            for copy in table(b):
                copy.wait()
            for g in range(groups):
                acc = tab[0, SUB * g:SUB * g + SUB, :] * means[0]
                for i in range(1, BATCH):
                    acc = acc + tab[i, SUB * g:SUB * g + SUB, :] * means[i]
                column = jnp.broadcast_to(jnp.sum(acc, axis=1, keepdims=True), (SUB, LANES))
                result = jnp.where(lane8 == g + half, result + column, result)
            return result

        pay[0:SUB, 0:LANES] = lax.fori_loop(0, (high_part - low_part) // BATCH + 1, batch, zero)

    tall = 3 * layers

    def pack(ref, base, near):
        for c in range(3):
            for r in range(layers):
                at = base + c * layers + r
                ref[at:at + 1, :] = u[c, r, near:near + 1, :]
                if r == 0:
                    row = jnp.where(odd, face1[1, c, near:near + 1, :], face2[1, c, near:near + 1, :])
                elif r == top:
                    row = jnp.where(odd, face2[1, c, near:near + 1, :], face1[1, c, near:near + 1, :])
                else:
                    row = rims[c, r - 1, near // (rows - 1), near % SUB:near % SUB + 1, :]
                ref[at + tall:at + tall + 1, :] = row

    pack(pay, SUB, 0)
    pack(pay, SUB + 2 * tall, rows - 1)


def relay_kernel(ring, send, out):
    cores = 2
    lat, lats = lax.axis_index("lat"), lax.axis_size("lat")
    core = lax.rem(lax.axis_index("rad"), cores)
    members, _, width = ring.shape
    tall = (ring.shape[1] - SUB) // 4
    layers = tall // 3
    coef = ring[0, 0:SUB, 0:LANES]
    for i in range(1, members):
        coef = coef + ring[i, 0:SUB, 0:LANES]
    out[0:SUB, :] = coef
    out[SUB:SUB + COEFS, :] = send[...]
    before, after = cores * jnp.maximum(lat - 1, 0) + core, cores * jnp.minimum(lat + 1, lats - 1) + core
    low_in, high_in = lat > 0, lat < lats - 1
    for j in range(width // LANES):
        base = SUB + COEFS + SUB * j
        out[base:base + SUB, :] = jnp.zeros((SUB, LANES), jnp.float32)
        for c in range(3):
            for at, member, valid, start in ((c, before, low_in, 2 * tall), (3 + c, after, high_in, 0)):
                row = SUB + start + c * layers
                bottom, top = ring[member, row:row + 1, chunk(j)], ring[member, row + layers - 1:row + layers, chunk(j)]
                out[base + at:base + at + 1, :] = jnp.where(valid, jnp.where(core == 1, top, bottom), 0.0)


def sweep_kernel(
    u, f, own1, own2, inner_s, face1, face2, ring, got, every,
    out,
    s, rim, done, cf, out_sem,
):
    layers, rows, width = u.shape[1:]
    per_row = width // LANES
    total = rows // SUB
    tall = 3 * layers
    top = layers - 1
    lat, lats = lax.axis_index("lat"), lax.axis_size("lat")
    rad, rads = lax.axis_index("rad"), lax.axis_size("rad")
    rad_odd = lax.rem(rad, 2) == 1
    cores = 2
    core = lax.rem(rad, cores)
    lower, upper = cores * jnp.maximum(lat - 1, 0), cores * jnp.minimum(lat + 1, lats - 1)
    low_in, high_in = lat > 0, lat < lats - 1
    sub8 = iota((SUB, LANES), 0)

    def side_rows(base, j):
        at = SUB + base
        low = ring[lower + core, at + 2 * tall:at + 2 * tall + layers, chunk(j)]
        high = ring[upper + core, at:at + layers, chunk(j)]
        low, high = jnp.where(low_in, low, 0.0), jnp.where(high_in, high, 0.0)
        return jnp.concatenate([low, high], axis=0)

    mate = 1 - core
    own_chip = jnp.concatenate(
        [ring[cores * lat + mate, 0:SUB, LANES:2 * LANES], ring[cores * lat + mate, 0:SUB, 2 * LANES:3 * LANES]], axis=0
    )
    other_chip = got[SUB:SUB + COEFS, :]
    lowest, highest = rad == 0, rad == rads - 1
    cf[0] = jnp.where(rad_odd, own_chip, jnp.where(lowest, 0.0, other_chip))
    cf[layers + 1] = jnp.where(rad_odd, jnp.where(highest, 0.0, other_chip), own_chip)
    for r in range(layers):
        cf[1 + r] = every[r]
    corner_low, corner_high = [], []
    for j in range(per_row):
        base = SUB + COEFS + SUB * j
        other = got[base:base + SUB, :]
        rows_own = []
        for member, valid, start in ((lower + mate, low_in, 2 * tall), (upper + mate, high_in, 0)):
            for c in range(3):
                row = SUB + start + c * layers
                near_end, far_end = ring[member, row:row + 1, chunk(j)], ring[member, row + top:row + top + 1, chunk(j)]
                rows_own.append(jnp.where(valid, jnp.where(rad_odd, far_end, near_end), 0.0))
        rows_own.append(jnp.zeros((SUB - 6, LANES), jnp.float32))
        own = jnp.concatenate(rows_own, axis=0)
        corner_low.append(jnp.where(rad_odd, own, jnp.where(lowest, 0.0, other)))
        corner_high.append(jnp.where(rad_odd, jnp.where(highest, 0.0, other), own))

    def coefficients(layer):
        return [jnp.broadcast_to(cf[layer, j:j + 1, :], (SUB, LANES)) for j in range(12)]

    near_rows = [[side_rows(c * layers, j) for j in range(per_row)] for c in range(3)]
    keep = jnp.where(sub8 < layers, jnp.where(low_in, 1.0, 0.0), jnp.where(high_in, 1.0, 0.0))
    for c in range(3):
        gain = jnp.zeros((SUB, LANES), jnp.float32)
        for r in range(layers):
            here = jnp.broadcast_to(cf[1 + r, 3 + c:4 + c, :], (SUB, LANES))
            gain = jnp.where(jnp.logical_or(sub8 == r, sub8 == layers + r), here, gain)
        for j in range(per_row):
            near = jnp.zeros((SUB, LANES), jnp.float32)
            for r in range(layers):
                head = jnp.broadcast_to(u[c, r, 0:1, chunk(j)], near.shape)
                tail = jnp.broadcast_to(u[c, r, rows - 1:rows, chunk(j)], near.shape)
                near = jnp.where(sub8 == r, head, jnp.where(sub8 == layers + r, tail, near))
            ends = (
                (0, corner_low[j][c:c + 1, :]), (layers, corner_low[j][3 + c:4 + c, :]),
                (layers - 1, corner_high[j][c:c + 1, :]), (SUB - 1, corner_high[j][3 + c:4 + c, :]),
            )
            for row, corner in ends:
                near = near + jnp.where(sub8 == row, jnp.broadcast_to(corner, near.shape), 0.0)
            value = (side_rows(tall + c * layers, j) + gain * near) * keep
            for i in range(2 * layers):
                rim[i, c, :, chunk(j)] = jnp.broadcast_to(value[i:i + 1, :], (SUB, LANES))

    def beyond(layer, side, c, j):
        if layer == 0:
            return corner_low[j][3 * side + c:3 * side + c + 1, :]
        if layer == layers + 1:
            return corner_high[j][3 * side + c:3 * side + c + 1, :]
        at = layers * side + layer - 1
        return near_rows[c][j][at:at + 1, :]

    def lo(index):
        return jnp.where(rad_odd, face1[index], face2[index])

    def hi(index):
        return jnp.where(rad_odd, face2[index], face1[index])

    for layer in range(layers + 2):
        for c in range(3):
            gain = jnp.broadcast_to(cf[layer, 3 + c:4 + c, :], (SUB, LANES))
            for j in range(per_row):
                for g in range(total):
                    at = (slice(SUB * g, SUB * g + SUB), chunk(j))
                    if layer == 0:
                        value = lo((1, c) + at) + gain * u[(c, 0) + at]
                    elif layer == layers + 1:
                        value = hi((1, c) + at) + gain * u[(c, top) + at]
                    elif layer in (1, layers):
                        here1, here2 = own1[(1, c) + at], own2[(1, c) + at]
                        value = jnp.where(rad_odd, here1, here2) if layer == 1 else jnp.where(rad_odd, here2, here1)
                    else:
                        value = inner_s[(c, layer - 2) + at]
                    if layer == 1:
                        value = value + gain * lo((0, c) + at)
                    if layer == layers:
                        value = value + gain * hi((0, c) + at)
                    if g == 0:
                        row = jnp.broadcast_to(beyond(layer, 0, c, j), value.shape)
                        value = value + jnp.where(sub8 == 0, gain * row, 0.0)
                    if g == total - 1:
                        row = jnp.broadcast_to(beyond(layer, 1, c, j), value.shape)
                        value = value + jnp.where(sub8 == SUB - 1, gain * row, 0.0)
                    s[(c, layer) + at] = value

    stores = [pltpu.make_async_copy(done.at[:, r], out.at[:, r], out_sem.at[r]) for r in range(layers)]
    for r in range(layers):
        layer = r + 1
        coef = coefficients(layer)
        for g in range(total):
            here = slice(SUB * g, SUB * g + SUB)
            values = [spans(per_row, s, c, layer, here) for c in range(3)]
            for c in range(3):
                aside = roll_columns(values[c])
                for j in range(per_row):
                    at = (c, layer)
                    if g > 0:
                        above_row = s[at + (slice(SUB * g - 1, SUB * g), chunk(j))]
                    else:
                        above_row = rim[r, c, :, chunk(j)]
                    if g < total - 1:
                        under_row = s[at + (slice(SUB * g + SUB, SUB * g + SUB + 1), chunk(j))]
                    else:
                        under_row = rim[layers + r, c, :, chunk(j)]
                    near = roll_rows(values[c][j], above_row, under_row) + aside[j]
                    near = near + (s[c, layer - 1, here, chunk(j)] + s[c, layer + 1, here, chunk(j)])
                    done[c, r, here, chunk(j)] = relax(
                        c, [values[d][j] for d in range(3)], near, f[c, r, here, chunk(j)], coef
                    )
        stores[r].start()
    for copy in stores:
        copy.wait()


def synthesis_kernel(scale, coef, rest, near, far, gains, ids, tab, out, factors):
    rows, width = ids.shape
    chunks = tab.shape[0]
    groups = tab.shape[1] // SUB
    per_row = width // LANES
    lane8 = iota((SUB, LANES), 1)
    here = (coef[...] + rest[...]) + (near[...] + far[...])
    other = pltpu.roll(here, groups, 1)
    left = lane8 < groups
    surface = jnp.where(left, here, other)
    core = jnp.where(left, other, here)
    modes = (gains[0] * surface + gains[1] * core) * scale
    zero = jnp.zeros((SUB, LANES), jnp.float32)
    for i in range(2 * groups):
        factors[i] = jnp.broadcast_to(modes[:, i:i + 1], (SUB, LANES))
    low_part = jnp.right_shift(jnp.min(ids[0:1, 0:LANES]), 7)
    high_part = jnp.right_shift(jnp.max(ids[rows - 1:rows, width - LANES:width]), 7)

    def batch(b, carry):
        parts = [low_part + b * BATCH + i for i in range(BATCH)]
        blocks = [jnp.minimum(part, chunks - 1) for part in parts]
        sums = [[zero] * BATCH for _ in range(2)]
        for g in range(groups):
            for i in range(BATCH):
                block = tab[blocks[i], SUB * g:SUB * g + SUB, :]
                for k in range(2):
                    sums[k][i] = sums[k][i] + factors[k * groups + g] * block
        for k in range(2):
            for i in range(BATCH):
                sums[k][i] = jnp.broadcast_to(jnp.sum(sums[k][i], axis=0, keepdims=True), (SUB, LANES))
        for a in range(rows // SUB):
            for j in range(per_row):
                spot = (slice(SUB * a, SUB * a + SUB), chunk(j))
                cycle = ids[spot]
                place, part = jnp.bitwise_and(cycle, LANES - 1), jnp.right_shift(cycle, 7)
                values = [zero if isinstance(b, int) else out[(k,) + spot] for k in range(2)]
                for i in range(BATCH):
                    chosen = part == parts[i]
                    for k in range(2):
                        values[k] = jnp.where(chosen, lane_gather(sums[k][i], place), values[k])
                for k in range(2):
                    out[(k,) + spot] = values[k]
        return carry

    batch(0, 0)
    lax.fori_loop(1, (high_part - low_part) // BATCH + 1, batch, 0)


def even_pairs(count):
    return [(i, i ^ 1) for i in range(count)]


def odd_pairs(count):
    pairs = []
    for i in range(1, count, 2):
        j = (i + 1) % count
        pairs += [(i, j), (j, i)]
    return pairs


def local(displacement, forcing, layer_id, stiffness, coupling, cycle_id, cycle_count, gravity):
    _, layers, rows, width = displacement.shape
    cycles, degrees = cycle_count.shape[0], gravity.shape[2]
    chunks, groups = cycles // LANES, degrees // SUB
    lats, rads, cores = lax.axis_size("lat"), lax.axis_size("rad"), 2
    if 2 * groups != LANES or 2 * layers != SUB or rads % cores or width < 3 * LANES:
        raise ValueError("unsupported sizes")
    f32 = jnp.float32
    table = jnp.asarray(basis_table(degrees, cycles))
    per_row = width // LANES
    tall = 3 * layers
    face = jax.ShapeDtypeStruct((2, 3, rows, width), f32)

    whole = jax.ShapeDtypeStruct(displacement.shape, f32)
    pinned = [
        pltpu.with_memory_space_constraint(value, pltpu.HBM)
        for value in (
            displacement, forcing, layer_id, stiffness, jnp.transpose(coupling, (1, 2, 0)), cycle_id,
            cycle_count.reshape(chunks, LANES), gravity, table,
        )
    ]
    u, f, face1, face2, mine, every, cyc, num, gain_in = pl.pallas_call(
        faces_kernel,
        out_shape=(
            whole, whole,
            face, face,
            jax.ShapeDtypeStruct((COEFS, LANES), f32),
            jax.ShapeDtypeStruct((layers, COEFS, LANES), f32),
            jax.ShapeDtypeStruct(cycle_id.shape, jnp.int32),
            jax.ShapeDtypeStruct((chunks, LANES), jnp.int32),
            jax.ShapeDtypeStruct(gravity.shape, f32),
        ),
        in_specs=[HBM] * 8,
        out_specs=(VMEM,) * 9,
        scratch_shapes=[
            pltpu.SMEM(layer_id.shape, jnp.int32),
            pltpu.SMEM(stiffness.shape, f32),
            pltpu.SMEM(coupling.shape[1:] + coupling.shape[:1], f32),
            pltpu.SemaphoreType.DMA((3,)),
            pltpu.SemaphoreType.DMA((3,)),
            pltpu.SemaphoreType.DMA((layers,)),
            pltpu.SemaphoreType.DMA((layers,)),
        ],
        compiler_params=pltpu.CompilerParams(vmem_limit_bytes=VMEM_LIMIT),
        name="faces",
    )(*pinned[:8])

    beside2 = lax.ppermute(face2, "rad", odd_pairs(rads)[:-2])
    beside1 = lax.ppermute(face1, "rad", even_pairs(rads))

    pay = pl.pallas_call(
        analysis_kernel,
        out_shape=jax.ShapeDtypeStruct((SUB + 4 * tall, width), f32),
        in_specs=[VMEM] * 7 + [HBM],
        out_specs=VMEM,
        scratch_shapes=[
            pltpu.VMEM((rows, width), f32),
            pltpu.VMEM((3, layers - 2, 2, SUB, width), f32),
            pltpu.VMEM((BATCH, degrees, LANES), f32),
            pltpu.VMEM((2, COEFS, LANES), f32),
            pltpu.VMEM((2, rows // SUB + 1, SUB, LANES), f32),
            pltpu.SemaphoreType.DMA((BATCH,)),
        ],
        compiler_params=pltpu.CompilerParams(vmem_limit_bytes=VMEM_LIMIT),
        name="analysis",
    )(u, f, face1, face2, every, cyc, num, pinned[8])

    chips = [[a * rads + b + c for a in range(lats) for c in range(cores)] for b in range(0, rads, cores)]
    ring = lax.all_gather(pay, ("lat", "rad"), axis_index_groups=chips)
    outward = pl.pallas_call(
        relay_kernel,
        out_shape=jax.ShapeDtypeStruct((SUB + COEFS + SUB * per_row, LANES), f32),
        in_specs=[VMEM] * 2,
        out_specs=VMEM,
        compiler_params=pltpu.CompilerParams(vmem_limit_bytes=VMEM_LIMIT),
        name="relay",
    )(ring, mine)
    outward, beside1, beside2 = lax.optimization_barrier((outward, beside1, beside2))
    got = lax.ppermute(outward, "rad", odd_pairs(rads))
    inner_s, gains = pl.pallas_call(
        inner_kernel,
        out_shape=(
            jax.ShapeDtypeStruct((3, layers - 2, rows, width), f32),
            jax.ShapeDtypeStruct((2, SUB, LANES), f32),
        ),
        in_specs=[VMEM] * 4,
        out_specs=(VMEM,) * 2,
        compiler_params=pltpu.CompilerParams(vmem_limit_bytes=VMEM_LIMIT),
        name="inner",
    )(u, f, every, gain_in)
    got, inner_s = lax.optimization_barrier((got, inner_s))
    coef = outward[:SUB]
    if rads == 8:
        near = lax.ppermute(coef, "rad", [(0, 3), (3, 0), (7, 4), (4, 7), (1, 5), (5, 1), (2, 6), (6, 2)])
        far = lax.ppermute(coef, "rad", [(0, 4), (4, 0), (7, 3), (3, 7), (1, 6), (6, 1), (2, 5), (5, 2)])
        rest = got[:SUB]
    else:
        coef = lax.psum(coef, "rad") * (1.0 / cores)
        near = far = rest = jnp.zeros_like(coef)

    smoothed = pl.pallas_call(
        sweep_kernel,
        out_shape=whole,
        in_specs=[VMEM] * 10,
        out_specs=HBM,
        scratch_shapes=[
            pltpu.VMEM((3, layers + 2, rows, width), f32),
            pltpu.VMEM((2 * layers, 3, SUB, width), f32),
            pltpu.VMEM((3, layers, rows, width), f32),
            pltpu.VMEM((layers + 2, COEFS, LANES), f32),
            pltpu.SemaphoreType.DMA((layers,)),
        ],
        compiler_params=pltpu.CompilerParams(vmem_limit_bytes=VMEM_LIMIT),
        name="sweeps",
    )(u, f, face1, face2, inner_s, beside1, beside2, ring, got, every)
    coef, smoothed = lax.optimization_barrier((coef, smoothed))

    potential = pl.pallas_call(
        functools.partial(synthesis_kernel, 2.0 / cycles),
        out_shape=jax.ShapeDtypeStruct((2, rows, width), f32),
        in_specs=[VMEM] * 7,
        out_specs=VMEM,
        scratch_shapes=[pltpu.VMEM((2 * groups, SUB, LANES), f32)],
        compiler_params=pltpu.CompilerParams(vmem_limit_bytes=VMEM_LIMIT),
        name="synthesis",
    )(coef, rest, near, far, gains, cyc, table)
    return smoothed, potential


def solution(mesh):
    in_specs = (
        P(None, "rad", "lat", None),
        P(None, "rad", "lat", None),
        P("rad"),
        P(),
        P(),
        P("lat", None),
        P(),
        P(),
    )
    out_specs = (P(None, "rad", "lat", None), P(None, "lat", None))
    return jax.shard_map(local, mesh=mesh, in_specs=in_specs, out_specs=out_specs, check_vma=False)
```

```python
import functools
import math

import jax
import jax.numpy as jnp
import numpy as np
from jax import lax
from jax.experimental import pallas as pl
from jax.experimental.pallas import tpu as pltpu
from jax.sharding import PartitionSpec as P

SWEEPS = 2
OMEGA = 0.8
LEAST_COUNT = 32
LANES = 128
SUB = 8
PAD = 8
COEFS = 16
BATCH = 5
VMEM_LIMIT = 16 * 1024 * 1024

VMEM = pl.BlockSpec(memory_space=pltpu.VMEM)
SMEM = pl.BlockSpec(memory_space=pltpu.SMEM)
HBM = pl.BlockSpec(memory_space=pltpu.HBM)
ANY = pl.BlockSpec(memory_space=pl.ANY)


def basis_table(degrees, cycles):
    groups = degrees // SUB
    degree = np.arange(degrees, dtype=np.int64)[:, None]
    cycle = np.arange(cycles, dtype=np.int64)[None, :]
    phase = degree * (2 * cycle + 1) % (4 * cycles)
    table = np.cos(np.pi * phase / (2.0 * cycles)).astype(np.float32)
    table = table.reshape(SUB, groups, cycles // LANES, LANES).transpose(2, 1, 0, 3)
    return np.ascontiguousarray(table.reshape(cycles // LANES, degrees, LANES))


def iota(shape, dim):
    return lax.broadcasted_iota(jnp.int32, shape, dim)


def lane_gather(values, index):
    return jnp.take_along_axis(values, index, axis=1, mode="promise_in_bounds")


def layer_scalars(layer, lid, stiff, coup):
    material = lid[layer]
    mu = stiff[material]
    return mu, [[coup[c, d, material] for d in range(3)] for c in range(3)]


def coefficient_rows(mu, k, width=LANES):
    row = iota((COEFS, width), 0)
    top = jnp.zeros((COEFS, width), jnp.float32)
    below = jnp.ones((COEFS, width), jnp.float32)
    for c in range(3):
        diag = 6.0 * mu + k[c][c]
        others = [d for d in range(3) if d != c]
        entries = [(c, 1.0), (3 + c, mu), (6 + 2 * c, k[c][others[0]]), (7 + 2 * c, k[c][others[1]])]
        for at, value in entries:
            top = jnp.where(row == at, OMEGA * value, top)
            below = jnp.where(row == at, diag, below)
    return top / below


def roll_rows(value, before, after):
    sub = iota(value.shape, 0)
    up = jnp.where(sub == 0, jnp.broadcast_to(before, value.shape), pltpu.roll(value, 1, 0))
    down = jnp.where(sub == SUB - 1, jnp.broadcast_to(after, value.shape), pltpu.roll(value, SUB - 1, 0))
    return up + down


def roll_columns(values):
    lane = iota(values[0].shape, 1)
    right = [pltpu.roll(value, 1, 1) for value in values]
    left = [pltpu.roll(value, LANES - 1, 1) for value in values]
    last = len(values) - 1
    return [
        jnp.where(lane == 0, right[j - 1] if j > 0 else 0.0, right[j])
        + jnp.where(lane == LANES - 1, left[j + 1] if j < last else 0.0, left[j])
        for j in range(len(values))
    ]


def relax(c, centers, neighbours, force, rows):
    d0, d1 = [d for d in range(3) if d != c]
    value = rows[c] * force + rows[3 + c] * neighbours
    value = value - (rows[6 + 2 * c] * centers[d0] + rows[7 + 2 * c] * centers[d1])
    return value + (1.0 - OMEGA) * centers[c]


def chunk(j):
    return pl.ds(LANES * j, LANES)


def spans(per_row, ref, *index):
    return [ref[index + (chunk(j),)] for j in range(per_row)]


def lane_scan(values, steps):
    lane = iota(values.shape, 1)
    step = 1
    while step < steps:
        values = values + jnp.where(lane >= step, pltpu.roll(values, step, 1), 0)
        step *= 2
    return values


def local_sweep(u, f, every, layer, beside, store, groups=None, parts=(0, 1, 2)):
    rows, width = u.shape[2:]
    per_row, total = width // LANES, rows // SUB
    coef = [jnp.broadcast_to(every[layer, j:j + 1, :], (SUB, LANES)) for j in range(12)]
    none = jnp.zeros((1, LANES), jnp.float32)
    for g in range(total) if groups is None else groups:
        here = slice(SUB * g, SUB * g + SUB)
        values = [spans(per_row, u, c, layer, here) for c in range(3)]
        for c in parts:
            aside = roll_columns(values[c])
            for j in range(per_row):
                at = (c, layer)
                above = u[at + (slice(SUB * g - 1, SUB * g), chunk(j))] if g > 0 else none
                under = u[at + (slice(SUB * g + SUB, SUB * g + SUB + 1), chunk(j))] if g < total - 1 else none
                near = roll_rows(values[c][j], above, under) + aside[j]
                for other in beside:
                    near = near + u[c, other, here, chunk(j)]
                value = relax(c, [values[d][j] for d in range(3)], near, f[c, layer, here, chunk(j)], coef)
                store(c, g, j, values[c][j], value)


def faces_kernel(
    disp, forc, lid, stiff, coup, ids, cnt, grav,
    u, f, face1, face2, send, every, cyc, num, gain_in,
    lids, stiffs, coups, small_sem, near_sem, u_sem, f_sem,
):
    layers = disp.shape[1]
    top = layers - 1
    odd = lax.rem(lax.axis_index("rad"), 2) == 1
    small = [
        pltpu.make_async_copy(lid, lids, small_sem.at[0]),
        pltpu.make_async_copy(stiff, stiffs, small_sem.at[1]),
        pltpu.make_async_copy(coup, coups, small_sem.at[2]),
    ]
    cycles = [
        pltpu.make_async_copy(cnt, num, near_sem.at[0]),
        pltpu.make_async_copy(ids, cyc, near_sem.at[1]),
        pltpu.make_async_copy(grav, gain_in, near_sem.at[2]),
    ]
    loads_u = [pltpu.make_async_copy(disp.at[:, r], u.at[:, r], u_sem.at[r]) for r in range(layers)]
    loads_f = [pltpu.make_async_copy(forc.at[:, r], f.at[:, r], f_sem.at[r]) for r in range(layers)]
    for copy in small:
        copy.start()
    for r in [0, 1, top] + list(range(top - 1, 1, -1)):
        loads_u[r].start()
        if r in (0, top):
            loads_f[r].start()
    for r in range(1, top):
        loads_f[r].start()
    for copy in cycles:
        copy.start()
    for copy in small:
        copy.wait()
    for r in range(layers):
        every[r] = coefficient_rows(*layer_scalars(r, lids, stiffs, coups))
    send[...] = every[jnp.where(odd, top, 0)]

    for copy in loads_u + [loads_f[0], loads_f[top]]:
        copy.wait()
    for face, layer in ((face1, jnp.where(odd, 0, top)), (face2, jnp.where(odd, top, 0))):
        def store(c, g, j, value, swept, face=face):
            at = (c, slice(SUB * g, SUB * g + SUB), chunk(j))
            face[(0,) + at] = value
            face[(1,) + at] = swept

        local_sweep(u, f, every, layer, (jnp.where(layer == 0, 1, top - 1),), store)
    for copy in loads_f[1:top] + cycles:
        copy.wait()


def inner_kernel(u, f, every, gain_in, inner_s, gains):
    groups = gain_in.shape[2] // SUB

    def middle(r, carry):
        def store(c, g, j, value, swept):
            inner_s[c, r - 1, SUB * g:SUB * g + SUB, chunk(j)] = swept

        local_sweep(u, f, every, r, (r - 1, r + 1), store)
        return carry

    lax.fori_loop(1, u.shape[1] - 1, middle, 0)

    lane1 = iota((1, LANES), 1)
    for load in range(2):
        for m in range(groups * SUB // LANES):
            one, two = gain_in[0, load:load + 1, chunk(m)], gain_in[1, load:load + 1, chunk(m)]
            gains[load, 2 * m:2 * m + 1, :] = jnp.where(lane1 < groups, one, pltpu.roll(two, groups, 1))
            gains[load, 2 * m + 1:2 * m + 2, :] = jnp.where(lane1 < groups, pltpu.roll(one, groups, 1), two)


def analysis_kernel(
    u, f, face1, face2, every, cyc, num, tbl,
    pay,
    plane, rims, tab, mat, windows, tab_sem,
):
    layers, rows, width = u.shape[1:]
    chunks = num.shape[0]
    groups = tbl.shape[1] // SUB
    per_row = width // LANES
    lat, lats = lax.axis_index("lat"), lax.axis_size("lat")
    rad, rads = lax.axis_index("rad"), lax.axis_size("rad")
    bottom = rad == 0
    at_end = jnp.logical_or(bottom, rad == rads - 1)
    top = layers - 1
    edge, inner = jnp.where(bottom, 0, top), jnp.where(bottom, 1, top - 1)
    total = rows // SUB
    odd = lax.rem(rad, 2) == 1
    at_core = every[jnp.where(odd, 0, top)]
    reach = 2 * width // LEAST_COUNT + 2
    low_part = jnp.right_shift(jnp.maximum(jnp.min(cyc[0:1, 0:LANES]) - reach, 0), 7)
    high_part = jnp.right_shift(jnp.max(cyc[rows - 1:rows, width - LANES:width]) + reach, 7)
    high_part = jnp.minimum(high_part, chunks - 1)

    def table(b):
        return [
            pltpu.make_async_copy(
                tbl.at[jnp.minimum(low_part + b * BATCH + i, chunks - 1)], tab.at[i], tab_sem.at[i]
            )
            for i in range(BATCH)
        ]

    @pl.when(at_end)
    def _():
        for copy in table(0):
            copy.start()

    for r in range(1, top):
        def store(c, g, j, value, swept, r=r):
            rims[c, r - 1, 0 if g == 0 else 1, :, chunk(j)] = swept

        local_sweep(u, f, every, r, (r - 1, r + 1), store, groups=(0, total - 1))

    sub8, lane8 = iota((SUB, LANES), 0), iota((SUB, LANES), 1)
    before = sub8 < 2
    zero = jnp.zeros((SUB, LANES), jnp.float32)
    pay[0:SUB, 0:LANES] = jnp.zeros((SUB, LANES), jnp.float32)
    pay[0:SUB, LANES:2 * LANES] = at_core[0:SUB]
    pay[0:SUB, 2 * LANES:3 * LANES] = at_core[SUB:]

    @pl.when(at_end)
    def _():
        def keep_plane(c, g, j, value, swept):
            plane[SUB * g:SUB * g + SUB, chunk(j)] = swept

        local_sweep(u, f, every, inner, (inner - 1, inner + 1), keep_plane, parts=(0,))
        first = jnp.broadcast_to(cyc[0:1, 0:1], (SUB, LANES))
        last = jnp.broadcast_to(cyc[rows - 1:rows, width - 1:width], (SUB, LANES))
        own_first = jnp.zeros((SUB, LANES), jnp.int32)
        own_last = own_first
        for j in range(per_row):
            own_first = own_first + jnp.where(cyc[0:SUB, LANES * j:LANES * j + LANES] == first, 1, 0)
            own_last = own_last + jnp.where(cyc[rows - SUB:rows, LANES * j:LANES * j + LANES] == last, 1, 0)

        def total_of(count):
            count = jnp.sum(count.astype(jnp.float32), axis=1, keepdims=True)
            return jnp.broadcast_to(jnp.sum(count, axis=0, keepdims=True), (SUB, LANES)).astype(jnp.int32)

        held_here = jnp.where(before, total_of(own_first), total_of(own_last))
        index = jnp.where(before, first - lane8, last + lane8)
        place, part = jnp.bitwise_and(index, LANES - 1), jnp.right_shift(index, 7)
        lengths = jnp.full((SUB, LANES), 2 ** 20, jnp.int32)
        for q in range(chunks):
            row = jnp.broadcast_to(num[q:q + 1, :], (SUB, LANES))
            lengths = jnp.where(part == q, lane_gather(row, place), lengths)
        lengths = lengths - jnp.where(lane8 == 0, held_here, 0)
        limits = lane_scan(lengths, reach)
        caps = [jnp.broadcast_to(limits[:, i:i + 1], (SUB, LANES)) for i in range(reach)]
        spill_ids = []
        for j in range(per_row):
            column = LANES * j + lane8
            away = jnp.where(before, (width - 1 - column) + jnp.where(sub8 == 0, width, 0),
                             column + jnp.where(sub8 == 3, width, 0))
            passed = jnp.zeros((SUB, LANES), jnp.int32)
            for i in range(reach):
                passed = passed + jnp.where(away >= caps[i], 1, 0)
            spill_ids.append(jnp.where(sub8 < 4, jnp.where(before, first - passed, last + passed), 0))

        mat[0] = every[edge]
        mat[1] = every[inner]
        outer = [jnp.broadcast_to(mat[0, j:j + 1, :], (SUB, LANES)) for j in range(12)]
        below = [jnp.broadcast_to(mat[1, j:j + 1, :], (SUB, LANES)) for j in range(12)]

        def rows_of(g):
            return slice(SUB * g, SUB * g + SUB)

        def lateral(ref, g, index, ends):
            values = spans(per_row, ref, *index, rows_of(g))
            aside = roll_columns(values)
            out = []
            for j in range(per_row):
                above = ref[index + (slice(SUB * g - 1, SUB * g), chunk(j))] if g > 0 else ends[0][j]
                under = ref[index + (slice(SUB * g + SUB, SUB * g + SUB + 1), chunk(j))] if g < total - 1 else ends[1][j]
                out.append(roll_rows(values[j], above, under) + aside[j])
            return out

        low_in = jnp.where(lat > 0, 1.0, 0.0)
        high_in = jnp.where(lat < lats - 1, 1.0, 0.0)
        weight = jnp.where(sub8 == 1, low_in, jnp.where(sub8 == 2, high_in, 0.0))

        def ends_of(ref, index, j):
            low = jnp.broadcast_to(ref[index + (slice(0, 1), chunk(j))], (SUB, LANES))
            high = jnp.broadcast_to(ref[index + (slice(rows - 1, rows), chunk(j))], (SUB, LANES))
            return jnp.where(sub8 == 1, low, jnp.where(sub8 == 2, high, 0.0))

        over = [[outer[3 + c] * ends_of(u, (c, edge), j) * weight for j in range(per_row)] for c in range(3)]
        over_inner = [below[3] * ends_of(u, (0, inner), j) * weight for j in range(per_row)]
        aside = roll_columns(over[0])
        spill = []
        for j in range(per_row):
            shifted = jnp.where(sub8 == 0, pltpu.roll(over[0][j], SUB - 1, 0),
                                jnp.where(sub8 == 3, pltpu.roll(over[0][j], 1, 0), 0.0))
            near = over_inner[j] + aside[j] + shifted + ends_of(face2, (1, 0), j)
            value = relax(0, [over[c][j] for c in range(3)], near, zero, outer)
            spill.append(value * jnp.where(before, low_in, high_in))
        ends = [[over[0][j][1:2, :] for j in range(per_row)], [over[0][j][2:3, :] for j in range(per_row)]]

        met = (width - 2) // LEAST_COUNT + 2

        def window_of(values, cycles):
            start = jnp.broadcast_to(cycles[0][:, 0:1], (SUB, LANES))
            offsets = [cycle - start for cycle in cycles]
            window = zero
            for t in range(met):
                picked = [jnp.where(offset == t, value, 0.0) for offset, value in zip(offsets, values)]
                sum_t = jnp.sum(functools.reduce(jnp.add, picked), axis=1, keepdims=True)
                window = jnp.where(lane8 == t, jnp.broadcast_to(sum_t, (SUB, LANES)), window)
            return window, start

        windowed = [window_of(spill, spill_ids)]
        for g in range(total):
            here = rows_of(g)
            centers = [spans(per_row, face2, 1, c, here) for c in range(3)]
            near = lateral(face2, g, (1, 0), ends)
            inners = spans(per_row, plane, here)
            force = spans(per_row, f, 0, edge, here)
            values = [
                relax(0, [center[j] for center in centers], near[j] + inners[j], force[j], outer)
                for j in range(per_row)
            ]
            windowed.append(window_of(values, spans(per_row, cyc, here)))
        for i, (window, start) in enumerate(windowed):
            windows[0, i] = window
            windows[1, i] = start.astype(jnp.float32)

        half = jnp.where(bottom, groups, 0)


        def batch(b, result):
            @pl.when(b > 0)
            def _():
                for copy in table(b):
                    copy.start()

            means = []
            for i in range(BATCH):
                q = low_part + b * BATCH + i
                part = jnp.minimum(q, chunks - 1)
                acc = zero
                for w in range(total + 1):
                    at = q * LANES + lane8 - windows[1, w].astype(jnp.int32)
                    got = lane_gather(windows[0, w], jnp.bitwise_and(at, LANES - 1))
                    acc = acc + jnp.where(jnp.right_shift(at, 7) == 0, got, 0.0)
                mean = jnp.sum(acc, axis=0, keepdims=True) / num[pl.ds(part, 1), :].astype(jnp.float32)
                mean = jnp.where(q < chunks, mean, 0.0)
                means.append(jnp.broadcast_to(mean, (SUB, LANES)))
            for copy in table(b):
                copy.wait()
            for g in range(groups):
                acc = tab[0, SUB * g:SUB * g + SUB, :] * means[0]
                for i in range(1, BATCH):
                    acc = acc + tab[i, SUB * g:SUB * g + SUB, :] * means[i]
                column = jnp.broadcast_to(jnp.sum(acc, axis=1, keepdims=True), (SUB, LANES))
                result = jnp.where(lane8 == g + half, result + column, result)
            return result

        pay[0:SUB, 0:LANES] = lax.fori_loop(0, (high_part - low_part) // BATCH + 1, batch, zero)

    tall = 3 * layers

    def pack(ref, base, near):
        for c in range(3):
            for r in range(layers):
                at = base + c * layers + r
                ref[at:at + 1, :] = u[c, r, near:near + 1, :]
                if r == 0:
                    row = jnp.where(odd, face1[1, c, near:near + 1, :], face2[1, c, near:near + 1, :])
                elif r == top:
                    row = jnp.where(odd, face2[1, c, near:near + 1, :], face1[1, c, near:near + 1, :])
                else:
                    row = rims[c, r - 1, near // (rows - 1), near % SUB:near % SUB + 1, :]
                ref[at + tall:at + tall + 1, :] = row

    pack(pay, SUB, 0)
    pack(pay, SUB + 2 * tall, rows - 1)


def first_chunk(cyc):
    return jnp.right_shift(jnp.min(cyc[0:1, 0:LANES]), 7)


def relay_kernel(ring, send, out):
    cores = 2
    lat, lats = lax.axis_index("lat"), lax.axis_size("lat")
    core = lax.rem(lax.axis_index("rad"), cores)
    members, _, width = ring.shape
    tall = (ring.shape[1] - SUB) // 4
    layers = tall // 3
    coef = ring[0, 0:SUB, 0:LANES]
    for i in range(1, members):
        coef = coef + ring[i, 0:SUB, 0:LANES]
    out[0:SUB, :] = coef
    out[SUB:SUB + COEFS, :] = send[...]
    before, after = cores * jnp.maximum(lat - 1, 0) + core, cores * jnp.minimum(lat + 1, lats - 1) + core
    low_in, high_in = lat > 0, lat < lats - 1
    for j in range(width // LANES):
        base = SUB + COEFS + SUB * j
        out[base:base + SUB, :] = jnp.zeros((SUB, LANES), jnp.float32)
        for c in range(3):
            for at, member, valid, start in ((c, before, low_in, 2 * tall), (3 + c, after, high_in, 0)):
                row = SUB + start + c * layers
                bottom, top = ring[member, row:row + 1, chunk(j)], ring[member, row + layers - 1:row + layers, chunk(j)]
                out[base + at:base + at + 1, :] = jnp.where(valid, jnp.where(core == 1, top, bottom), 0.0)


def sweep_kernel(
    u, f, own1, own2, inner_s, face1, face2, ring, got, every, cyc, tbl,
    out, tab,
    s, rim, done, cf, out_sem, tab_sem,
):
    layers, rows, width = u.shape[1:]
    per_row = width // LANES
    first = first_chunk(cyc)
    table = [
        pltpu.make_async_copy(tbl.at[jnp.minimum(first + i, tbl.shape[0] - 1)], tab.at[i], tab_sem.at[i])
        for i in range(BATCH)
    ]
    for copy in table:
        copy.start()
    total = rows // SUB
    tall = 3 * layers
    top = layers - 1
    lat, lats = lax.axis_index("lat"), lax.axis_size("lat")
    rad, rads = lax.axis_index("rad"), lax.axis_size("rad")
    rad_odd = lax.rem(rad, 2) == 1
    cores = 2
    core = lax.rem(rad, cores)
    lower, upper = cores * jnp.maximum(lat - 1, 0), cores * jnp.minimum(lat + 1, lats - 1)
    low_in, high_in = lat > 0, lat < lats - 1
    sub8 = iota((SUB, LANES), 0)

    def side_rows(base, j):
        at = SUB + base
        low = ring[lower + core, at + 2 * tall:at + 2 * tall + layers, chunk(j)]
        high = ring[upper + core, at:at + layers, chunk(j)]
        low, high = jnp.where(low_in, low, 0.0), jnp.where(high_in, high, 0.0)
        return jnp.concatenate([low, high], axis=0)

    mate = 1 - core
    own_chip = jnp.concatenate(
        [ring[cores * lat + mate, 0:SUB, LANES:2 * LANES], ring[cores * lat + mate, 0:SUB, 2 * LANES:3 * LANES]], axis=0
    )
    other_chip = got[SUB:SUB + COEFS, :]
    lowest, highest = rad == 0, rad == rads - 1
    cf[0] = jnp.where(rad_odd, own_chip, jnp.where(lowest, 0.0, other_chip))
    cf[layers + 1] = jnp.where(rad_odd, jnp.where(highest, 0.0, other_chip), own_chip)
    for r in range(layers):
        cf[1 + r] = every[r]
    corner_low, corner_high = [], []
    for j in range(per_row):
        base = SUB + COEFS + SUB * j
        other = got[base:base + SUB, :]
        rows_own = []
        for member, valid, start in ((lower + mate, low_in, 2 * tall), (upper + mate, high_in, 0)):
            for c in range(3):
                row = SUB + start + c * layers
                near_end, far_end = ring[member, row:row + 1, chunk(j)], ring[member, row + top:row + top + 1, chunk(j)]
                rows_own.append(jnp.where(valid, jnp.where(rad_odd, far_end, near_end), 0.0))
        rows_own.append(jnp.zeros((SUB - 6, LANES), jnp.float32))
        own = jnp.concatenate(rows_own, axis=0)
        corner_low.append(jnp.where(rad_odd, own, jnp.where(lowest, 0.0, other)))
        corner_high.append(jnp.where(rad_odd, jnp.where(highest, 0.0, other), own))

    def coefficients(layer):
        return [jnp.broadcast_to(cf[layer, j:j + 1, :], (SUB, LANES)) for j in range(12)]

    near_rows = [[side_rows(c * layers, j) for j in range(per_row)] for c in range(3)]
    keep = jnp.where(sub8 < layers, jnp.where(low_in, 1.0, 0.0), jnp.where(high_in, 1.0, 0.0))
    for c in range(3):
        gain = jnp.zeros((SUB, LANES), jnp.float32)
        for r in range(layers):
            here = jnp.broadcast_to(cf[1 + r, 3 + c:4 + c, :], (SUB, LANES))
            gain = jnp.where(jnp.logical_or(sub8 == r, sub8 == layers + r), here, gain)
        for j in range(per_row):
            near = jnp.zeros((SUB, LANES), jnp.float32)
            for r in range(layers):
                head = jnp.broadcast_to(u[c, r, 0:1, chunk(j)], near.shape)
                tail = jnp.broadcast_to(u[c, r, rows - 1:rows, chunk(j)], near.shape)
                near = jnp.where(sub8 == r, head, jnp.where(sub8 == layers + r, tail, near))
            ends = (
                (0, corner_low[j][c:c + 1, :]), (layers, corner_low[j][3 + c:4 + c, :]),
                (layers - 1, corner_high[j][c:c + 1, :]), (SUB - 1, corner_high[j][3 + c:4 + c, :]),
            )
            for row, corner in ends:
                near = near + jnp.where(sub8 == row, jnp.broadcast_to(corner, near.shape), 0.0)
            value = (side_rows(tall + c * layers, j) + gain * near) * keep
            for i in range(2 * layers):
                rim[i, c, :, chunk(j)] = jnp.broadcast_to(value[i:i + 1, :], (SUB, LANES))

    def beyond(layer, side, c, j):
        if layer == 0:
            return corner_low[j][3 * side + c:3 * side + c + 1, :]
        if layer == layers + 1:
            return corner_high[j][3 * side + c:3 * side + c + 1, :]
        at = layers * side + layer - 1
        return near_rows[c][j][at:at + 1, :]

    def lo(index):
        return jnp.where(rad_odd, face1[index], face2[index])

    def hi(index):
        return jnp.where(rad_odd, face2[index], face1[index])

    for layer in range(layers + 2):
        for c in range(3):
            gain = jnp.broadcast_to(cf[layer, 3 + c:4 + c, :], (SUB, LANES))
            for j in range(per_row):
                for g in range(total):
                    at = (slice(SUB * g, SUB * g + SUB), chunk(j))
                    if layer == 0:
                        value = lo((1, c) + at) + gain * u[(c, 0) + at]
                    elif layer == layers + 1:
                        value = hi((1, c) + at) + gain * u[(c, top) + at]
                    elif layer in (1, layers):
                        here1, here2 = own1[(1, c) + at], own2[(1, c) + at]
                        value = jnp.where(rad_odd, here1, here2) if layer == 1 else jnp.where(rad_odd, here2, here1)
                    else:
                        value = inner_s[(c, layer - 2) + at]
                    if layer == 1:
                        value = value + gain * lo((0, c) + at)
                    if layer == layers:
                        value = value + gain * hi((0, c) + at)
                    if g == 0:
                        row = jnp.broadcast_to(beyond(layer, 0, c, j), value.shape)
                        value = value + jnp.where(sub8 == 0, gain * row, 0.0)
                    if g == total - 1:
                        row = jnp.broadcast_to(beyond(layer, 1, c, j), value.shape)
                        value = value + jnp.where(sub8 == SUB - 1, gain * row, 0.0)
                    s[(c, layer) + at] = value

    stores = [pltpu.make_async_copy(done.at[:, r], out.at[:, r], out_sem.at[r]) for r in range(layers)]
    for r in range(layers):
        layer = r + 1
        coef = coefficients(layer)
        for g in range(total):
            here = slice(SUB * g, SUB * g + SUB)
            values = [spans(per_row, s, c, layer, here) for c in range(3)]
            for c in range(3):
                aside = roll_columns(values[c])
                for j in range(per_row):
                    at = (c, layer)
                    if g > 0:
                        above_row = s[at + (slice(SUB * g - 1, SUB * g), chunk(j))]
                    else:
                        above_row = rim[r, c, :, chunk(j)]
                    if g < total - 1:
                        under_row = s[at + (slice(SUB * g + SUB, SUB * g + SUB + 1), chunk(j))]
                    else:
                        under_row = rim[layers + r, c, :, chunk(j)]
                    near = roll_rows(values[c][j], above_row, under_row) + aside[j]
                    near = near + (s[c, layer - 1, here, chunk(j)] + s[c, layer + 1, here, chunk(j)])
                    done[c, r, here, chunk(j)] = relax(
                        c, [values[d][j] for d in range(3)], near, f[c, r, here, chunk(j)], coef
                    )
        stores[r].start()
    for copy in stores + table:
        copy.wait()


def synthesis_kernel(scale, coef, rest, near, far, gains, ids, tab, tbl, out, factors, more, more_sem):
    rows, width = ids.shape
    chunks = tbl.shape[0]
    groups = tab.shape[1] // SUB
    per_row = width // LANES
    lane8 = iota((SUB, LANES), 1)
    here = (coef[...] + rest[...]) + (near[...] + far[...])
    other = pltpu.roll(here, groups, 1)
    left = lane8 < groups
    surface = jnp.where(left, here, other)
    core = jnp.where(left, other, here)
    modes = (gains[0] * surface + gains[1] * core) * scale
    zero = jnp.zeros((SUB, LANES), jnp.float32)
    for i in range(2 * groups):
        factors[i] = jnp.broadcast_to(modes[:, i:i + 1], (SUB, LANES))
    low_part = first_chunk(ids)
    high_part = jnp.right_shift(jnp.max(ids[rows - 1:rows, width - LANES:width]), 7)

    def batch(b, carry):
        parts = [low_part + b * BATCH + i for i in range(BATCH)]
        source = tab
        if not isinstance(b, int):
            source = more
            copies = [
                pltpu.make_async_copy(tbl.at[jnp.minimum(part, chunks - 1)], more.at[i], more_sem.at[i])
                for i, part in enumerate(parts)
            ]
            for copy in copies:
                copy.start()
            for copy in copies:
                copy.wait()
        sums = [[zero] * BATCH for _ in range(2)]
        for g in range(groups):
            for i in range(BATCH):
                block = source[i, SUB * g:SUB * g + SUB, :]
                for k in range(2):
                    sums[k][i] = sums[k][i] + factors[k * groups + g] * block
        for k in range(2):
            for i in range(BATCH):
                sums[k][i] = jnp.broadcast_to(jnp.sum(sums[k][i], axis=0, keepdims=True), (SUB, LANES))
        for a in range(rows // SUB):
            for j in range(per_row):
                spot = (slice(SUB * a, SUB * a + SUB), chunk(j))
                cycle = ids[spot]
                place, part = jnp.bitwise_and(cycle, LANES - 1), jnp.right_shift(cycle, 7)
                values = [zero if isinstance(b, int) else out[(k,) + spot] for k in range(2)]
                for i in range(BATCH):
                    chosen = part == parts[i]
                    for k in range(2):
                        values[k] = jnp.where(chosen, lane_gather(sums[k][i], place), values[k])
                for k in range(2):
                    out[(k,) + spot] = values[k]
        return carry

    batch(0, 0)
    lax.fori_loop(1, (high_part - low_part) // BATCH + 1, batch, 0)


def even_pairs(count):
    return [(i, i ^ 1) for i in range(count)]


def odd_pairs(count):
    pairs = []
    for i in range(1, count, 2):
        j = (i + 1) % count
        pairs += [(i, j), (j, i)]
    return pairs


def local(displacement, forcing, layer_id, stiffness, coupling, cycle_id, cycle_count, gravity):
    _, layers, rows, width = displacement.shape
    cycles, degrees = cycle_count.shape[0], gravity.shape[2]
    chunks, groups = cycles // LANES, degrees // SUB
    lats, rads, cores = lax.axis_size("lat"), lax.axis_size("rad"), 2
    if 2 * groups != LANES or 2 * layers != SUB or rads % cores or width < 3 * LANES:
        raise ValueError("unsupported sizes")
    f32 = jnp.float32
    table = jnp.asarray(basis_table(degrees, cycles))
    per_row = width // LANES
    tall = 3 * layers
    face = jax.ShapeDtypeStruct((2, 3, rows, width), f32)

    whole = jax.ShapeDtypeStruct(displacement.shape, f32)
    pinned = [
        pltpu.with_memory_space_constraint(value, pltpu.HBM)
        for value in (
            displacement, forcing, layer_id, stiffness, jnp.transpose(coupling, (1, 2, 0)), cycle_id,
            cycle_count.reshape(chunks, LANES), gravity, table,
        )
    ]
    u, f, face1, face2, mine, every, cyc, num, gain_in = pl.pallas_call(
        faces_kernel,
        out_shape=(
            whole, whole,
            face, face,
            jax.ShapeDtypeStruct((COEFS, LANES), f32),
            jax.ShapeDtypeStruct((layers, COEFS, LANES), f32),
            jax.ShapeDtypeStruct(cycle_id.shape, jnp.int32),
            jax.ShapeDtypeStruct((chunks, LANES), jnp.int32),
            jax.ShapeDtypeStruct(gravity.shape, f32),
        ),
        in_specs=[HBM] * 8,
        out_specs=(VMEM,) * 9,
        scratch_shapes=[
            pltpu.SMEM(layer_id.shape, jnp.int32),
            pltpu.SMEM(stiffness.shape, f32),
            pltpu.SMEM(coupling.shape[1:] + coupling.shape[:1], f32),
            pltpu.SemaphoreType.DMA((3,)),
            pltpu.SemaphoreType.DMA((3,)),
            pltpu.SemaphoreType.DMA((layers,)),
            pltpu.SemaphoreType.DMA((layers,)),
        ],
        compiler_params=pltpu.CompilerParams(vmem_limit_bytes=VMEM_LIMIT),
        name="faces",
    )(*pinned[:8])

    beside2 = lax.ppermute(face2, "rad", odd_pairs(rads)[:-2])
    beside1 = lax.ppermute(face1, "rad", even_pairs(rads))

    pay = pl.pallas_call(
        analysis_kernel,
        out_shape=jax.ShapeDtypeStruct((SUB + 4 * tall, width), f32),
        in_specs=[VMEM] * 7 + [HBM],
        out_specs=VMEM,
        scratch_shapes=[
            pltpu.VMEM((rows, width), f32),
            pltpu.VMEM((3, layers - 2, 2, SUB, width), f32),
            pltpu.VMEM((BATCH, degrees, LANES), f32),
            pltpu.VMEM((2, COEFS, LANES), f32),
            pltpu.VMEM((2, rows // SUB + 1, SUB, LANES), f32),
            pltpu.SemaphoreType.DMA((BATCH,)),
        ],
        compiler_params=pltpu.CompilerParams(vmem_limit_bytes=VMEM_LIMIT),
        name="analysis",
    )(u, f, face1, face2, every, cyc, num, pinned[8])

    chips = [[a * rads + b + c for a in range(lats) for c in range(cores)] for b in range(0, rads, cores)]
    ring = lax.all_gather(pay, ("lat", "rad"), axis_index_groups=chips)
    outward = pl.pallas_call(
        relay_kernel,
        out_shape=jax.ShapeDtypeStruct((SUB + COEFS + SUB * per_row, LANES), f32),
        in_specs=[VMEM] * 2,
        out_specs=VMEM,
        compiler_params=pltpu.CompilerParams(vmem_limit_bytes=VMEM_LIMIT),
        name="relay",
    )(ring, mine)
    outward, beside1, beside2 = lax.optimization_barrier((outward, beside1, beside2))
    got = lax.ppermute(outward, "rad", odd_pairs(rads))
    inner_s, gains = pl.pallas_call(
        inner_kernel,
        out_shape=(
            jax.ShapeDtypeStruct((3, layers - 2, rows, width), f32),
            jax.ShapeDtypeStruct((2, SUB, LANES), f32),
        ),
        in_specs=[VMEM] * 4,
        out_specs=(VMEM,) * 2,
        compiler_params=pltpu.CompilerParams(vmem_limit_bytes=VMEM_LIMIT),
        name="inner",
    )(u, f, every, gain_in)
    got, inner_s = lax.optimization_barrier((got, inner_s))
    coef = outward[:SUB]
    if rads == 8:
        far = lax.ppermute(coef, "rad", [(0, 4), (4, 0), (7, 3), (3, 7), (1, 6), (6, 1), (2, 5), (5, 2)])
        near = lax.ppermute(coef, "rad", [(0, 3), (3, 0), (7, 4), (4, 7), (1, 5), (5, 1), (2, 6), (6, 2)])
        rest = got[:SUB]
    else:
        coef = lax.psum(coef, "rad") * (1.0 / cores)
        near = far = rest = jnp.zeros_like(coef)

    smoothed, tab = pl.pallas_call(
        sweep_kernel,
        out_shape=(whole, jax.ShapeDtypeStruct((BATCH, degrees, LANES), f32)),
        in_specs=[VMEM] * 11 + [HBM],
        out_specs=(HBM, VMEM),
        scratch_shapes=[
            pltpu.VMEM((3, layers + 2, rows, width), f32),
            pltpu.VMEM((2 * layers, 3, SUB, width), f32),
            pltpu.VMEM((3, layers, rows, width), f32),
            pltpu.VMEM((layers + 2, COEFS, LANES), f32),
            pltpu.SemaphoreType.DMA((layers,)),
            pltpu.SemaphoreType.DMA((BATCH,)),
        ],
        compiler_params=pltpu.CompilerParams(vmem_limit_bytes=VMEM_LIMIT),
        name="sweeps",
    )(u, f, face1, face2, inner_s, beside1, beside2, ring, got, every, cyc, pinned[8])

    potential = pl.pallas_call(
        functools.partial(synthesis_kernel, 2.0 / cycles),
        out_shape=jax.ShapeDtypeStruct((2, rows, width), f32),
        in_specs=[VMEM] * 7 + [HBM],
        out_specs=VMEM,
        scratch_shapes=[
            pltpu.VMEM((2 * groups, SUB, LANES), f32),
            pltpu.VMEM((BATCH, degrees, LANES), f32),
            pltpu.SemaphoreType.DMA((BATCH,)),
        ],
        compiler_params=pltpu.CompilerParams(vmem_limit_bytes=VMEM_LIMIT),
        name="synthesis",
    )(coef, rest, far, near, gains, cyc, tab, pinned[8])
    return smoothed, potential


def solution(mesh):
    in_specs = (
        P(None, "rad", "lat", None),
        P(None, "rad", "lat", None),
        P("rad"),
        P(),
        P(),
        P("lat", None),
        P(),
        P(),
    )
    out_specs = (P(None, "rad", "lat", None), P(None, "lat", None))
    return jax.shard_map(local, mesh=mesh, in_specs=in_specs, out_specs=out_specs, check_vma=False)
```

```python
import functools
import math

import jax
import jax.numpy as jnp
import numpy as np
from jax import lax
from jax.experimental import pallas as pl
from jax.experimental.pallas import tpu as pltpu
from jax.sharding import PartitionSpec as P

SWEEPS = 2
OMEGA = 0.8
LEAST_COUNT = 32
LANES = 128
SUB = 8
PAD = 8
COEFS = 16
BATCH = 5
VMEM_LIMIT = 16 * 1024 * 1024

VMEM = pl.BlockSpec(memory_space=pltpu.VMEM)
SMEM = pl.BlockSpec(memory_space=pltpu.SMEM)
HBM = pl.BlockSpec(memory_space=pltpu.HBM)
ANY = pl.BlockSpec(memory_space=pl.ANY)


def basis_table(degrees, cycles):
    groups = degrees // SUB
    degree = np.arange(degrees, dtype=np.int64)[:, None]
    cycle = np.arange(cycles, dtype=np.int64)[None, :]
    phase = degree * (2 * cycle + 1) % (4 * cycles)
    table = np.cos(np.pi * phase / (2.0 * cycles)).astype(np.float32)
    table = table.reshape(SUB, groups, cycles // LANES, LANES).transpose(2, 1, 0, 3)
    return np.ascontiguousarray(table.reshape(cycles // LANES, degrees, LANES))


def iota(shape, dim):
    return lax.broadcasted_iota(jnp.int32, shape, dim)


def lane_gather(values, index):
    return jnp.take_along_axis(values, index, axis=1, mode="promise_in_bounds")


def layer_scalars(layer, lid, stiff, coup):
    material = lid[layer]
    mu = stiff[material]
    return mu, [[coup[c, d, material] for d in range(3)] for c in range(3)]


def coefficient_rows(mu, k, width=LANES):
    row = iota((COEFS, width), 0)
    top = jnp.zeros((COEFS, width), jnp.float32)
    below = jnp.ones((COEFS, width), jnp.float32)
    for c in range(3):
        diag = 6.0 * mu + k[c][c]
        others = [d for d in range(3) if d != c]
        entries = [(c, 1.0), (3 + c, mu), (6 + 2 * c, k[c][others[0]]), (7 + 2 * c, k[c][others[1]])]
        for at, value in entries:
            top = jnp.where(row == at, OMEGA * value, top)
            below = jnp.where(row == at, diag, below)
    return top / below


def roll_rows(value, before, after):
    sub = iota(value.shape, 0)
    up = jnp.where(sub == 0, jnp.broadcast_to(before, value.shape), pltpu.roll(value, 1, 0))
    down = jnp.where(sub == SUB - 1, jnp.broadcast_to(after, value.shape), pltpu.roll(value, SUB - 1, 0))
    return up + down


def roll_columns(values):
    lane = iota(values[0].shape, 1)
    right = [pltpu.roll(value, 1, 1) for value in values]
    left = [pltpu.roll(value, LANES - 1, 1) for value in values]
    last = len(values) - 1
    return [
        jnp.where(lane == 0, right[j - 1] if j > 0 else 0.0, right[j])
        + jnp.where(lane == LANES - 1, left[j + 1] if j < last else 0.0, left[j])
        for j in range(len(values))
    ]


def relax(c, centers, neighbours, force, rows):
    d0, d1 = [d for d in range(3) if d != c]
    value = rows[c] * force + rows[3 + c] * neighbours
    value = value - (rows[6 + 2 * c] * centers[d0] + rows[7 + 2 * c] * centers[d1])
    return value + (1.0 - OMEGA) * centers[c]


def chunk(j):
    return pl.ds(LANES * j, LANES)


def spans(per_row, ref, *index):
    return [ref[index + (chunk(j),)] for j in range(per_row)]


def lane_scan(values, steps):
    lane = iota(values.shape, 1)
    step = 1
    while step < steps:
        values = values + jnp.where(lane >= step, pltpu.roll(values, step, 1), 0)
        step *= 2
    return values


def local_sweep(u, f, every, layer, beside, store, groups=None, parts=(0, 1, 2)):
    rows, width = u.shape[2:]
    per_row, total = width // LANES, rows // SUB
    coef = [jnp.broadcast_to(every[layer, j:j + 1, :], (SUB, LANES)) for j in range(12)]
    none = jnp.zeros((1, LANES), jnp.float32)
    for g in range(total) if groups is None else groups:
        here = slice(SUB * g, SUB * g + SUB)
        values = [spans(per_row, u, c, layer, here) for c in range(3)]
        for c in parts:
            aside = roll_columns(values[c])
            for j in range(per_row):
                at = (c, layer)
                above = u[at + (slice(SUB * g - 1, SUB * g), chunk(j))] if g > 0 else none
                under = u[at + (slice(SUB * g + SUB, SUB * g + SUB + 1), chunk(j))] if g < total - 1 else none
                near = roll_rows(values[c][j], above, under) + aside[j]
                for other in beside:
                    near = near + u[c, other, here, chunk(j)]
                value = relax(c, [values[d][j] for d in range(3)], near, f[c, layer, here, chunk(j)], coef)
                store(c, g, j, values[c][j], value)


def faces_kernel(
    disp, forc, lid, stiff, coup, ids, cnt, grav,
    u, f, face1, face2, send, every, cyc, num, gain_in,
    lids, stiffs, coups, small_sem, near_sem, u_sem, f_sem,
):
    layers = disp.shape[1]
    top = layers - 1
    odd = lax.rem(lax.axis_index("rad"), 2) == 1
    small = [
        pltpu.make_async_copy(lid, lids, small_sem.at[0]),
        pltpu.make_async_copy(stiff, stiffs, small_sem.at[1]),
        pltpu.make_async_copy(coup, coups, small_sem.at[2]),
    ]
    cycles = [
        pltpu.make_async_copy(cnt, num, near_sem.at[0]),
        pltpu.make_async_copy(ids, cyc, near_sem.at[1]),
        pltpu.make_async_copy(grav, gain_in, near_sem.at[2]),
    ]
    loads_u = [pltpu.make_async_copy(disp.at[:, r], u.at[:, r], u_sem.at[r]) for r in range(layers)]
    loads_f = [pltpu.make_async_copy(forc.at[:, r], f.at[:, r], f_sem.at[r]) for r in range(layers)]
    for copy in small:
        copy.start()
    for r in [0, 1, top] + list(range(top - 1, 1, -1)):
        loads_u[r].start()
        if r in (0, top):
            loads_f[r].start()
    for r in range(1, top):
        loads_f[r].start()
    for copy in cycles:
        copy.start()
    for copy in small:
        copy.wait()
    for r in range(layers):
        every[r] = coefficient_rows(*layer_scalars(r, lids, stiffs, coups))
    send[...] = every[jnp.where(odd, top, 0)]

    for copy in loads_u + [loads_f[0], loads_f[top]]:
        copy.wait()
    for face, layer in ((face1, jnp.where(odd, 0, top)), (face2, jnp.where(odd, top, 0))):
        def store(c, g, j, value, swept, face=face):
            at = (c, slice(SUB * g, SUB * g + SUB), chunk(j))
            face[(0,) + at] = value
            face[(1,) + at] = swept

        local_sweep(u, f, every, layer, (jnp.where(layer == 0, 1, top - 1),), store)
    for copy in loads_f[1:top] + cycles:
        copy.wait()


def inner_kernel(u, f, every, gain_in, inner_s, gains):
    groups = gain_in.shape[2] // SUB

    def middle(r, carry):
        def store(c, g, j, value, swept):
            inner_s[c, r - 1, SUB * g:SUB * g + SUB, chunk(j)] = swept

        local_sweep(u, f, every, r, (r - 1, r + 1), store)
        return carry

    lax.fori_loop(1, u.shape[1] - 1, middle, 0)

    lane1 = iota((1, LANES), 1)
    for load in range(2):
        for m in range(groups * SUB // LANES):
            one, two = gain_in[0, load:load + 1, chunk(m)], gain_in[1, load:load + 1, chunk(m)]
            gains[load, 2 * m:2 * m + 1, :] = jnp.where(lane1 < groups, one, pltpu.roll(two, groups, 1))
            gains[load, 2 * m + 1:2 * m + 2, :] = jnp.where(lane1 < groups, pltpu.roll(one, groups, 1), two)


def analysis_kernel(
    u, f, face1, face2, every, cyc, num, tbl,
    pay,
    plane, rims, tab, mat, windows, tab_sem,
):
    layers, rows, width = u.shape[1:]
    chunks = num.shape[0]
    groups = tbl.shape[1] // SUB
    per_row = width // LANES
    lat, lats = lax.axis_index("lat"), lax.axis_size("lat")
    rad, rads = lax.axis_index("rad"), lax.axis_size("rad")
    bottom = rad == 0
    at_end = jnp.logical_or(bottom, rad == rads - 1)
    top = layers - 1
    edge, inner = jnp.where(bottom, 0, top), jnp.where(bottom, 1, top - 1)
    total = rows // SUB
    odd = lax.rem(rad, 2) == 1
    at_core = every[jnp.where(odd, 0, top)]
    reach = 2 * width // LEAST_COUNT + 2
    low_part = jnp.right_shift(jnp.maximum(jnp.min(cyc[0:1, 0:LANES]) - reach, 0), 7)
    high_part = jnp.right_shift(jnp.max(cyc[rows - 1:rows, width - LANES:width]) + reach, 7)
    high_part = jnp.minimum(high_part, chunks - 1)

    def table(b):
        return [
            pltpu.make_async_copy(
                tbl.at[jnp.minimum(low_part + b * BATCH + i, chunks - 1)], tab.at[i], tab_sem.at[i]
            )
            for i in range(BATCH)
        ]

    @pl.when(at_end)
    def _():
        for copy in table(0):
            copy.start()

    for r in range(1, top):
        def store(c, g, j, value, swept, r=r):
            rims[c, r - 1, 0 if g == 0 else 1, :, chunk(j)] = swept

        local_sweep(u, f, every, r, (r - 1, r + 1), store, groups=(0, total - 1))

    sub8, lane8 = iota((SUB, LANES), 0), iota((SUB, LANES), 1)
    before = sub8 < 2
    zero = jnp.zeros((SUB, LANES), jnp.float32)
    pay[0:SUB, 0:LANES] = jnp.zeros((SUB, LANES), jnp.float32)
    pay[0:SUB, LANES:2 * LANES] = at_core[0:SUB]
    pay[0:SUB, 2 * LANES:3 * LANES] = at_core[SUB:]

    @pl.when(at_end)
    def _():
        def keep_plane(c, g, j, value, swept):
            plane[SUB * g:SUB * g + SUB, chunk(j)] = swept

        local_sweep(u, f, every, inner, (inner - 1, inner + 1), keep_plane, parts=(0,))
        first = jnp.broadcast_to(cyc[0:1, 0:1], (SUB, LANES))
        last = jnp.broadcast_to(cyc[rows - 1:rows, width - 1:width], (SUB, LANES))
        own_first = jnp.zeros((SUB, LANES), jnp.int32)
        own_last = own_first
        for j in range(per_row):
            own_first = own_first + jnp.where(cyc[0:SUB, LANES * j:LANES * j + LANES] == first, 1, 0)
            own_last = own_last + jnp.where(cyc[rows - SUB:rows, LANES * j:LANES * j + LANES] == last, 1, 0)

        def total_of(count):
            count = jnp.sum(count.astype(jnp.float32), axis=1, keepdims=True)
            return jnp.broadcast_to(jnp.sum(count, axis=0, keepdims=True), (SUB, LANES)).astype(jnp.int32)

        held_here = jnp.where(before, total_of(own_first), total_of(own_last))
        index = jnp.where(before, first - lane8, last + lane8)
        place, part = jnp.bitwise_and(index, LANES - 1), jnp.right_shift(index, 7)
        lengths = jnp.full((SUB, LANES), 2 ** 20, jnp.int32)
        for q in range(chunks):
            row = jnp.broadcast_to(num[q:q + 1, :], (SUB, LANES))
            lengths = jnp.where(part == q, lane_gather(row, place), lengths)
        lengths = lengths - jnp.where(lane8 == 0, held_here, 0)
        limits = lane_scan(lengths, reach)
        caps = [jnp.broadcast_to(limits[:, i:i + 1], (SUB, LANES)) for i in range(reach)]
        spill_ids = []
        for j in range(per_row):
            column = LANES * j + lane8
            away = jnp.where(before, (width - 1 - column) + jnp.where(sub8 == 0, width, 0),
                             column + jnp.where(sub8 == 3, width, 0))
            passed = jnp.zeros((SUB, LANES), jnp.int32)
            for i in range(reach):
                passed = passed + jnp.where(away >= caps[i], 1, 0)
            spill_ids.append(jnp.where(sub8 < 4, jnp.where(before, first - passed, last + passed), 0))

        mat[0] = every[edge]
        mat[1] = every[inner]
        outer = [jnp.broadcast_to(mat[0, j:j + 1, :], (SUB, LANES)) for j in range(12)]
        below = [jnp.broadcast_to(mat[1, j:j + 1, :], (SUB, LANES)) for j in range(12)]

        def rows_of(g):
            return slice(SUB * g, SUB * g + SUB)

        def lateral(ref, g, index, ends):
            values = spans(per_row, ref, *index, rows_of(g))
            aside = roll_columns(values)
            out = []
            for j in range(per_row):
                above = ref[index + (slice(SUB * g - 1, SUB * g), chunk(j))] if g > 0 else ends[0][j]
                under = ref[index + (slice(SUB * g + SUB, SUB * g + SUB + 1), chunk(j))] if g < total - 1 else ends[1][j]
                out.append(roll_rows(values[j], above, under) + aside[j])
            return out

        low_in = jnp.where(lat > 0, 1.0, 0.0)
        high_in = jnp.where(lat < lats - 1, 1.0, 0.0)
        weight = jnp.where(sub8 == 1, low_in, jnp.where(sub8 == 2, high_in, 0.0))

        def ends_of(ref, index, j):
            low = jnp.broadcast_to(ref[index + (slice(0, 1), chunk(j))], (SUB, LANES))
            high = jnp.broadcast_to(ref[index + (slice(rows - 1, rows), chunk(j))], (SUB, LANES))
            return jnp.where(sub8 == 1, low, jnp.where(sub8 == 2, high, 0.0))

        over = [[outer[3 + c] * ends_of(u, (c, edge), j) * weight for j in range(per_row)] for c in range(3)]
        over_inner = [below[3] * ends_of(u, (0, inner), j) * weight for j in range(per_row)]
        aside = roll_columns(over[0])
        spill = []
        for j in range(per_row):
            shifted = jnp.where(sub8 == 0, pltpu.roll(over[0][j], SUB - 1, 0),
                                jnp.where(sub8 == 3, pltpu.roll(over[0][j], 1, 0), 0.0))
            near = over_inner[j] + aside[j] + shifted + ends_of(face2, (1, 0), j)
            value = relax(0, [over[c][j] for c in range(3)], near, zero, outer)
            spill.append(value * jnp.where(before, low_in, high_in))
        ends = [[over[0][j][1:2, :] for j in range(per_row)], [over[0][j][2:3, :] for j in range(per_row)]]

        met = (width - 2) // LEAST_COUNT + 2

        def window_of(values, cycles):
            start = jnp.broadcast_to(cycles[0][:, 0:1], (SUB, LANES))
            offsets = [cycle - start for cycle in cycles]
            window = zero
            for t in range(met):
                picked = [jnp.where(offset == t, value, 0.0) for offset, value in zip(offsets, values)]
                sum_t = jnp.sum(functools.reduce(jnp.add, picked), axis=1, keepdims=True)
                window = jnp.where(lane8 == t, jnp.broadcast_to(sum_t, (SUB, LANES)), window)
            return window, start

        windowed = [window_of(spill, spill_ids)]
        for g in range(total):
            here = rows_of(g)
            centers = [spans(per_row, face2, 1, c, here) for c in range(3)]
            near = lateral(face2, g, (1, 0), ends)
            inners = spans(per_row, plane, here)
            force = spans(per_row, f, 0, edge, here)
            values = [
                relax(0, [center[j] for center in centers], near[j] + inners[j], force[j], outer)
                for j in range(per_row)
            ]
            windowed.append(window_of(values, spans(per_row, cyc, here)))
        for i, (window, start) in enumerate(windowed):
            windows[0, i] = window
            windows[1, i] = start.astype(jnp.float32)

        half = jnp.where(bottom, groups, 0)


        def batch(b, result):
            @pl.when(b > 0)
            def _():
                for copy in table(b):
                    copy.start()

            means = []
            for i in range(BATCH):
                q = low_part + b * BATCH + i
                part = jnp.minimum(q, chunks - 1)
                acc = zero
                for w in range(total + 1):
                    at = q * LANES + lane8 - windows[1, w].astype(jnp.int32)
                    got = lane_gather(windows[0, w], jnp.bitwise_and(at, LANES - 1))
                    acc = acc + jnp.where(jnp.right_shift(at, 7) == 0, got, 0.0)
                mean = jnp.sum(acc, axis=0, keepdims=True) / num[pl.ds(part, 1), :].astype(jnp.float32)
                mean = jnp.where(q < chunks, mean, 0.0)
                means.append(jnp.broadcast_to(mean, (SUB, LANES)))
            for copy in table(b):
                copy.wait()
            for g in range(groups):
                acc = tab[0, SUB * g:SUB * g + SUB, :] * means[0]
                for i in range(1, BATCH):
                    acc = acc + tab[i, SUB * g:SUB * g + SUB, :] * means[i]
                column = jnp.broadcast_to(jnp.sum(acc, axis=1, keepdims=True), (SUB, LANES))
                result = jnp.where(lane8 == g + half, result + column, result)
            return result

        pay[0:SUB, 0:LANES] = lax.fori_loop(0, (high_part - low_part) // BATCH + 1, batch, zero)

    tall = 3 * layers

    def pack(ref, base, near):
        for c in range(3):
            for r in range(layers):
                at = base + c * layers + r
                ref[at:at + 1, :] = u[c, r, near:near + 1, :]
                if r == 0:
                    row = jnp.where(odd, face1[1, c, near:near + 1, :], face2[1, c, near:near + 1, :])
                elif r == top:
                    row = jnp.where(odd, face2[1, c, near:near + 1, :], face1[1, c, near:near + 1, :])
                else:
                    row = rims[c, r - 1, near // (rows - 1), near % SUB:near % SUB + 1, :]
                ref[at + tall:at + tall + 1, :] = row

    pack(pay, SUB, 0)
    pack(pay, SUB + 2 * tall, rows - 1)


def first_chunk(cyc):
    return jnp.right_shift(jnp.min(cyc[0:1, 0:LANES]), 7)


def relay_kernel(ring, send, out):
    cores = 2
    lat, lats = lax.axis_index("lat"), lax.axis_size("lat")
    core = lax.rem(lax.axis_index("rad"), cores)
    members, _, width = ring.shape
    tall = (ring.shape[1] - SUB) // 4
    layers = tall // 3
    coef = ring[0, 0:SUB, 0:LANES]
    for i in range(1, members):
        coef = coef + ring[i, 0:SUB, 0:LANES]
    out[0:SUB, :] = coef
    out[SUB:2 * SUB, :] = send[0:SUB, :]
    before, after = cores * jnp.maximum(lat - 1, 0) + core, cores * jnp.minimum(lat + 1, lats - 1) + core
    low_in, high_in = lat > 0, lat < lats - 1
    for j in range(width // LANES):
        base = 2 * SUB + SUB * j
        out[base:base + SUB, :] = jnp.zeros((SUB, LANES), jnp.float32)
        for c in range(3):
            for at, member, valid, start in ((c, before, low_in, 2 * tall), (3 + c, after, high_in, 0)):
                row = SUB + start + c * layers
                bottom, top = ring[member, row:row + 1, chunk(j)], ring[member, row + layers - 1:row + layers, chunk(j)]
                out[base + at:base + at + 1, :] = jnp.where(valid, jnp.where(core == 1, top, bottom), 0.0)


def sweep_kernel(
    u, f, own1, own2, inner_s, face1, face2, ring, got, every, cyc, tbl,
    out, tab,
    s, rim, done, cf, out_sem, tab_sem,
):
    layers, rows, width = u.shape[1:]
    per_row = width // LANES
    first = first_chunk(cyc)
    table = [
        pltpu.make_async_copy(tbl.at[jnp.minimum(first + i, tbl.shape[0] - 1)], tab.at[i], tab_sem.at[i])
        for i in range(BATCH)
    ]
    for copy in table:
        copy.start()
    total = rows // SUB
    tall = 3 * layers
    top = layers - 1
    lat, lats = lax.axis_index("lat"), lax.axis_size("lat")
    rad, rads = lax.axis_index("rad"), lax.axis_size("rad")
    rad_odd = lax.rem(rad, 2) == 1
    cores = 2
    core = lax.rem(rad, cores)
    lower, upper = cores * jnp.maximum(lat - 1, 0), cores * jnp.minimum(lat + 1, lats - 1)
    low_in, high_in = lat > 0, lat < lats - 1
    sub8 = iota((SUB, LANES), 0)

    def side_rows(base, j):
        at = SUB + base
        low = ring[lower + core, at + 2 * tall:at + 2 * tall + layers, chunk(j)]
        high = ring[upper + core, at:at + layers, chunk(j)]
        low, high = jnp.where(low_in, low, 0.0), jnp.where(high_in, high, 0.0)
        return jnp.concatenate([low, high], axis=0)

    mate = 1 - core
    own_chip = ring[cores * lat + mate, 0:SUB, LANES:2 * LANES]
    other_chip = got[SUB:2 * SUB, :]
    lowest, highest = rad == 0, rad == rads - 1
    cf[0, 0:SUB, :] = jnp.where(rad_odd, own_chip, jnp.where(lowest, 0.0, other_chip))
    cf[layers + 1, 0:SUB, :] = jnp.where(rad_odd, jnp.where(highest, 0.0, other_chip), own_chip)
    for r in range(layers):
        cf[1 + r] = every[r]
    corner_low, corner_high = [], []
    for j in range(per_row):
        base = 2 * SUB + SUB * j
        other = got[base:base + SUB, :]
        rows_own = []
        for member, valid, start in ((lower + mate, low_in, 2 * tall), (upper + mate, high_in, 0)):
            for c in range(3):
                row = SUB + start + c * layers
                near_end, far_end = ring[member, row:row + 1, chunk(j)], ring[member, row + top:row + top + 1, chunk(j)]
                rows_own.append(jnp.where(valid, jnp.where(rad_odd, far_end, near_end), 0.0))
        rows_own.append(jnp.zeros((SUB - 6, LANES), jnp.float32))
        own = jnp.concatenate(rows_own, axis=0)
        corner_low.append(jnp.where(rad_odd, own, jnp.where(lowest, 0.0, other)))
        corner_high.append(jnp.where(rad_odd, jnp.where(highest, 0.0, other), own))

    def coefficients(layer):
        return [jnp.broadcast_to(cf[layer, j:j + 1, :], (SUB, LANES)) for j in range(12)]

    near_rows = [[side_rows(c * layers, j) for j in range(per_row)] for c in range(3)]
    keep = jnp.where(sub8 < layers, jnp.where(low_in, 1.0, 0.0), jnp.where(high_in, 1.0, 0.0))
    for c in range(3):
        gain = jnp.zeros((SUB, LANES), jnp.float32)
        for r in range(layers):
            here = jnp.broadcast_to(cf[1 + r, 3 + c:4 + c, :], (SUB, LANES))
            gain = jnp.where(jnp.logical_or(sub8 == r, sub8 == layers + r), here, gain)
        for j in range(per_row):
            near = jnp.zeros((SUB, LANES), jnp.float32)
            for r in range(layers):
                head = jnp.broadcast_to(u[c, r, 0:1, chunk(j)], near.shape)
                tail = jnp.broadcast_to(u[c, r, rows - 1:rows, chunk(j)], near.shape)
                near = jnp.where(sub8 == r, head, jnp.where(sub8 == layers + r, tail, near))
            ends = (
                (0, corner_low[j][c:c + 1, :]), (layers, corner_low[j][3 + c:4 + c, :]),
                (layers - 1, corner_high[j][c:c + 1, :]), (SUB - 1, corner_high[j][3 + c:4 + c, :]),
            )
            for row, corner in ends:
                near = near + jnp.where(sub8 == row, jnp.broadcast_to(corner, near.shape), 0.0)
            value = (side_rows(tall + c * layers, j) + gain * near) * keep
            for i in range(2 * layers):
                rim[i, c, :, chunk(j)] = jnp.broadcast_to(value[i:i + 1, :], (SUB, LANES))

    def beyond(layer, side, c, j):
        if layer == 0:
            return corner_low[j][3 * side + c:3 * side + c + 1, :]
        if layer == layers + 1:
            return corner_high[j][3 * side + c:3 * side + c + 1, :]
        at = layers * side + layer - 1
        return near_rows[c][j][at:at + 1, :]

    def lo(index):
        return jnp.where(rad_odd, face1[index], face2[index])

    def hi(index):
        return jnp.where(rad_odd, face2[index], face1[index])

    for layer in range(layers + 2):
        for c in range(3):
            gain = jnp.broadcast_to(cf[layer, 3 + c:4 + c, :], (SUB, LANES))
            for j in range(per_row):
                for g in range(total):
                    at = (slice(SUB * g, SUB * g + SUB), chunk(j))
                    if layer == 0:
                        value = lo((1, c) + at) + gain * u[(c, 0) + at]
                    elif layer == layers + 1:
                        value = hi((1, c) + at) + gain * u[(c, top) + at]
                    elif layer in (1, layers):
                        here1, here2 = own1[(1, c) + at], own2[(1, c) + at]
                        value = jnp.where(rad_odd, here1, here2) if layer == 1 else jnp.where(rad_odd, here2, here1)
                    else:
                        value = inner_s[(c, layer - 2) + at]
                    if layer == 1:
                        value = value + gain * lo((0, c) + at)
                    if layer == layers:
                        value = value + gain * hi((0, c) + at)
                    if g == 0:
                        row = jnp.broadcast_to(beyond(layer, 0, c, j), value.shape)
                        value = value + jnp.where(sub8 == 0, gain * row, 0.0)
                    if g == total - 1:
                        row = jnp.broadcast_to(beyond(layer, 1, c, j), value.shape)
                        value = value + jnp.where(sub8 == SUB - 1, gain * row, 0.0)
                    s[(c, layer) + at] = value

    stores = [pltpu.make_async_copy(done.at[:, r], out.at[:, r], out_sem.at[r]) for r in range(layers)]
    for r in range(layers):
        layer = r + 1
        coef = coefficients(layer)
        for g in range(total):
            here = slice(SUB * g, SUB * g + SUB)
            values = [spans(per_row, s, c, layer, here) for c in range(3)]
            for c in range(3):
                aside = roll_columns(values[c])
                for j in range(per_row):
                    at = (c, layer)
                    if g > 0:
                        above_row = s[at + (slice(SUB * g - 1, SUB * g), chunk(j))]
                    else:
                        above_row = rim[r, c, :, chunk(j)]
                    if g < total - 1:
                        under_row = s[at + (slice(SUB * g + SUB, SUB * g + SUB + 1), chunk(j))]
                    else:
                        under_row = rim[layers + r, c, :, chunk(j)]
                    near = roll_rows(values[c][j], above_row, under_row) + aside[j]
                    near = near + (s[c, layer - 1, here, chunk(j)] + s[c, layer + 1, here, chunk(j)])
                    done[c, r, here, chunk(j)] = relax(
                        c, [values[d][j] for d in range(3)], near, f[c, r, here, chunk(j)], coef
                    )
        stores[r].start()
    for copy in stores + table:
        copy.wait()


def synthesis_kernel(scale, coef, rest, near, far, gains, ids, tab, tbl, out, factors, more, more_sem):
    rows, width = ids.shape
    chunks = tbl.shape[0]
    groups = tab.shape[1] // SUB
    per_row = width // LANES
    lane8 = iota((SUB, LANES), 1)
    here = (coef[...] + rest[...]) + (near[...] + far[...])
    other = pltpu.roll(here, groups, 1)
    left = lane8 < groups
    surface = jnp.where(left, here, other)
    core = jnp.where(left, other, here)
    modes = (gains[0] * surface + gains[1] * core) * scale
    zero = jnp.zeros((SUB, LANES), jnp.float32)
    for i in range(2 * groups):
        factors[i] = jnp.broadcast_to(modes[:, i:i + 1], (SUB, LANES))
    low_part = first_chunk(ids)
    high_part = jnp.right_shift(jnp.max(ids[rows - 1:rows, width - LANES:width]), 7)

    def batch(b, carry):
        parts = [low_part + b * BATCH + i for i in range(BATCH)]
        source = tab
        if not isinstance(b, int):
            source = more
            copies = [
                pltpu.make_async_copy(tbl.at[jnp.minimum(part, chunks - 1)], more.at[i], more_sem.at[i])
                for i, part in enumerate(parts)
            ]
            for copy in copies:
                copy.start()
            for copy in copies:
                copy.wait()
        sums = [[zero] * BATCH for _ in range(2)]
        for g in range(groups):
            for i in range(BATCH):
                block = source[i, SUB * g:SUB * g + SUB, :]
                for k in range(2):
                    sums[k][i] = sums[k][i] + factors[k * groups + g] * block
        for k in range(2):
            for i in range(BATCH):
                sums[k][i] = jnp.broadcast_to(jnp.sum(sums[k][i], axis=0, keepdims=True), (SUB, LANES))
        for a in range(rows // SUB):
            for j in range(per_row):
                spot = (slice(SUB * a, SUB * a + SUB), chunk(j))
                cycle = ids[spot]
                place, part = jnp.bitwise_and(cycle, LANES - 1), jnp.right_shift(cycle, 7)
                values = [zero if isinstance(b, int) else out[(k,) + spot] for k in range(2)]
                for i in range(BATCH):
                    chosen = part == parts[i]
                    for k in range(2):
                        values[k] = jnp.where(chosen, lane_gather(sums[k][i], place), values[k])
                for k in range(2):
                    out[(k,) + spot] = values[k]
        return carry

    batch(0, 0)
    lax.fori_loop(1, (high_part - low_part) // BATCH + 1, batch, 0)


def even_pairs(count):
    return [(i, i ^ 1) for i in range(count)]


def odd_pairs(count):
    pairs = []
    for i in range(1, count, 2):
        j = (i + 1) % count
        pairs += [(i, j), (j, i)]
    return pairs


def local(displacement, forcing, layer_id, stiffness, coupling, cycle_id, cycle_count, gravity):
    _, layers, rows, width = displacement.shape
    cycles, degrees = cycle_count.shape[0], gravity.shape[2]
    chunks, groups = cycles // LANES, degrees // SUB
    lats, rads, cores = lax.axis_size("lat"), lax.axis_size("rad"), 2
    if 2 * groups != LANES or 2 * layers != SUB or rads % cores or width < 3 * LANES:
        raise ValueError("unsupported sizes")
    f32 = jnp.float32
    table = jnp.asarray(basis_table(degrees, cycles))
    per_row = width // LANES
    tall = 3 * layers
    face = jax.ShapeDtypeStruct((2, 3, rows, width), f32)

    whole = jax.ShapeDtypeStruct(displacement.shape, f32)
    pinned = [
        pltpu.with_memory_space_constraint(value, pltpu.HBM)
        for value in (
            displacement, forcing, layer_id, stiffness, jnp.transpose(coupling, (1, 2, 0)), cycle_id,
            cycle_count.reshape(chunks, LANES), gravity, table,
        )
    ]
    u, f, face1, face2, mine, every, cyc, num, gain_in = pl.pallas_call(
        faces_kernel,
        out_shape=(
            whole, whole,
            face, face,
            jax.ShapeDtypeStruct((COEFS, LANES), f32),
            jax.ShapeDtypeStruct((layers, COEFS, LANES), f32),
            jax.ShapeDtypeStruct(cycle_id.shape, jnp.int32),
            jax.ShapeDtypeStruct((chunks, LANES), jnp.int32),
            jax.ShapeDtypeStruct(gravity.shape, f32),
        ),
        in_specs=[HBM] * 8,
        out_specs=(VMEM,) * 9,
        scratch_shapes=[
            pltpu.SMEM(layer_id.shape, jnp.int32),
            pltpu.SMEM(stiffness.shape, f32),
            pltpu.SMEM(coupling.shape[1:] + coupling.shape[:1], f32),
            pltpu.SemaphoreType.DMA((3,)),
            pltpu.SemaphoreType.DMA((3,)),
            pltpu.SemaphoreType.DMA((layers,)),
            pltpu.SemaphoreType.DMA((layers,)),
        ],
        compiler_params=pltpu.CompilerParams(vmem_limit_bytes=VMEM_LIMIT),
        name="faces",
    )(*pinned[:8])

    beside2 = lax.ppermute(face2, "rad", odd_pairs(rads)[:-2])
    beside1 = lax.ppermute(face1, "rad", even_pairs(rads))

    pay = pl.pallas_call(
        analysis_kernel,
        out_shape=jax.ShapeDtypeStruct((SUB + 4 * tall, width), f32),
        in_specs=[VMEM] * 7 + [HBM],
        out_specs=VMEM,
        scratch_shapes=[
            pltpu.VMEM((rows, width), f32),
            pltpu.VMEM((3, layers - 2, 2, SUB, width), f32),
            pltpu.VMEM((BATCH, degrees, LANES), f32),
            pltpu.VMEM((2, COEFS, LANES), f32),
            pltpu.VMEM((2, rows // SUB + 1, SUB, LANES), f32),
            pltpu.SemaphoreType.DMA((BATCH,)),
        ],
        compiler_params=pltpu.CompilerParams(vmem_limit_bytes=VMEM_LIMIT),
        name="analysis",
    )(u, f, face1, face2, every, cyc, num, pinned[8])

    chips = [[a * rads + b + c for a in range(lats) for c in range(cores)] for b in range(0, rads, cores)]
    ring = lax.all_gather(pay, ("lat", "rad"), axis_index_groups=chips)
    outward = pl.pallas_call(
        relay_kernel,
        out_shape=jax.ShapeDtypeStruct((2 * SUB + SUB * per_row, LANES), f32),
        in_specs=[VMEM] * 2,
        out_specs=VMEM,
        compiler_params=pltpu.CompilerParams(vmem_limit_bytes=VMEM_LIMIT),
        name="relay",
    )(ring, mine)
    outward, beside1, beside2 = lax.optimization_barrier((outward, beside1, beside2))
    got = lax.ppermute(outward, "rad", odd_pairs(rads))
    inner_s, gains = pl.pallas_call(
        inner_kernel,
        out_shape=(
            jax.ShapeDtypeStruct((3, layers - 2, rows, width), f32),
            jax.ShapeDtypeStruct((2, SUB, LANES), f32),
        ),
        in_specs=[VMEM] * 4,
        out_specs=(VMEM,) * 2,
        compiler_params=pltpu.CompilerParams(vmem_limit_bytes=VMEM_LIMIT),
        name="inner",
    )(u, f, every, gain_in)
    got, inner_s = lax.optimization_barrier((got, inner_s))
    coef = outward[:SUB]
    if rads == 8:
        far = lax.ppermute(coef, "rad", [(0, 4), (4, 0), (7, 3), (3, 7), (1, 6), (6, 1), (2, 5), (5, 2)])
        near = lax.ppermute(coef, "rad", [(0, 3), (3, 0), (7, 4), (4, 7), (1, 5), (5, 1), (2, 6), (6, 2)])
        rest = got[:SUB]
    else:
        coef = lax.psum(coef, "rad") * (1.0 / cores)
        near = far = rest = jnp.zeros_like(coef)

    smoothed, tab = pl.pallas_call(
        sweep_kernel,
        out_shape=(whole, jax.ShapeDtypeStruct((BATCH, degrees, LANES), f32)),
        in_specs=[VMEM] * 11 + [HBM],
        out_specs=(HBM, VMEM),
        scratch_shapes=[
            pltpu.VMEM((3, layers + 2, rows, width), f32),
            pltpu.VMEM((2 * layers, 3, SUB, width), f32),
            pltpu.VMEM((3, layers, rows, width), f32),
            pltpu.VMEM((layers + 2, COEFS, LANES), f32),
            pltpu.SemaphoreType.DMA((layers,)),
            pltpu.SemaphoreType.DMA((BATCH,)),
        ],
        compiler_params=pltpu.CompilerParams(vmem_limit_bytes=VMEM_LIMIT),
        name="sweeps",
    )(u, f, face1, face2, inner_s, beside1, beside2, ring, got, every, cyc, pinned[8])

    potential = pl.pallas_call(
        functools.partial(synthesis_kernel, 2.0 / cycles),
        out_shape=jax.ShapeDtypeStruct((2, rows, width), f32),
        in_specs=[VMEM] * 7 + [HBM],
        out_specs=VMEM,
        scratch_shapes=[
            pltpu.VMEM((2 * groups, SUB, LANES), f32),
            pltpu.VMEM((BATCH, degrees, LANES), f32),
            pltpu.SemaphoreType.DMA((BATCH,)),
        ],
        compiler_params=pltpu.CompilerParams(vmem_limit_bytes=VMEM_LIMIT),
        name="synthesis",
    )(coef, rest, far, near, gains, cyc, tab, pinned[8])
    return smoothed, potential


def solution(mesh):
    in_specs = (
        P(None, "rad", "lat", None),
        P(None, "rad", "lat", None),
        P("rad"),
        P(),
        P(),
        P("lat", None),
        P(),
        P(),
    )
    out_specs = (P(None, "rad", "lat", None), P(None, "lat", None))
    return jax.shard_map(local, mesh=mesh, in_specs=in_specs, out_specs=out_specs, check_vma=False)
```
